128 devices in a mesh: patch: 128 (over z, x, y, core).
Axes of the slice: x: 4, y: 4, z: 4, core: 2. Of those that a mesh axis runs over, the one named last changes fastest.
Arguments:
- fine_nodes: float32 [32768, 512], P('patch'), may hold values from -6 to 6
- coarse_nodes: float32 [642, 512], replicated, may hold values from -6 to 6
- edge_feats: float32 [131072, 512], P('patch'), may hold values from -6 to 6
- senders: int32 [131072], P('patch'), may hold values from 0 to 1921, as said below
- receivers: int32 [131072], P('patch'), may hold values from 0 to 897, as said below
- send_rows: int32 [128, 128, 8], P('patch'), may hold values from 0 to 255
- w_edge_in: float32 [1536, 512], replicated, may hold values from -0.15625 to 0.15625
- w_edge_out: float32 [512, 512], replicated, may hold values from -0.25 to 0.25
- w_node_in: float32 [1024, 512], replicated, may hold values from -0.1875 to 0.1875
- w_node_out: float32 [512, 512], replicated, may hold values from -0.25 to 0.25
- cot_fine: float32 [32768, 512], P('patch'), may hold values from -6 to 6
- cot_coarse: float32 [642, 512], replicated, may hold values from -6 to 6
- cot_edges: float32 [131072, 512], P('patch'), may hold values from -6 to 6
Outputs:
- grad_fine: float32 [32768, 512], P('patch')
- grad_coarse: float32 [642, 512], replicated
- grad_edges: float32 [131072, 512], P('patch')
- grad_edge_in: float32 [1536, 512], replicated
- grad_edge_out: float32 [512, 512], replicated
- grad_node_in: float32 [1024, 512], replicated
- grad_node_out: float32 [512, 512], replicated
The draws below stay inside these ranges and needn't reach their ends.
Inputs may be any that keep to these rules, and one draw needn't show every extreme that they name: Each patch's senders index its node table: its 256 fine nodes, then the 642 coarse nodes, then 8 halo rows from each patch in patch order; halo rows may come from any patch. Each patch's receivers index its own fine nodes, then the coarse nodes.
All inputs are finite; a program needn't handle non-finite values.
Results may differ from the reference program's by a relative error of at most 0.000076.
Values sent between devices are 32-bit elements; how exact they have to be, the bound alone decides.
A program may use at most 192 MiB of HBM per device.

```python
import jax
import jax.numpy as jnp
from jax import lax

W = 512
NODE_DEV = 256
EDGE_DEV = 1024
SLOT = 8
COARSE = 642
NODES = 32768
EDGES = 131072
N_PATCH = 128


def draw_senders(key, part):
    key = jax.random.fold_in(key, 11)
    key_kind, key_local, key_coarse = jax.random.split(key, 3)
    kind = jax.random.randint(key_kind, (EDGES,), 0, 10)
    local = jax.random.randint(key_local, (EDGES,), 0, NODE_DEV)
    coarse = NODE_DEV + jax.random.randint(key_coarse, (EDGES,), 0, COARSE)
    owner = jnp.arange(EDGES, dtype=jnp.int32) // EDGE_DEV
    position = jnp.arange(EDGES, dtype=jnp.int32) % EDGE_DEV
    halo = NODE_DEV + COARSE + (position + owner * 7) % (N_PATCH * SLOT)
    picked = jnp.where(kind < 2, local, jnp.where(kind < 3, coarse, halo))
    first_edge = jnp.arange(EDGES) == 0
    picked = jnp.where(first_edge, NODE_DEV + COARSE + N_PATCH * SLOT - 1, picked)
    picked = jnp.where(position == 1, 0, picked)
    return picked.astype(jnp.int32)


def draw_receivers(key, part):
    key = jax.random.fold_in(key, 23)
    key_kind, key_local, key_coarse = jax.random.split(key, 3)
    kind = jax.random.randint(key_kind, (EDGES,), 0, 20)
    local = jax.random.randint(key_local, (EDGES,), 0, NODE_DEV)
    coarse = NODE_DEV + jax.random.randint(key_coarse, (EDGES,), 0, COARSE)
    picked = jnp.where(kind < 17, local, coarse)
    position = jnp.arange(EDGES) % EDGE_DEV
    picked = jnp.where(position == 1, NODE_DEV + COARSE - 1, picked)
    picked = jnp.where(position == 2, 0, picked)
    return picked.astype(jnp.int32)


def touch_ends(values, stream_key, smallest, largest):
    place = [jax.random.randint(jax.random.fold_in(stream_key, axis), (), 0, length) for axis, length in enumerate(values.shape)]
    longest = values.shape.index(max(values.shape))
    beside = place[:longest] + [(place[longest] + 1) % values.shape[longest]] + place[longest + 1:]
    return values.at[tuple(place)].set(smallest).at[tuple(beside)].set(largest)


def shard_levels(own_key, shape, cuts, smallest, high):
    def one(axis_at, shards_of):
        steps = jax.random.uniform(jax.random.fold_in(jax.random.fold_in(own_key, 6), axis_at), (shards_of,), jnp.float32, smallest / len(cuts), high / len(cuts))
        return jnp.repeat(jnp.exp(steps), shape[axis_at] // shards_of).reshape((-1,) + (1,) * (len(shape) - axis_at - 1))

    level = one(*cuts[0])
    for cut in cuts[1:]:
        level = level * one(*cut)
    return level


def centred(rng, shape, width, bound, cuts=(), held_as=jnp.bfloat16):
    drawn = jax.random.normal(rng, shape, jnp.float32) * width
    if len(cuts) > 0:
        drawn = shard_levels(rng, shape, cuts, -0.22, 0.18) * drawn
    return jnp.clip(drawn, min=-bound, max=bound).astype(held_as)


def setup_inputs(seed: int = 0) -> dict:
    splits = jax.random.split(jax.random.key(seed), 14)
    fine_nodes = centred(splits[0], (NODES, W), 1.0, 6.0, ((0, 128),), jnp.float32)
    coarse_nodes = centred(splits[1], (COARSE, W), 1.0, 6.0, (), jnp.float32)
    edge_feats = centred(splits[2], (EDGES, W), 1.0, 6.0, ((0, 128),), jnp.float32)
    senders = draw_senders(jax.random.fold_in(splits[13], 71), 0)
    receivers = draw_receivers(jax.random.fold_in(splits[13], 71), 0)
    send_rows = touch_ends(jax.random.randint(splits[5], (N_PATCH, N_PATCH, SLOT), 0, NODE_DEV), jax.random.fold_in(splits[5], 1), 0, NODE_DEV - 1).astype(jnp.int32)
    w_edge_in = centred(splits[6], (3 * W, W), (3 * W) ** -0.5, 0.15625, (), jnp.float32)
    w_edge_out = centred(splits[7], (W, W), W ** -0.5, 0.25, (), jnp.float32)
    w_node_in = centred(splits[8], (2 * W, W), (2 * W) ** -0.5, 0.1875, (), jnp.float32)
    w_node_out = centred(splits[9], (W, W), W ** -0.5, 0.25, (), jnp.float32)
    cot_fine = centred(splits[10], (NODES, W), 1.0, 6.0, ((0, 128),), jnp.float32)
    cot_coarse = centred(splits[11], (COARSE, W), 1.0, 6.0, (), jnp.float32)
    cot_edges = centred(splits[12], (EDGES, W), 1.0, 6.0, ((0, 128),), jnp.float32)
    return dict(fine_nodes=fine_nodes, coarse_nodes=coarse_nodes, edge_feats=edge_feats, senders=senders, receivers=receivers, send_rows=send_rows, w_edge_in=w_edge_in, w_edge_out=w_edge_out, w_node_in=w_node_in, w_node_out=w_node_out, cot_fine=cot_fine, cot_coarse=cot_coarse, cot_edges=cot_edges)


def mat_mul(left, right):
    return jnp.dot(left, right, precision=lax.Precision.HIGHEST, preferred_element_type=jnp.float32)

def layer_norm(values):
    center = values - lax.optimization_barrier(jnp.mean(values, axis=1, keepdims=True))
    return center * lax.rsqrt(lax.optimization_barrier(jnp.mean(center * center, axis=1, keepdims=True)) + 1e-05)

def edge_tail(pre_act, edge_in, w_out):
    return edge_in + layer_norm(mat_mul(jax.nn.silu(pre_act), w_out))

def node_update(node_feats, aggregate, w_in, w_out):
    hidden = jax.nn.silu(mat_mul(jnp.concatenate([node_feats, aggregate], axis=1), w_in))
    return node_feats + layer_norm(mat_mul(hidden, w_out))

def reference(fine_nodes, coarse_nodes, edge_feats, senders, receivers, send_rows, w_edge_in, w_edge_out, w_node_in, w_node_out, cot_fine, cot_coarse, cot_edges):
    node_total = NODES + COARSE
    device_of = (jnp.arange(EDGES, dtype=jnp.int32) // EDGE_DEV).astype(jnp.int32)
    halo_pos = jnp.maximum(senders - NODE_DEV - COARSE, 0).astype(jnp.int32)
    peer_of = (halo_pos // SLOT).astype(jnp.int32)
    halo_global = peer_of * NODE_DEV + send_rows[peer_of, device_of, halo_pos % SLOT]
    sender_global = jnp.where(senders < NODE_DEV, device_of * NODE_DEV + senders, jnp.where(senders < NODE_DEV + COARSE, NODES + senders - NODE_DEV, halo_global)).astype(jnp.int32)
    receiver_global = jnp.where(receivers < NODE_DEV, device_of * NODE_DEV + receivers, NODES + receivers - NODE_DEV).astype(jnp.int32)

    def forward(fine_in, coarse_in, edge_in, w_ei, w_eo, w_ni, w_no):
        all_nodes = jnp.concatenate([fine_in, coarse_in], axis=0)
        stacked = jnp.concatenate([edge_in, all_nodes[sender_global], all_nodes[receiver_global]], axis=1)
        new_edges = edge_tail(mat_mul(stacked, w_ei), edge_in, w_eo)
        aggregate = jax.ops.segment_sum(new_edges, receiver_global, num_segments=node_total)
        new_nodes = node_update(all_nodes, aggregate, w_ni, w_no)
        return (new_nodes[:NODES], new_nodes[NODES:], new_edges)
    _, backward = jax.vjp(forward, fine_nodes, coarse_nodes, edge_feats, w_edge_in, w_edge_out, w_node_in, w_node_out)
    gradients = backward((cot_fine, cot_coarse, cot_edges))
    edge_scale = EDGES ** (-0.5)
    node_scale = node_total ** (-0.5)
    return (gradients[0], gradients[1], gradients[2], gradients[3] * edge_scale, gradients[4] * edge_scale, gradients[5] * node_scale, gradients[6] * node_scale)
```

```python
import functools
import math

import jax
import jax.numpy as jnp
from jax import lax
from jax.experimental import pallas as pl
from jax.experimental.pallas import tpu as pltpu
from jax.sharding import PartitionSpec as P

MESH = pl.DeviceIdType.MESH
F32 = jnp.float32
BF16 = jnp.bfloat16
FEAT = 512
FINE = 256
COARSE = 642
NEAR = 1024
EDGE = 1024
BLOCK = 256
LINKS = 6
VMEM_BYTES = 60 << 20

NN = (((1,), (0,)), ((), ()))
NT = (((1,), (1,)), ((), ()))
TN = (((0,), (0,)), ((), ()))


def split(value):
    high = value.astype(BF16)
    return high, (value - high.astype(F32)).astype(BF16)


def dot(left, right, dims=NN):
    return lax.dot_general(left, right, dims, preferred_element_type=F32)


def dot3(left, right, dims=NN):
    return dot(left[0], right[0], dims) + dot(left[0], right[1], dims) + dot(left[1], right[0], dims)


def dot2(left, right, dims=NN):
    return dot(left, right[0], dims) + dot(left, right[1], dims)


def block_at(step):
    return pl.ds(pl.multiple_of(step * BLOCK, BLOCK), BLOCK)


def pair_at(refs, rows):
    return refs[0][rows, :], refs[1][rows, :]


def put_pair(refs, rows, value):
    high, low = split(value)
    refs[0][rows, :] = high
    refs[1][rows, :] = low


def spread(index_row):
    return jnp.transpose(jnp.broadcast_to(index_row, (128, index_row.shape[1])))


def hot_rows(spread_block, first, width):
    lane = lax.broadcasted_iota(jnp.int32, (spread_block.shape[0], 128), 1)
    local = spread_block - first
    tiles = [jnp.where(local == lane + at, 1.0, 0.0).astype(BF16) for at in range(0, width, 128)]
    return jnp.concatenate(tiles, axis=1)


def hot_columns(index_row, first, height):
    row = lax.broadcasted_iota(jnp.int32, (height, index_row.shape[1]), 0) + first
    return jnp.where(row == index_row, 1.0, 0.0).astype(BF16)


def sigmoid(value):
    return 1.0 / (1.0 + jnp.exp(-value))


def mean(value):
    return jnp.sum(value, axis=1, keepdims=True) * (1.0 / FEAT)


def norm(value):
    center = value - mean(value)
    scale = lax.rsqrt(mean(center * center) + 1e-05)
    return center * scale, scale


def norm_back(grad, normed, scale):
    return scale * (grad - mean(grad) - normed * mean(grad * normed))


def put_tiles(ref, value):
    for at in range(FEAT // 128):
        ref[:, at] = value[:, at * 128 : (at + 1) * 128].reshape(-1, 8, 128)


def vmem_specs(count):
    return [pl.BlockSpec(memory_space=pltpu.VMEM)] * count


def local_call(kernel, outs, scratch, flops, *args):
    moved = sum(math.prod(a.shape) * 4 for a in args) + sum(math.prod(o.shape) * 4 for o in outs)
    return pl.pallas_call(
        kernel,
        out_shape=outs,
        in_specs=vmem_specs(len(args)),
        out_specs=vmem_specs(len(outs)),
        scratch_shapes=scratch,
        compiler_params=pltpu.CompilerParams(vmem_limit_bytes=VMEM_BYTES),
        cost_estimate=pl.CostEstimate(flops=int(flops), bytes_accessed=moved, transcendentals=0),
    )(*args)


def f32_out(*shape):
    return jax.ShapeDtypeStruct(shape, F32)


def bf16_out(*shape):
    return jax.ShapeDtypeStruct(shape, BF16)


TILES = f32_out(64, 4, 8, 128)


def outgoing_kernel(fine_ref, w_ref, list_ref, out_ref, own_ref, list_rep):
    own = dot3(split(fine_ref[...]), split(w_ref[FEAT : 2 * FEAT, :]))
    own_ref[...] = own
    parts = split(own)
    list_rep[...] = spread(list_ref[...])

    def step(at, carry):
        rows = block_at(at)
        out_ref[rows, :] = dot2(hot_rows(list_rep[rows, :], 0, FINE), parts)
        return carry

    lax.fori_loop(0, EDGE // BLOCK, step, 0)


def near_kernel(near_ref, own_ref, edge_ref, w_ref, send_ref, recv_ref, pre_ref, p0, p1, q0, q1, send_rep, recv_rep):
    put_pair((p0, p1), pl.ds(0, FINE), own_ref[...])
    send_rep[...] = spread(send_ref[...])
    recv_rep[...] = spread(recv_ref[...])
    w_send = split(w_ref[FEAT : 2 * FEAT, :])
    w_recv = split(w_ref[2 * FEAT :, :])

    put_pair((q0, q1), pl.ds(0, FINE), dot3(split(near_ref[:FINE, :]), w_recv))

    def project(at, carry):
        rows = block_at(at)
        feats = split(near_ref[rows, :])
        put_pair((p0, p1), rows, dot3(feats, w_send))
        put_pair((q0, q1), rows, dot3(feats, w_recv))
        return carry

    lax.fori_loop(1, NEAR // BLOCK, project, 0)
    w_edge = split(w_ref[:FEAT, :])

    def step(at, carry):
        rows = block_at(at)
        total = dot3(split(edge_ref[rows, :]), w_edge)
        total += dot2(hot_rows(recv_rep[rows, :], 0, NEAR), (q0[...], q1[...]))
        total += dot2(hot_rows(send_rep[rows, :], 0, NEAR), (p0[...], p1[...]))
        pre_ref[rows, :] = total
        return carry

    lax.fori_loop(0, EDGE // BLOCK, step, 0)


def edge_kernel(part_ref, halo_ref, edge_ref, w_ref, send_ref, recv_ref, pre_ref, normed_ref, scale_ref, agg_ref, h0, h1, n0, n1, send_rep):
    send_rep[...] = spread(send_ref[...])
    h0[...], h1[...] = split(halo_ref[...])
    w_out = split(w_ref[...])

    def step(at, carry):
        rows = block_at(at)
        pre = part_ref[rows, :] + dot2(hot_rows(send_rep[rows, :], NEAR, EDGE), (h0[...], h1[...]))
        pre_ref[rows, :] = pre
        normed, scale = norm(dot3(split(pre * sigmoid(pre)), w_out))
        normed_ref[rows, :] = normed
        scale_ref[rows, :] = jnp.broadcast_to(scale, (BLOCK, 128))
        put_pair((n0, n1), rows, edge_ref[rows, :] + normed)
        return carry

    lax.fori_loop(0, EDGE // BLOCK, step, 0)

    def gather(at, carry):
        rows = block_at(at)
        agg_ref[rows, :] = dot2(hot_columns(recv_ref[...], at * BLOCK, BLOCK), (n0[...], n1[...]))
        return carry

    lax.fori_loop(0, NEAR // BLOCK, gather, 0)


def cube_place():
    me = lax.axis_index("patch")
    core = me % 2
    y = (me // 2) % 4
    x = (me // 8) % 4
    z = me // 32
    bits, mates = [core], [me + 1 - 2 * core]
    for low in (True, False):
        for place, stride in ((z, 32), (x, 8), (y, 2)):
            if low:
                bits.append(((place + 1) // 2) % 2)
                mates.append(me + (1 - 2 * (place % 2)) * stride)
            else:
                bits.append(place // 2)
                mates.append(me + (3 - 2 * place) * stride)
    return bits, mates


def greet(mates):
    barrier = pltpu.get_barrier_semaphore()
    for mate in mates:
        pl.semaphore_signal(barrier, inc=1, device_id=(mate,), device_id_type=MESH)
    pl.semaphore_wait(barrier, len(mates))


def push(src, dst, send_sem, recv_sem, mate):
    copy = pltpu.make_async_remote_copy(
        src_ref=src, dst_ref=dst, send_sem=send_sem, recv_sem=recv_sem, device_id=(mate,), device_id_type=MESH
    )
    copy.start()
    return copy


def cube_bit(part, step):
    return 0 if step == 0 else 1 + (part + step - 1) % LINKS


def sum_kernel(*refs):
    weight_refs, (coarse_ref, direct_ref), (out_ref,) = refs[:6], refs[6:8], refs[8:9]
    buf, got, s1, r1, s2, r2 = refs[9:]
    flat = buf.reshape(LINKS * 128 * 3, 8, 128)
    at = 0
    for ref in weight_refs:
        size = ref.shape[0] * 4
        flat[at : at + size] = ref[...].reshape(size, 8, 128)
        at += size
    size = coarse_ref.shape[0] * 4
    flat[at : at + size] = coarse_ref[...].reshape(size, 8, 128)
    flat[at + size :] = jnp.zeros((flat.shape[0] - at - size, 8, 128), F32)
    me = lax.axis_index("patch")
    mine = pl.ds(at + me * 4, 4)
    flat[mine] += direct_ref[...]
    bits, mates = cube_place()
    greet(mates)

    bases = [0] * LINKS
    copies = {}

    def reduce_start(part, step):
        bit = cube_bit(part, step)
        half = 64 >> step
        away = bases[part] + (1 - bits[bit]) * half
        copies[part] = push(
            buf.at[part, pl.ds(away, half)], got.at[part, pl.ds(128 - 2 * half, half)], s1.at[step, part], r1.at[step, part], mates[bit]
        )
        bases[part] = bases[part] + bits[bit] * half

    def gather_start(part, step):
        bit = cube_bit(part, step)
        half = 64 >> step
        block = out_ref.at[part, pl.ds(bases[part], half)]
        copies[part] = push(block, block, s2.at[step, part], r2.at[step, part], mates[bit])
        bases[part] = bases[part] - bits[bit] * half

    for part in range(LINKS):
        reduce_start(part, 0)
    for step in range(7):
        half = 64 >> step
        for part in range(LINKS):
            copies[part].wait()
            kept = pl.ds(bases[part], half)
            arrived = got[part, pl.ds(128 - 2 * half, half)]
            if step < 6:
                buf[part, kept] += arrived
                reduce_start(part, step + 1)
            else:
                out_ref[part, kept] = buf[part, kept] + arrived
                gather_start(part, step)
    for step in reversed(range(7)):
        for part in range(LINKS):
            copies[part].wait()
            if step > 0:
                gather_start(part, step - 1)


def sum_all(weights, coarse, direct):
    sem = pltpu.SemaphoreType.DMA((7, LINKS))
    shape = (LINKS, 128, 3, 8, 128)
    return pl.pallas_call(
        sum_kernel,
        out_shape=f32_out(*shape),
        in_specs=vmem_specs(8),
        out_specs=pl.BlockSpec(memory_space=pltpu.VMEM),
        scratch_shapes=[pltpu.VMEM(shape, F32), pltpu.VMEM((LINKS, 127, 3, 8, 128), F32)] + [sem] * 4,
        compiler_params=pltpu.CompilerParams(collective_id=1, has_side_effects=True, vmem_limit_bytes=VMEM_BYTES),
    )(*weights, coarse, direct)


COLUMN_ORDERS = ((0, 1, 2), (1, 2, 0), (2, 0, 1), (0, 2, 1))
STRIDES = (32, 8, 2)


def axis_places(device):
    return [(device // 32) % 4, (device // 8) % 4, (device // 2) % 4], device % 2


def position(device, part):
    places, core = axis_places(device)
    spot = core
    for axis in COLUMN_ORDERS[part]:
        spot = spot * 4 + places[axis]
    return spot


def node_pass(feats, agg, cot, w_in, w_out):
    feat_pair, agg_pair = split(feats), split(agg)
    pre = dot3(feat_pair, pair_at(w_in, pl.ds(0, FEAT))) + dot3(agg_pair, pair_at(w_in, pl.ds(FEAT, FEAT)))
    gate = sigmoid(pre)
    hidden = split(pre * gate)
    out_pair = (w_out[0][...], w_out[1][...])
    normed, scale = norm(dot3(hidden, out_pair))
    tail = split(norm_back(cot, normed, scale))
    grad_pre = split(dot3(tail, out_pair, NT) * (gate * (1.0 + pre * (1.0 - gate))))
    return feat_pair, agg_pair, hidden, tail, grad_pre


def node_kernel(*refs):
    agg_ref, fine_ref, cot_ref, few_ref, few_cot_ref, w_in_ref, w_out_ref = refs[:7]
    grad_agg_ref, own_ref, direct_ref, in_ref, out_ref = refs[7:12]
    buf, got, full, wi0, wi1, wo0, wo1, total = refs[12:20]
    s1, r1, s2, r2 = refs[20:]
    me = lax.axis_index("patch")
    places, core = axis_places(me)
    mate = me + 1 - 2 * core

    def peer(axis, shift):
        return me + ((places[axis] + shift) % 4 - places[axis]) * STRIDES[axis]

    for part in range(4):
        for device in range(128):
            first = FINE + 8 * device
            if first < NEAR and 8 * device < COARSE:
                buf[part, position(device, part)] = agg_ref[first : first + 8, part * 128 : (part + 1) * 128]
            else:
                buf[part, position(device, part)] = jnp.zeros((8, 128), F32)
    greet([mate] + [peer(axis, shift) for axis in range(3) for shift in (1, 2, 3)])

    wi, wo = (wi0, wi1), (wo0, wo1)
    keep = {}

    def cut_weights():
        wi0[...], wi1[...] = split(w_in_ref[...])
        wo0[...], wo1[...] = split(w_out_ref[...])

    def fine_pass():
        keep["fine"] = node_pass(fine_ref[...], agg_ref[:FINE, :], cot_ref[...], wi, wo)

    def fine_back():
        grad_pre = keep["fine"][4]
        own_ref[...] = cot_ref[...] + dot3(grad_pre, pair_at(wi, pl.ds(0, FEAT)), NT)
        grad_agg_ref[:FINE, :] = dot3(grad_pre, pair_at(wi, pl.ds(FEAT, FEAT)), NT)

    beside = [cut_weights, fine_pass, fine_back]

    bases = [0] * 4
    for stage in range(4):
        sub = (64, 16, 4, 1)[stage]
        offset = (0, 64, 112, 124)[stage]
        copies = []
        for part in range(4):
            if stage == 0:
                away = (1 - core) * sub
                copies.append(push(buf.at[part, pl.ds(away, sub)], got.at[part, pl.ds(0, sub)], s1.at[part, 0], r1.at[part, 0], mate))
                bases[part] = core * sub
                continue
            axis = COLUMN_ORDERS[part][stage - 1]
            for shift in (1, 2, 3):
                away = bases[part] + ((places[axis] + shift) % 4) * sub
                sem = 3 * stage - 3 + shift
                copies.append(
                    push(
                        buf.at[part, pl.ds(away, sub)],
                        got.at[part, pl.ds(offset + (shift - 1) * sub, sub)],
                        s1.at[part, sem],
                        r1.at[part, sem],
                        peer(axis, shift),
                    )
                )
            bases[part] = bases[part] + places[axis] * sub
        if beside:
            beside.pop(0)()
        count = len(copies) // 4
        for part in range(4):
            for copy in copies[part * count : (part + 1) * count]:
                copy.wait()
            kept = pl.ds(bases[part], sub)
            value = buf[part, kept]
            for shift in range(count):
                value += got[part, pl.ds(offset + shift * sub, sub)]
            buf[part, kept] = value

    few_agg = jnp.concatenate([buf[part, bases[part]] for part in range(4)], axis=1)
    blank = jnp.zeros((8, FEAT), F32)
    few = node_pass(
        jnp.concatenate([few_ref[...], blank], axis=0),
        jnp.concatenate([few_agg, blank], axis=0),
        jnp.concatenate([few_cot_ref[...], blank], axis=0),
        wi,
        wo,
    )
    few_grad = dot3(few[4], pair_at(wi, pl.ds(FEAT, FEAT)), NT)[:8]
    for part in range(4):
        full[part, bases[part]] = few_grad[:, part * 128 : (part + 1) * 128]

    def few_back():
        direct = few_cot_ref[...] + dot3(few[4], pair_at(wi, pl.ds(0, FEAT)), NT)[:8]
        for at in range(4):
            direct_ref[at] = direct[:, at * 128 : (at + 1) * 128]

    def weights_back(which, grad, ref, first):
        def run():
            total[...] = dot3(keep["fine"][which], keep["fine"][grad], TN) + dot3(few[which], few[grad], TN)
            put_tiles(ref.at[pl.ds(first, 64)], total)

        return run

    beside = [few_back, weights_back(0, 4, in_ref, 0), weights_back(1, 4, in_ref, 64), weights_back(2, 3, out_ref, 0)]
    for stage in (3, 2, 1, 0):
        sub = (64, 16, 4, 1)[stage]
        copies = []
        for part in range(4):
            block = full.at[part, pl.ds(bases[part], sub)]
            if stage == 0:
                copies.append(push(block, block, s2.at[part, 0], r2.at[part, 0], mate))
                continue
            axis = COLUMN_ORDERS[part][stage - 1]
            for shift in (1, 2, 3):
                sem = 3 * stage - 3 + shift
                copies.append(push(block, block, s2.at[part, sem], r2.at[part, sem], peer(axis, shift)))
            bases[part] = bases[part] - places[axis] * sub
        if beside:
            beside.pop(0)()
        for copy in copies:
            copy.wait()
    for part in range(4):
        for device in range((NEAR - FINE) // 8):
            first = FINE + 8 * device
            grad_agg_ref[first : first + 8, part * 128 : (part + 1) * 128] = full[part, position(device, part)]


def node_step(agg, fine, cot_fine, few, few_cot, w_in, w_out):
    sem = pltpu.SemaphoreType.DMA((4, 10))
    return pl.pallas_call(
        node_kernel,
        out_shape=[f32_out(NEAR, FEAT), f32_out(FINE, FEAT), f32_out(4, 8, 128), f32_out(128, 4, 8, 128), TILES],
        in_specs=vmem_specs(7),
        out_specs=vmem_specs(5),
        scratch_shapes=[
            pltpu.VMEM((4, 128, 8, 128), F32),
            pltpu.VMEM((4, 127, 8, 128), F32),
            pltpu.VMEM((4, 128, 8, 128), F32),
            pltpu.VMEM((2 * FEAT, FEAT), BF16),
            pltpu.VMEM((2 * FEAT, FEAT), BF16),
            pltpu.VMEM((FEAT, FEAT), BF16),
            pltpu.VMEM((FEAT, FEAT), BF16),
            pltpu.VMEM((FEAT, FEAT), F32),
        ]
        + [sem] * 4,
        compiler_params=pltpu.CompilerParams(collective_id=2, has_side_effects=True, vmem_limit_bytes=VMEM_BYTES),
    )(agg, fine, cot_fine, few, few_cot, w_in, w_out)


def edge_back_kernel(grad_agg_ref, cot_ref, pre_ref, normed_ref, scale_ref, w_ref, send_ref, recv_ref, grad_ref, t0, t1, d0, d1, halo_ref, a0, a1, recv_rep):
    recv_rep[...] = spread(recv_ref[...])
    a0[...], a1[...] = split(grad_agg_ref[...])
    w_out = split(w_ref[...])

    def step(at, carry):
        rows = block_at(at)
        grad = cot_ref[rows, :] + dot2(hot_rows(recv_rep[rows, :], 0, NEAR), (a0[...], a1[...]))
        grad_ref[rows, :] = grad
        tail = split(norm_back(grad, normed_ref[rows, :], scale_ref[rows, :1]))
        t0[rows, :], t1[rows, :] = tail
        pre = pre_ref[rows, :]
        gate = sigmoid(pre)
        put_pair((d0, d1), rows, dot3(tail, w_out, NT) * (gate * (1.0 + pre * (1.0 - gate))))
        return carry

    lax.fori_loop(0, EDGE // BLOCK, step, 0)

    def gather(at, carry):
        rows = block_at(at)
        halo_ref[rows, :] = dot2(hot_columns(send_ref[...], NEAR + at * BLOCK, BLOCK), (d0[...], d1[...]))
        return carry

    lax.fori_loop(0, EDGE // BLOCK, gather, 0)


def weights_kernel(*refs):
    grad_ref, t0, t1, d0, d1, pre_ref, edge_ref, near_ref, w_ref, send_ref, recv_ref = refs[:11]
    grad_edges_ref, in_edge_ref, in_send_ref, in_recv_ref, out_ref, own_send_ref, own_ref, coarse_ref = refs[11:19]
    edge_total, tail_total, recv_total = refs[19:]
    edge_total[...] = jnp.zeros_like(edge_total)
    tail_total[...] = jnp.zeros_like(tail_total)
    w_edge = split(w_ref[:FEAT, :])

    def step(at, carry):
        rows = block_at(at)
        grad_pre = (d0[rows, :], d1[rows, :])
        grad_edges_ref[rows, :] = grad_ref[rows, :] + dot3(grad_pre, w_edge, NT)
        edge_total[...] += dot3(split(edge_ref[rows, :]), grad_pre, TN)
        pre = pre_ref[rows, :]
        tail_total[...] += dot3(split(pre * sigmoid(pre)), (t0[rows, :], t1[rows, :]), TN)
        return carry

    lax.fori_loop(0, EDGE // BLOCK, step, 0)
    put_tiles(in_edge_ref, edge_total)
    put_tiles(out_ref, tail_total)
    w_send = split(w_ref[FEAT : 2 * FEAT, :])
    w_recv = split(w_ref[2 * FEAT :, :])

    def sums(at):
        grad_pre = (d0[...], d1[...])
        sent = dot2(hot_columns(send_ref[...], at * BLOCK, BLOCK), grad_pre)
        return sent, split(dot2(hot_columns(recv_ref[...], at * BLOCK, BLOCK), grad_pre))

    sent, received = sums(0)
    own_send_ref[...] = sent
    own_ref[...] = dot3(received, w_recv, NT)
    recv_total[...] = dot3(split(near_ref[:FINE, :]), received, TN)
    in_send_ref[...] = jnp.zeros_like(in_send_ref)

    def coarse_step(at, carry):
        rows = block_at(at)
        sent, received = sums(at)
        sent = split(sent)
        value = dot3(sent, w_send, NT) + dot3(received, w_recv, NT)
        put_tiles(coarse_ref.at[pl.ds((at - 1) * (BLOCK // 8), BLOCK // 8)], value)
        feats = split(near_ref[rows, :])
        recv_total[...] += dot3(feats, received, TN)
        in_send_ref[...] += dot3(feats, sent, TN)
        return carry

    lax.fori_loop(1, NEAR // BLOCK, coarse_step, 0)
    put_tiles(in_recv_ref, recv_total)


def fine_kernel(back_ref, list_ref, own_send_ref, own_ref, direct_ref, fine_ref, w_ref, partial_ref, grad_ref, in_send_ref):
    sent = split(own_send_ref[...] + dot2(hot_columns(list_ref[...], 0, FINE), split(back_ref[...])))
    grad_ref[...] = direct_ref[...] + own_ref[...] + dot3(sent, split(w_ref[FEAT : 2 * FEAT, :]), NT)
    put_tiles(in_send_ref, partial_ref[...] + dot3(split(fine_ref[...]), sent, TN))


def per_device(
    fine_nodes,
    coarse_nodes,
    edge_feats,
    senders,
    receivers,
    send_rows,
    w_edge_in,
    w_edge_out,
    w_node_in,
    w_node_out,
    cot_fine,
    cot_coarse,
    cot_edges,
):
    me = lax.axis_index("patch")
    peers = lax.axis_size("patch")
    send_list = send_rows.reshape(1, EDGE)
    near_count = FINE + COARSE
    send_at = jnp.where(senders < near_count, senders, senders + (NEAR - near_count)).reshape(1, EDGE)
    recv_at = receivers.reshape(1, EDGE)
    pair = [pltpu.VMEM((EDGE, FEAT), BF16)] * 2
    index = pltpu.VMEM((EDGE, 128), jnp.int32)
    square = pltpu.VMEM((FEAT, FEAT), F32)
    wide = f32_out(EDGE, FEAT)
    fine_out = f32_out(FINE, FEAT)

    outgoing, own = local_call(outgoing_kernel, [wide, fine_out], [index], 1e9, fine_nodes, w_edge_in, send_list)
    incoming = lax.all_to_all(outgoing.reshape(peers, 8, FEAT), "patch", split_axis=0, concat_axis=0, tiled=True)
    incoming = incoming.reshape(EDGE, FEAT)
    near = jnp.concatenate([fine_nodes, coarse_nodes, jnp.zeros((NEAR - near_count, FEAT), F32)], axis=0)
    pre_near = local_call(
        near_kernel, [wide], pair * 2 + [index] * 2, 1e10, near, own, edge_feats, w_edge_in, send_at, recv_at
    )[0]
    pre, normed, scale, agg = local_call(
        edge_kernel,
        [wide, wide, f32_out(EDGE, 128), wide],
        pair * 2 + [index],
        5e9,
        pre_near,
        incoming,
        edge_feats,
        w_edge_out,
        send_at,
        recv_at,
    )
    blank = jnp.zeros((8 * peers - COARSE, FEAT), F32)
    few = lax.dynamic_slice(jnp.concatenate([coarse_nodes, blank], axis=0), (me * 8, 0), (8, FEAT))
    few_cot = lax.dynamic_slice(jnp.concatenate([cot_coarse, blank], axis=0), (me * 8, 0), (8, FEAT))
    grad_agg, direct, few_direct, node_in, node_out = node_step(agg, fine_nodes, cot_fine, few, few_cot, w_node_in, w_node_out)
    half = bf16_out(EDGE, FEAT)
    grad, t0, t1, d0, d1, halo = local_call(
        edge_back_kernel,
        [wide, half, half, half, half, wide],
        pair + [index],
        8e9,
        grad_agg,
        cot_edges,
        pre,
        normed,
        scale,
        w_edge_out,
        send_at,
        recv_at,
    )
    back = lax.all_to_all(halo.reshape(peers, 8, FEAT), "patch", split_axis=0, concat_axis=0, tiled=True)
    grad_edges, in_edge, in_send, in_recv, edge_out, own_send, own_grad, coarse = local_call(
        weights_kernel,
        [wide, TILES, f32_out(FEAT, FEAT), TILES, TILES, fine_out, fine_out, f32_out(96, 4, 8, 128)],
        [square] * 3,
        1.6e10,
        grad,
        t0,
        t1,
        d0,
        d1,
        pre,
        edge_feats,
        near,
        w_edge_in,
        send_at,
        recv_at,
    )
    grad_fine, in_send = local_call(
        fine_kernel,
        [fine_out, TILES],
        [],
        2e9,
        back.reshape(EDGE, FEAT),
        send_list,
        own_send,
        own_grad,
        direct,
        fine_nodes,
        w_edge_in,
        in_send,
    )
    summed = sum_all((in_edge, in_send, in_recv, edge_out, node_in, node_out), coarse, few_direct)
    rows = summed.reshape(-1, 4, 8, 128).transpose(0, 2, 1, 3).reshape(-1, FEAT)
    edge_scale = 1.0 / math.sqrt(EDGE * peers)
    node_scale = 1.0 / math.sqrt(FINE * peers + COARSE)
    return (
        grad_fine,
        rows[7 * FEAT : 7 * FEAT + COARSE],
        grad_edges,
        rows[: 3 * FEAT] * edge_scale,
        rows[3 * FEAT : 4 * FEAT] * edge_scale,
        rows[4 * FEAT : 6 * FEAT] * node_scale,
        rows[6 * FEAT : 7 * FEAT] * node_scale,
    )


def solution(mesh):
    return jax.shard_map(
        per_device,
        mesh=mesh,
        in_specs=(
            P("patch", None),
            P(),
            P("patch", None),
            P("patch"),
            P("patch"),
            P("patch", None, None),
            P(),
            P(),
            P(),
            P(),
            P("patch", None),
            P(),
            P("patch", None),
        ),
        out_specs=(P("patch", None), P(), P("patch", None), P(), P(), P(), P()),
        check_vma=False,
    )
```

```python
import functools
import math

import jax
import jax.numpy as jnp
from jax import lax
from jax.experimental import pallas as pl
from jax.experimental.pallas import tpu as pltpu
from jax.sharding import PartitionSpec as P

MESH = pl.DeviceIdType.MESH
F32 = jnp.float32
BF16 = jnp.bfloat16
FEAT = 512
FINE = 256
COARSE = 642
NEAR = 1024
EDGE = 1024
BLOCK = 256
LINKS = 6
LOCAL_BYTES = 30 << 20

NN = (((1,), (0,)), ((), ()))
NT = (((1,), (1,)), ((), ()))
TN = (((0,), (0,)), ((), ()))


def split(value):
    high = value.astype(BF16)
    return high, (value - high.astype(F32)).astype(BF16)


def dot(left, right, dims=NN):
    return lax.dot_general(left, right, dims, preferred_element_type=F32)


def dot3(left, right, dims=NN):
    return dot(left[0], right[0], dims) + dot(left[0], right[1], dims) + dot(left[1], right[0], dims)


def dot2(left, right, dims=NN):
    return dot(left, right[0], dims) + dot(left, right[1], dims)


def block_at(step):
    return pl.ds(pl.multiple_of(step * BLOCK, BLOCK), BLOCK)


def pair_at(refs, rows):
    return refs[0][rows, :], refs[1][rows, :]


def put_pair(refs, rows, value):
    high, low = split(value)
    refs[0][rows, :] = high
    refs[1][rows, :] = low


def spread(index_row):
    return jnp.transpose(jnp.broadcast_to(index_row, (128, index_row.shape[1])))


def hot_rows(spread_block, first, width):
    lane = lax.broadcasted_iota(jnp.int32, (spread_block.shape[0], 128), 1)
    local = spread_block - first
    tiles = [jnp.where(local == lane + at, 1.0, 0.0).astype(BF16) for at in range(0, width, 128)]
    return jnp.concatenate(tiles, axis=1)


def hot_columns(index_row, first, height):
    row = lax.broadcasted_iota(jnp.int32, (height, index_row.shape[1]), 0) + first
    return jnp.where(row == index_row, 1.0, 0.0).astype(BF16)


def sigmoid(value):
    return 1.0 / (1.0 + jnp.exp(-value))


def mean(value):
    return jnp.sum(value, axis=1, keepdims=True) * (1.0 / FEAT)


def norm(value):
    center = value - mean(value)
    scale = lax.rsqrt(mean(center * center) + 1e-05)
    return center * scale, scale


def norm_back(grad, normed, scale):
    return scale * (grad - mean(grad) - normed * mean(grad * normed))


def put_tiles(ref, value):
    for at in range(FEAT // 128):
        ref[:, at] = value[:, at * 128 : (at + 1) * 128].reshape(-1, 8, 128)


def vmem_specs(count):
    return [pl.BlockSpec(memory_space=pltpu.VMEM)] * count


def local_call(kernel, outs, scratch, flops, *args):
    moved = sum(math.prod(a.shape) * 4 for a in args) + sum(math.prod(o.shape) * 4 for o in outs)
    return pl.pallas_call(
        kernel,
        out_shape=outs,
        in_specs=vmem_specs(len(args)),
        out_specs=vmem_specs(len(outs)),
        scratch_shapes=scratch,
        compiler_params=pltpu.CompilerParams(vmem_limit_bytes=LOCAL_BYTES),
        cost_estimate=pl.CostEstimate(flops=int(flops), bytes_accessed=moved, transcendentals=0),
    )(*args)


def f32_out(*shape):
    return jax.ShapeDtypeStruct(shape, F32)


def bf16_out(*shape):
    return jax.ShapeDtypeStruct(shape, BF16)


TILES = f32_out(64, 4, 8, 128)


def outgoing_kernel(fine_ref, w_ref, list_ref, out_ref, own_ref, list_rep):
    own = dot3(split(fine_ref[...]), split(w_ref[FEAT : 2 * FEAT, :]))
    own_ref[...] = own
    parts = split(own)
    list_rep[...] = spread(list_ref[...])

    def step(at, carry):
        rows = block_at(at)
        out_ref[rows, :] = dot2(hot_rows(list_rep[rows, :], 0, FINE), parts)
        return carry

    lax.fori_loop(0, EDGE // BLOCK, step, 0)


def near_kernel(near_ref, own_ref, edge_ref, w_ref, send_ref, recv_ref, pre_ref, p0, p1, q0, q1, send_rep, recv_rep):
    put_pair((p0, p1), pl.ds(0, FINE), own_ref[...])
    send_rep[...] = spread(send_ref[...])
    recv_rep[...] = spread(recv_ref[...])
    w_send = split(w_ref[FEAT : 2 * FEAT, :])
    w_recv = split(w_ref[2 * FEAT :, :])

    put_pair((q0, q1), pl.ds(0, FINE), dot3(split(near_ref[:FINE, :]), w_recv))

    def project(at, carry):
        rows = block_at(at)
        feats = split(near_ref[rows, :])
        put_pair((p0, p1), rows, dot3(feats, w_send))
        put_pair((q0, q1), rows, dot3(feats, w_recv))
        return carry

    lax.fori_loop(1, NEAR // BLOCK, project, 0)
    w_edge = split(w_ref[:FEAT, :])

    def step(at, carry):
        rows = block_at(at)
        total = dot3(split(edge_ref[rows, :]), w_edge)
        total += dot2(hot_rows(recv_rep[rows, :], 0, NEAR), (q0[...], q1[...]))
        total += dot2(hot_rows(send_rep[rows, :], 0, NEAR), (p0[...], p1[...]))
        pre_ref[rows, :] = total
        return carry

    lax.fori_loop(0, EDGE // BLOCK, step, 0)


def edge_kernel(part_ref, halo_ref, edge_ref, w_ref, send_ref, recv_ref, pre_ref, normed_ref, scale_ref, agg_ref, h0, h1, n0, n1, send_rep):
    send_rep[...] = spread(send_ref[...])
    h0[...], h1[...] = split(halo_ref[...])
    w_out = split(w_ref[...])

    def step(at, carry):
        rows = block_at(at)
        pre = part_ref[rows, :] + dot2(hot_rows(send_rep[rows, :], NEAR, EDGE), (h0[...], h1[...]))
        pre_ref[rows, :] = pre
        normed, scale = norm(dot3(split(pre * sigmoid(pre)), w_out))
        normed_ref[rows, :] = normed
        scale_ref[rows, :] = jnp.broadcast_to(scale, (BLOCK, 128))
        put_pair((n0, n1), rows, edge_ref[rows, :] + normed)
        return carry

    lax.fori_loop(0, EDGE // BLOCK, step, 0)

    def gather(at, carry):
        rows = block_at(at)
        agg_ref[rows, :] = dot2(hot_columns(recv_ref[...], at * BLOCK, BLOCK), (n0[...], n1[...]))
        return carry

    lax.fori_loop(0, NEAR // BLOCK, gather, 0)


STRIDES = (32, 8, 2)
ALL_PARTS = tuple((part % 3, part // 3) for part in range(6))
FOUR_PARTS = ALL_PARTS[:4]
GOT_CHUNKS = 127
SEM_COUNT = 24


def axis_places(device):
    return [(device // 32) % 4, (device // 8) % 4, (device // 2) % 4], device % 2


def axis_bits(place):
    return ((place + 1) // 2) % 2, place // 2


def position(device, spec):
    places, core = axis_places(device)
    first, flip = spec
    bits = axis_bits(places[first])
    spot = (core * 2 + bits[flip]) * 2 + bits[1 - flip]
    return (spot * 4 + places[(first + 1) % 3]) * 4 + places[(first + 2) % 3]


class Exchange:
    def __init__(self, specs, buf, got, out, sends, recvs):
        self.specs, self.buf, self.got, self.out, self.sends, self.recvs = specs, buf, got, out, sends, recvs
        self.me = lax.axis_index("patch")
        self.places, self.core = axis_places(self.me)
        self.mate = self.me + 1 - 2 * self.core
        self.bits = [axis_bits(place) for place in self.places]
        self.flying = {}
        self.spot = {}
        for part, (first, flip) in enumerate(specs):
            one, two = self.bits[first][flip], self.bits[first][1 - flip]
            third, fourth = self.places[(first + 1) % 3], self.places[(first + 2) % 3]
            at_core = self.core * 64
            at_one = at_core + one * 32
            at_two = at_one + two * 16
            at_three = at_two + third * 4
            self.spot[part] = dict(
                one=one, two=two, core=at_core, first=at_one, second=at_two, third=at_three, last=at_three + fourth
            )

    def greet(self):
        mates = [self.mate]
        mates += [self.peer(axis, shift) for axis in range(3) for shift in (1, 2, 3)]
        barrier = pltpu.get_barrier_semaphore()
        for mate in mates:
            pl.semaphore_signal(barrier, inc=1, device_id=(mate,), device_id_type=MESH)
        pl.semaphore_wait(barrier, len(mates))

    def peer(self, axis, shift):
        return self.me + ((self.places[axis] + shift) % 4 - self.places[axis]) * STRIDES[axis]

    def neighbour(self, axis, flip):
        place = self.places[axis]
        step = 3 - 2 * place if flip else 1 - 2 * (place % 2)
        return self.me + step * STRIDES[axis]

    def push(self, part, sem, src, dst, device):
        copy = pltpu.make_async_remote_copy(
            src_ref=src,
            dst_ref=dst,
            send_sem=self.sends.at[sem, part],
            recv_sem=self.recvs.at[sem, part],
            device_id=(device,),
            device_id_type=MESH,
        )
        copy.start()
        self.flying[part, sem] = copy

    def wait(self, part, *sems):
        for sem in sems:
            self.flying.pop((part, sem)).wait()

    def send_sum(self, part, sem, at, size, slot, device):
        self.push(part, sem, self.buf.at[part, pl.ds(at, size)], self.got.at[part, pl.ds(slot, size)], device)

    def add(self, part, at, size, *slots):
        total = self.buf[part, pl.ds(at, size)]
        for slot in slots:
            total += self.got[part, pl.ds(slot, size)]
        self.buf[part, pl.ds(at, size)] = total

    def send_block(self, part, sem, at, size, device):
        block = self.out.at[part, pl.ds(at, size)]
        self.push(part, sem, block, block, device)


    def start(self, part):
        spot = self.spot[part]
        other = 64 - spot["core"]
        self.send_sum(part, 0, other + (1 - spot["one"]) * 32, 32, 0, self.mate)

    def start_kept(self, part):
        spot = self.spot[part]
        other = 64 - spot["core"]
        self.send_sum(part, 1, other + spot["one"] * 32, 32, 32, self.mate)

    def reduce_first(self, part):
        spot = self.spot[part]
        first, flip = self.specs[part]
        away = spot["core"] + (1 - spot["one"]) * 32
        device = self.neighbour(first, flip)
        self.wait(part, 0)
        self.add(part, away, 32, 0)
        self.send_sum(part, 2, away + (1 - spot["two"]) * 16, 16, 64, device)
        self.send_sum(part, 3, away + spot["two"] * 16, 16, 80, device)

    def reduce_kept(self, part):
        self.wait(part, 1)
        self.add(part, self.spot[part]["first"], 32, 32)

    def reduce_second(self, part):
        spot = self.spot[part]
        first, flip = self.specs[part]
        away = spot["first"] + (1 - spot["two"]) * 16
        self.wait(part, 2)
        self.add(part, away, 16, 64)
        self.send_sum(part, 4, away, 16, 96, self.neighbour(first, 1 - flip))

    def reduce_third(self, part):
        spot = self.spot[part]
        axis = (self.specs[part][0] + 1) % 3
        self.wait(part, 3, 4)
        self.add(part, spot["second"], 16, 80, 96)
        for shift in (1, 2, 3):
            at = spot["second"] + (self.places[axis] + shift) % 4 * 4
            self.send_sum(part, 4 + shift, at, 4, 108 + 4 * shift, self.peer(axis, shift))

    def reduce_fourth(self, part):
        spot = self.spot[part]
        axis = (self.specs[part][0] + 2) % 3
        self.wait(part, 5, 6, 7)
        self.add(part, spot["third"], 4, 112, 116, 120)
        for shift in (1, 2, 3):
            at = spot["third"] + (self.places[axis] + shift) % 4
            self.send_sum(part, 7 + shift, at, 1, 123 + shift, self.peer(axis, shift))

    def reduce_last(self, part):
        self.wait(part, 8, 9, 10)
        self.add(part, self.spot[part]["last"], 1, 124, 125, 126)

    def gather_fourth(self, part):
        axis = (self.specs[part][0] + 2) % 3
        for shift in (1, 2, 3):
            self.send_block(part, 10 + shift, self.spot[part]["last"], 1, self.peer(axis, shift))

    def gather_third(self, part):
        axis = (self.specs[part][0] + 1) % 3
        self.wait(part, 11, 12, 13)
        for shift in (1, 2, 3):
            self.send_block(part, 13 + shift, self.spot[part]["third"], 4, self.peer(axis, shift))

    def gather_second(self, part):
        spot = self.spot[part]
        first, flip = self.specs[part]
        self.wait(part, 14, 15, 16)
        self.send_block(part, 17, spot["second"], 16, self.neighbour(first, 1 - flip))
        self.send_block(part, 20, spot["second"], 16, self.mate)

    def gather_first(self, part):
        spot = self.spot[part]
        first, flip = self.specs[part]
        device = self.neighbour(first, flip)
        self.wait(part, 17)
        self.send_block(part, 18, spot["first"], 16, device)
        self.send_block(part, 19, spot["first"] + 16, 16, device)
        self.send_block(part, 21, spot["first"] + (1 - spot["two"]) * 16, 16, self.mate)

    def gather_core(self, part):
        spot = self.spot[part]
        self.wait(part, 18)
        self.send_block(part, 22, spot["core"] + (1 - spot["one"]) * 32, 16, self.mate)

    def gather_rest(self, part):
        spot = self.spot[part]
        self.wait(part, 19)
        self.send_block(part, 23, spot["core"] + (1 - spot["one"]) * 32 + 16, 16, self.mate)

    def gather_last(self, part):
        self.wait(part, 20, 21, 22, 23)

    REDUCE = ("reduce_first", "reduce_kept", "reduce_second", "reduce_third", "reduce_fourth", "reduce_last")
    GATHER = ("gather_fourth", "gather_third", "gather_second", "gather_first", "gather_core", "gather_rest", "gather_last")

    def run(self, stages, beside=()):
        beside = list(beside)
        for stage in stages:
            if beside:
                beside.pop(0)()
            for part in range(len(self.specs)):
                getattr(self, stage)(part)
        for work in beside:
            work()

    def finish_sum(self, part):
        self.reduce_last(part)
        last = pl.ds(self.spot[part]["last"], 1)
        self.out[part, last] = self.buf[part, last]
        self.gather_fourth(part)

    SUM = REDUCE[:-1] + ("finish_sum",) + GATHER[1:]


def exchange_scratch(parts, units):
    sem = pltpu.SemaphoreType.DMA((SEM_COUNT, parts))
    return [
        pltpu.VMEM((parts, 128, units, 8, 128), F32),
        pltpu.VMEM((parts, GOT_CHUNKS, units, 8, 128), F32),
        sem,
        sem,
    ]


def sum_out(units):
    return f32_out(LINKS, 128, units, 8, 128)


def remote_call(kernel, name_id, outs, scratch, limit, *args):
    return pl.pallas_call(
        kernel,
        out_shape=outs,
        in_specs=vmem_specs(len(args)),
        out_specs=vmem_specs(len(outs)),
        scratch_shapes=scratch,
        compiler_params=pltpu.CompilerParams(collective_id=name_id, has_side_effects=True, vmem_limit_bytes=limit << 20),
        cost_estimate=pl.CostEstimate(flops=int(3e10), bytes_accessed=int(3e7), transcendentals=0),
    )(*args)


def node_pass(feats, agg, cot, w_in, w_out):
    feat_pair, agg_pair = split(feats), split(agg)
    pre = dot3(feat_pair, pair_at(w_in, pl.ds(0, FEAT))) + dot3(agg_pair, pair_at(w_in, pl.ds(FEAT, FEAT)))
    gate = sigmoid(pre)
    hidden = split(pre * gate)
    out_pair = (w_out[0][...], w_out[1][...])
    normed, scale = norm(dot3(hidden, out_pair))
    tail = split(norm_back(cot, normed, scale))
    grad_pre = split(dot3(tail, out_pair, NT) * (gate * (1.0 + pre * (1.0 - gate))))
    return feat_pair, agg_pair, hidden, tail, grad_pre


def node_kernel(*refs):
    agg_ref, fine_ref, cot_ref, few_ref, few_cot_ref, w_in_ref, w_out_ref = refs[:7]
    grad_agg_ref, own_ref, direct_ref, node_ref = refs[7:11]
    buf, got, sends, recvs, full, wi0, wi1, wo0, wo1, total = refs[11:]
    ring = Exchange(FOUR_PARTS, buf, got, full, sends, recvs)
    ring.greet()
    for part, spec in enumerate(FOUR_PARTS):
        for device in range(128):
            first = FINE + 8 * device
            if first < NEAR and 8 * device < COARSE:
                buf[part, position(device, spec), 0] = agg_ref[first : first + 8, part * 128 : (part + 1) * 128]
            else:
                buf[part, position(device, spec), 0] = jnp.zeros((8, 128), F32)
        ring.start(part)
    for part in range(4):
        ring.start_kept(part)

    wi, wo = (wi0, wi1), (wo0, wo1)
    keep = {}

    def cut_weights():
        wi0[...], wi1[...] = split(w_in_ref[...])
        wo0[...], wo1[...] = split(w_out_ref[...])

    def fine_pass():
        keep["fine"] = node_pass(fine_ref[...], agg_ref[:FINE, :], cot_ref[...], wi, wo)

    def fine_back():
        grad_pre = keep["fine"][4]
        own_ref[...] = cot_ref[...] + dot3(grad_pre, pair_at(wi, pl.ds(0, FEAT)), NT)
        grad_agg_ref[:FINE, :] = dot3(grad_pre, pair_at(wi, pl.ds(FEAT, FEAT)), NT)

    def nothing():
        pass

    ring.run(ring.REDUCE, [nothing, cut_weights, nothing, fine_pass, fine_back])

    few_agg = jnp.concatenate([buf[part, ring.spot[part]["last"], 0] for part in range(4)], axis=1)
    blank = jnp.zeros((8, FEAT), F32)
    few = node_pass(
        jnp.concatenate([few_ref[...], blank], axis=0),
        jnp.concatenate([few_agg, blank], axis=0),
        jnp.concatenate([few_cot_ref[...], blank], axis=0),
        wi,
        wo,
    )
    few_grad = dot3(few[4], pair_at(wi, pl.ds(FEAT, FEAT)), NT)[:8]
    for part in range(4):
        full[part, ring.spot[part]["last"], 0] = few_grad[:, part * 128 : (part + 1) * 128]

    def few_back():
        direct = few_cot_ref[...] + dot3(few[4], pair_at(wi, pl.ds(0, FEAT)), NT)[:8]
        for at in range(4):
            direct_ref[at] = direct[:, at * 128 : (at + 1) * 128]

    def weights_back(which, grad, first):
        def run():
            total[...] = dot3(keep["fine"][which], keep["fine"][grad], TN) + dot3(few[which], few[grad], TN)
            put_tiles(node_ref.at[pl.ds(first, 64)], total)

        return run

    beside = [nothing, few_back, weights_back(0, 4, 0), weights_back(1, 4, 64), weights_back(2, 3, 128)]
    ring.run(ring.GATHER, beside)
    for part, spec in enumerate(FOUR_PARTS):
        for device in range((NEAR - FINE) // 8):
            first = FINE + 8 * device
            grad_agg_ref[first : first + 8, part * 128 : (part + 1) * 128] = full[part, position(device, spec), 0]


def node_step(agg, fine, cot_fine, few, few_cot, w_in, w_out):
    half = pltpu.VMEM((2 * FEAT, FEAT), BF16)
    quarter = pltpu.VMEM((FEAT, FEAT), BF16)
    return remote_call(
        node_kernel,
        2,
        [f32_out(NEAR, FEAT), f32_out(FINE, FEAT), f32_out(4, 8, 128), f32_out(192, 4, 8, 128)],
        exchange_scratch(4, 1)
        + [pltpu.VMEM((4, 128, 1, 8, 128), F32), half, half, quarter, quarter, pltpu.VMEM((FEAT, FEAT), F32)],
        34,
        agg,
        fine,
        cot_fine,
        few,
        few_cot,
        w_in,
        w_out,
    )


def edge_back_kernel(grad_agg_ref, cot_ref, pre_ref, normed_ref, scale_ref, w_ref, send_ref, recv_ref, grad_ref, t0, t1, d0, d1, halo_ref, a0, a1, recv_rep):
    recv_rep[...] = spread(recv_ref[...])
    a0[...], a1[...] = split(grad_agg_ref[...])
    w_out = split(w_ref[...])

    def step(at, carry):
        rows = block_at(at)
        grad = cot_ref[rows, :] + dot2(hot_rows(recv_rep[rows, :], 0, NEAR), (a0[...], a1[...]))
        grad_ref[rows, :] = grad
        tail = split(norm_back(grad, normed_ref[rows, :], scale_ref[rows, :1]))
        t0[rows, :], t1[rows, :] = tail
        pre = pre_ref[rows, :]
        gate = sigmoid(pre)
        put_pair((d0, d1), rows, dot3(tail, w_out, NT) * (gate * (1.0 + pre * (1.0 - gate))))
        return carry

    lax.fori_loop(0, EDGE // BLOCK, step, 0)

    def gather(at, carry):
        rows = block_at(at)
        halo_ref[rows, :] = dot2(hot_columns(send_ref[...], NEAR + at * BLOCK, BLOCK), (d0[...], d1[...]))
        return carry

    lax.fori_loop(0, EDGE // BLOCK, gather, 0)


def weights_kernel(*refs):
    grad_ref, t0, t1, d0, d1, pre_ref, edge_ref, near_ref, w_ref, send_ref, recv_ref, node_ref = refs[:12]
    grad_edges_ref, in_edge_ref, in_send_ref, in_recv_ref, out_ref, own_send_ref, own_ref, coarse_ref, sum_ref = refs[12:21]
    buf, got, sends, recvs, edge_total, tail_total, recv_total = refs[21:]
    ring = Exchange(ALL_PARTS, buf, got, sum_ref, sends, recvs)
    ring.greet()
    buf[...] = node_ref[...].reshape(buf.shape)
    for part in range(LINKS):
        ring.start(part)
    for part in range(LINKS):
        ring.start_kept(part)
    edge_total[...] = jnp.zeros_like(edge_total)
    tail_total[...] = jnp.zeros_like(tail_total)

    def edge_step(at):
        def run():
            rows = block_at(at)
            grad_pre = (d0[rows, :], d1[rows, :])
            grad_edges_ref[rows, :] = grad_ref[rows, :] + dot3(grad_pre, split(w_ref[:FEAT, :]), NT)
            edge_total[...] += dot3(split(edge_ref[rows, :]), grad_pre, TN)
            pre = pre_ref[rows, :]
            tail_total[...] += dot3(split(pre * sigmoid(pre)), (t0[rows, :], t1[rows, :]), TN)

        return run

    def store_totals():
        put_tiles(in_edge_ref, edge_total)
        put_tiles(out_ref, tail_total)

    def sums(at):
        grad_pre = (d0[...], d1[...])
        sent = dot2(hot_columns(send_ref[...], at * BLOCK, BLOCK), grad_pre)
        return sent, split(dot2(hot_columns(recv_ref[...], at * BLOCK, BLOCK), grad_pre))

    def fine_step():
        sent, received = sums(0)
        own_send_ref[...] = sent
        own_ref[...] = dot3(received, split(w_ref[2 * FEAT :, :]), NT)
        recv_total[...] = dot3(split(near_ref[:FINE, :]), received, TN)
        in_send_ref[...] = jnp.zeros_like(in_send_ref)

    def coarse_step(at):
        def run():
            rows = block_at(at)
            sent, received = sums(at)
            sent = split(sent)
            value = dot3(sent, split(w_ref[FEAT : 2 * FEAT, :]), NT) + dot3(received, split(w_ref[2 * FEAT :, :]), NT)
            put_tiles(coarse_ref.at[pl.ds((at - 1) * (BLOCK // 8), BLOCK // 8)], value)
            feats = split(near_ref[rows, :])
            recv_total[...] += dot3(feats, received, TN)
            in_send_ref[...] += dot3(feats, sent, TN)

        return run

    works = [edge_step(at) for at in range(EDGE // BLOCK)]
    works += [store_totals, fine_step] + [coarse_step(at) for at in range(1, NEAR // BLOCK)]
    ring.run(ring.SUM, works)
    put_tiles(in_recv_ref, recv_total)


def sum_kernel(*refs):
    in_edge_ref, in_recv_ref, out_ref, coarse_ref, direct_ref = refs[:5]
    back_ref, list_ref, own_send_ref, own_ref, fine_direct_ref, fine_ref, w_ref, partial_ref = refs[5:13]
    grad_ref, sum_ref, buf, got, sends, recvs, in_send = refs[13:]
    flat = buf.reshape(LINKS * 256, 8, 128)
    ring = Exchange(ALL_PARTS, buf, got, sum_ref, sends, recvs)
    ring.greet()
    for at, ref in enumerate((in_edge_ref, in_recv_ref, out_ref)):
        flat[at * 256 : (at + 1) * 256] = ref[...].reshape(256, 8, 128)
        ring.start(at)
    flat[768 : 768 + 384] = coarse_ref[...].reshape(384, 8, 128)
    flat[768 + 384 : 1280] = jnp.zeros((128, 8, 128), F32)
    mine = pl.ds(768 + ring.me * 4, 4)
    flat[mine] += direct_ref[...]
    for part in (3, 4):
        ring.start(part)
    for part in range(5):
        ring.start_kept(part)
    sent = split(own_send_ref[...] + dot2(hot_columns(list_ref[...], 0, FINE), split(back_ref[...])))
    in_send[...] = partial_ref[...] + dot3(split(fine_ref[...]), sent, TN)
    put_tiles(flat.at[pl.ds(1280, 256)].reshape(64, 4, 8, 128), in_send)
    ring.start(5)
    ring.start_kept(5)

    def fine_grad():
        grad_ref[...] = fine_direct_ref[...] + own_ref[...] + dot3(sent, split(w_ref[FEAT : 2 * FEAT, :]), NT)

    def nothing():
        pass

    ring.run(ring.SUM, [nothing, nothing, nothing, fine_grad])


def put_rows(ref, tiles, scale):
    for at in range(FEAT // 128):
        ref[:, at * 128 : (at + 1) * 128] = (tiles[:, at] * scale).reshape(-1, 128)


def finish_kernel(edge_scale, node_scale, edge_ref, node_ref, coarse_ref, in_ref, out_ref, node_in_ref, node_out_ref):
    tiles = edge_ref.reshape(384, 4, 8, 128)
    put_rows(in_ref.at[pl.ds(0, FEAT)], tiles[0:64], edge_scale)
    put_rows(in_ref.at[pl.ds(FEAT, FEAT)], tiles[320:384], edge_scale)
    put_rows(in_ref.at[pl.ds(2 * FEAT, FEAT)], tiles[64:128], edge_scale)
    put_rows(out_ref, tiles[128:192], edge_scale)
    whole = COARSE // 8
    put_rows(coarse_ref.at[pl.ds(0, whole * 8)], tiles[192 : 192 + whole], 1.0)
    for at in range(FEAT // 128):
        coarse_ref[whole * 8 :, at * 128 : (at + 1) * 128] = tiles[192 + whole, at][: COARSE - whole * 8]
    node = node_ref.reshape(192, 4, 8, 128)
    put_rows(node_in_ref, node[0:128], node_scale)
    put_rows(node_out_ref, node[128:192], node_scale)


def per_device(
    fine_nodes,
    coarse_nodes,
    edge_feats,
    senders,
    receivers,
    send_rows,
    w_edge_in,
    w_edge_out,
    w_node_in,
    w_node_out,
    cot_fine,
    cot_coarse,
    cot_edges,
):
    me = lax.axis_index("patch")
    peers = lax.axis_size("patch")
    send_list = send_rows.reshape(1, EDGE)
    near_count = FINE + COARSE
    send_at = jnp.where(senders < near_count, senders, senders + (NEAR - near_count)).reshape(1, EDGE)
    recv_at = receivers.reshape(1, EDGE)
    pair = [pltpu.VMEM((EDGE, FEAT), BF16)] * 2
    index = pltpu.VMEM((EDGE, 128), jnp.int32)
    square = pltpu.VMEM((FEAT, FEAT), F32)
    wide = f32_out(EDGE, FEAT)
    fine_out = f32_out(FINE, FEAT)

    outgoing, own = local_call(outgoing_kernel, [wide, fine_out], [index], 1e9, fine_nodes, w_edge_in, send_list)
    incoming = lax.all_to_all(outgoing.reshape(peers, 8, FEAT), "patch", split_axis=0, concat_axis=0, tiled=True)
    incoming = incoming.reshape(EDGE, FEAT)
    near = jnp.concatenate([fine_nodes, coarse_nodes, jnp.zeros((NEAR - near_count, FEAT), F32)], axis=0)
    pre_near = local_call(
        near_kernel, [wide], pair * 2 + [index] * 2, 1e10, near, own, edge_feats, w_edge_in, send_at, recv_at
    )[0]
    pre, normed, scale, agg = local_call(
        edge_kernel,
        [wide, wide, f32_out(EDGE, 128), wide],
        pair * 2 + [index],
        5e9,
        pre_near,
        incoming,
        edge_feats,
        w_edge_out,
        send_at,
        recv_at,
    )
    blank = jnp.zeros((8 * peers - COARSE, FEAT), F32)
    few = lax.dynamic_slice(jnp.concatenate([coarse_nodes, blank], axis=0), (me * 8, 0), (8, FEAT))
    few_cot = lax.dynamic_slice(jnp.concatenate([cot_coarse, blank], axis=0), (me * 8, 0), (8, FEAT))
    grad_agg, direct, few_direct, node = node_step(agg, fine_nodes, cot_fine, few, few_cot, w_node_in, w_node_out)
    half = bf16_out(EDGE, FEAT)
    grad, t0, t1, d0, d1, halo = local_call(
        edge_back_kernel,
        [wide, half, half, half, half, wide],
        pair + [index],
        8e9,
        grad_agg,
        cot_edges,
        pre,
        normed,
        scale,
        w_edge_out,
        send_at,
        recv_at,
    )
    back = lax.all_to_all(halo.reshape(peers, 8, FEAT), "patch", split_axis=0, concat_axis=0, tiled=True)
    grad_edges, in_edge, in_send, in_recv, edge_out, own_send, own_grad, coarse, node_sum = remote_call(
        weights_kernel,
        3,
        [wide, TILES, f32_out(FEAT, FEAT), TILES, TILES, fine_out, fine_out, f32_out(96, 4, 8, 128), sum_out(1)],
        exchange_scratch(LINKS, 1) + [square] * 3,
        44,
        grad,
        t0,
        t1,
        d0,
        d1,
        pre,
        edge_feats,
        near,
        w_edge_in,
        send_at,
        recv_at,
        node,
    )
    grad_fine, edge_sum = remote_call(
        sum_kernel,
        1,
        [fine_out, sum_out(2)],
        exchange_scratch(LINKS, 2) + [square],
        44,
        in_edge,
        in_recv,
        edge_out,
        coarse,
        few_direct,
        back.reshape(EDGE, FEAT),
        send_list,
        own_send,
        own_grad,
        direct,
        fine_nodes,
        w_edge_in,
        in_send,
    )
    grad_coarse, grad_in, grad_out, grad_node_in, grad_node_out = local_call(
        functools.partial(
            finish_kernel, 1.0 / math.sqrt(EDGE * peers), 1.0 / math.sqrt(FINE * peers + COARSE)
        ),
        [f32_out(COARSE, FEAT), f32_out(3 * FEAT, FEAT), f32_out(FEAT, FEAT), f32_out(2 * FEAT, FEAT), f32_out(FEAT, FEAT)],
        [],
        1e6,
        edge_sum,
        node_sum,
    )
    return grad_fine, grad_coarse, grad_edges, grad_in, grad_out, grad_node_in, grad_node_out


def solution(mesh):
    return jax.shard_map(
        per_device,
        mesh=mesh,
        in_specs=(
            P("patch", None),
            P(),
            P("patch", None),
            P("patch"),
            P("patch"),
            P("patch", None, None),
            P(),
            P(),
            P(),
            P(),
            P("patch", None),
            P(),
            P("patch", None),
        ),
        out_specs=(P("patch", None), P(), P("patch", None), P(), P(), P(), P()),
        check_vma=False,
    )
```

```python
import functools
import math

import jax
import jax.numpy as jnp
from jax import lax
from jax.experimental import pallas as pl
from jax.experimental.pallas import tpu as pltpu
from jax.sharding import PartitionSpec as P

MESH = pl.DeviceIdType.MESH
F32 = jnp.float32
BF16 = jnp.bfloat16
FEAT = 512
FINE = 256
COARSE = 642
NEAR = 1024
EDGE = 1024
BLOCK = 256
LINKS = 6
LOCAL_BYTES = 30 << 20
FRONT_MIB, BACK_MIB, SUM_MIB = 36, 40, 40

NN = (((1,), (0,)), ((), ()))
NT = (((1,), (1,)), ((), ()))
TN = (((0,), (0,)), ((), ()))


def split(value):
    high = value.astype(BF16)
    return high, (value - high.astype(F32)).astype(BF16)


def dot(left, right, dims=NN):
    return lax.dot_general(left, right, dims, preferred_element_type=F32)


def dot3(left, right, dims=NN):
    return dot(left[0], right[0], dims) + dot(left[0], right[1], dims) + dot(left[1], right[0], dims)


def dot2(left, right, dims=NN):
    return dot(left, right[0], dims) + dot(left, right[1], dims)


def block_at(step):
    return pl.ds(pl.multiple_of(step * BLOCK, BLOCK), BLOCK)


def pair_at(refs, rows):
    return refs[0][rows, :], refs[1][rows, :]


def put_pair(refs, rows, value):
    high, low = split(value)
    refs[0][rows, :] = high
    refs[1][rows, :] = low


def spread(index_row):
    return jnp.transpose(jnp.broadcast_to(index_row, (128, index_row.shape[1])))


def hot_rows(spread_block, first, width):
    lane = lax.broadcasted_iota(jnp.int32, (spread_block.shape[0], 128), 1)
    local = spread_block - first
    tiles = [jnp.where(local == lane + at, 1.0, 0.0).astype(BF16) for at in range(0, width, 128)]
    return jnp.concatenate(tiles, axis=1)


def hot_columns(index_row, first, height):
    row = lax.broadcasted_iota(jnp.int32, (height, index_row.shape[1]), 0) + first
    return jnp.where(row == index_row, 1.0, 0.0).astype(BF16)


def sigmoid(value):
    return 1.0 / (1.0 + jnp.exp(-value))


def mean(value):
    return jnp.sum(value, axis=1, keepdims=True) * (1.0 / FEAT)


def norm(value):
    center = value - mean(value)
    scale = lax.rsqrt(mean(center * center) + 1e-05)
    return center * scale, scale


def norm_back(grad, normed, scale):
    return scale * (grad - mean(grad) - normed * mean(grad * normed))


def put_tiles(ref, value):
    for at in range(FEAT // 128):
        ref[:, at] = value[:, at * 128 : (at + 1) * 128].reshape(-1, 8, 128)


def vmem_specs(count):
    return [pl.BlockSpec(memory_space=pltpu.VMEM)] * count


def local_call(kernel, outs, scratch, flops, *args):
    moved = sum(math.prod(a.shape) * 4 for a in args) + sum(math.prod(o.shape) * 4 for o in outs)
    return pl.pallas_call(
        kernel,
        out_shape=outs,
        in_specs=vmem_specs(len(args)),
        out_specs=vmem_specs(len(outs)),
        scratch_shapes=scratch,
        compiler_params=pltpu.CompilerParams(vmem_limit_bytes=LOCAL_BYTES),
        cost_estimate=pl.CostEstimate(flops=int(flops), bytes_accessed=moved, transcendentals=0),
    )(*args)


def f32_out(*shape):
    return jax.ShapeDtypeStruct(shape, F32)


def bf16_out(*shape):
    return jax.ShapeDtypeStruct(shape, BF16)


TILES = f32_out(64, 4, 8, 128)


STRIDES = (32, 8, 2)
ALL_PARTS = tuple((part % 3, part // 3) for part in range(6))
FOUR_PARTS = ALL_PARTS[:4]
GOT_CHUNKS = 127
SEM_COUNT = 24


def axis_places(device):
    return [(device // 32) % 4, (device // 8) % 4, (device // 2) % 4], device % 2


def axis_bits(place):
    return ((place + 1) // 2) % 2, place // 2


def position(device, spec):
    places, core = axis_places(device)
    first, flip = spec
    bits = axis_bits(places[first])
    spot = (core * 2 + bits[flip]) * 2 + bits[1 - flip]
    return (spot * 4 + places[(first + 1) % 3]) * 4 + places[(first + 2) % 3]


class Exchange:
    def __init__(self, specs, buf, got, out, sends, recvs):
        self.specs, self.buf, self.got, self.out, self.sends, self.recvs = specs, buf, got, out, sends, recvs
        self.me = lax.axis_index("patch")
        self.places, self.core = axis_places(self.me)
        self.mate = self.me + 1 - 2 * self.core
        self.bits = [axis_bits(place) for place in self.places]
        self.flying = {}
        self.spot = {}
        for part, (first, flip) in enumerate(specs):
            one, two = self.bits[first][flip], self.bits[first][1 - flip]
            third, fourth = self.places[(first + 1) % 3], self.places[(first + 2) % 3]
            at_core = self.core * 64
            at_one = at_core + one * 32
            at_two = at_one + two * 16
            at_three = at_two + third * 4
            self.spot[part] = dict(
                one=one, two=two, core=at_core, first=at_one, second=at_two, third=at_three, last=at_three + fourth
            )

    def greet(self):
        mates = [self.mate]
        mates += [self.peer(axis, shift) for axis in range(3) for shift in (1, 2, 3)]
        barrier = pltpu.get_barrier_semaphore()
        for mate in mates:
            pl.semaphore_signal(barrier, inc=1, device_id=(mate,), device_id_type=MESH)
        pl.semaphore_wait(barrier, len(mates))

    def peer(self, axis, shift):
        return self.me + ((self.places[axis] + shift) % 4 - self.places[axis]) * STRIDES[axis]

    def neighbour(self, axis, flip):
        place = self.places[axis]
        step = 3 - 2 * place if flip else 1 - 2 * (place % 2)
        return self.me + step * STRIDES[axis]

    def push(self, part, sem, src, dst, device):
        copy = pltpu.make_async_remote_copy(
            src_ref=src,
            dst_ref=dst,
            send_sem=self.sends.at[sem, part],
            recv_sem=self.recvs.at[sem, part],
            device_id=(device,),
            device_id_type=MESH,
        )
        copy.start()
        self.flying[part, sem] = copy

    def wait(self, part, *sems):
        for sem in sems:
            self.flying.pop((part, sem)).wait()

    def send_sum(self, part, sem, at, size, slot, device):
        self.push(part, sem, self.buf.at[part, pl.ds(at, size)], self.got.at[part, pl.ds(slot, size)], device)

    def add(self, part, at, size, *slots):
        total = self.buf[part, pl.ds(at, size)]
        for slot in slots:
            total += self.got[part, pl.ds(slot, size)]
        self.buf[part, pl.ds(at, size)] = total

    def send_block(self, part, sem, at, size, device):
        block = self.out.at[part, pl.ds(at, size)]
        self.push(part, sem, block, block, device)


    def start(self, part):
        spot = self.spot[part]
        other = 64 - spot["core"]
        self.send_sum(part, 0, other + (1 - spot["one"]) * 32, 32, 0, self.mate)

    def start_kept(self, part):
        spot = self.spot[part]
        other = 64 - spot["core"]
        self.send_sum(part, 1, other + spot["one"] * 32, 32, 32, self.mate)

    def reduce_first(self, part):
        spot = self.spot[part]
        first, flip = self.specs[part]
        away = spot["core"] + (1 - spot["one"]) * 32
        device = self.neighbour(first, flip)
        self.wait(part, 0)
        self.add(part, away, 32, 0)
        self.send_sum(part, 2, away + (1 - spot["two"]) * 16, 16, 64, device)
        self.send_sum(part, 3, away + spot["two"] * 16, 16, 80, device)

    def reduce_kept(self, part):
        self.wait(part, 1)
        self.add(part, self.spot[part]["first"], 32, 32)

    def reduce_second(self, part):
        spot = self.spot[part]
        first, flip = self.specs[part]
        away = spot["first"] + (1 - spot["two"]) * 16
        self.wait(part, 2)
        self.add(part, away, 16, 64)
        self.send_sum(part, 4, away, 16, 96, self.neighbour(first, 1 - flip))

    def reduce_third(self, part):
        spot = self.spot[part]
        axis = (self.specs[part][0] + 1) % 3
        self.wait(part, 3, 4)
        self.add(part, spot["second"], 16, 80, 96)
        for shift in (1, 2, 3):
            at = spot["second"] + (self.places[axis] + shift) % 4 * 4
            self.send_sum(part, 4 + shift, at, 4, 108 + 4 * shift, self.peer(axis, shift))

    def reduce_fourth(self, part):
        spot = self.spot[part]
        axis = (self.specs[part][0] + 2) % 3
        self.wait(part, 5, 6, 7)
        self.add(part, spot["third"], 4, 112, 116, 120)
        for shift in (1, 2, 3):
            at = spot["third"] + (self.places[axis] + shift) % 4
            self.send_sum(part, 7 + shift, at, 1, 123 + shift, self.peer(axis, shift))

    def reduce_last(self, part):
        self.wait(part, 8, 9, 10)
        self.add(part, self.spot[part]["last"], 1, 124, 125, 126)

    def gather_fourth(self, part):
        axis = (self.specs[part][0] + 2) % 3
        for shift in (1, 2, 3):
            self.send_block(part, 10 + shift, self.spot[part]["last"], 1, self.peer(axis, shift))

    def gather_third(self, part):
        axis = (self.specs[part][0] + 1) % 3
        self.wait(part, 11, 12, 13)
        for shift in (1, 2, 3):
            self.send_block(part, 13 + shift, self.spot[part]["third"], 4, self.peer(axis, shift))

    def gather_second(self, part):
        spot = self.spot[part]
        first, flip = self.specs[part]
        self.wait(part, 14, 15, 16)
        self.send_block(part, 17, spot["second"], 16, self.neighbour(first, 1 - flip))
        self.send_block(part, 20, spot["second"], 16, self.mate)

    def gather_first(self, part):
        spot = self.spot[part]
        first, flip = self.specs[part]
        device = self.neighbour(first, flip)
        self.wait(part, 17)
        self.send_block(part, 18, spot["first"], 16, device)
        self.send_block(part, 19, spot["first"] + 16, 16, device)
        self.send_block(part, 21, spot["first"] + (1 - spot["two"]) * 16, 16, self.mate)

    def gather_core(self, part):
        spot = self.spot[part]
        self.wait(part, 18)
        self.send_block(part, 22, spot["core"] + (1 - spot["one"]) * 32, 16, self.mate)

    def gather_rest(self, part):
        spot = self.spot[part]
        self.wait(part, 19)
        self.send_block(part, 23, spot["core"] + (1 - spot["one"]) * 32 + 16, 16, self.mate)

    def gather_last(self, part):
        self.wait(part, 20, 21, 22, 23)

    REDUCE = ("reduce_first", "reduce_kept", "reduce_second", "reduce_third", "reduce_fourth", "reduce_last")
    GATHER = ("gather_fourth", "gather_third", "gather_second", "gather_first", "gather_core", "gather_rest", "gather_last")

    def run(self, stages, beside=()):
        beside = list(beside)
        for stage in stages:
            if beside:
                beside.pop(0)()
            for part in range(len(self.specs)):
                getattr(self, stage)(part)
        for work in beside:
            work()

    def finish_sum(self, part):
        self.reduce_last(part)
        last = pl.ds(self.spot[part]["last"], 1)
        self.out[part, last] = self.buf[part, last]
        self.gather_fourth(part)

    SUM = REDUCE[:-1] + ("finish_sum",) + GATHER[1:]


def exchange_scratch(parts, units):
    sem = pltpu.SemaphoreType.DMA((SEM_COUNT, parts))
    return [
        pltpu.VMEM((parts, 128, units, 8, 128), F32),
        pltpu.VMEM((parts, GOT_CHUNKS, units, 8, 128), F32),
        sem,
        sem,
    ]


def sum_out(units):
    return f32_out(LINKS, 128, units, 8, 128)


def remote_call(kernel, name_id, outs, scratch, limit, *args):
    return pl.pallas_call(
        kernel,
        out_shape=outs,
        in_specs=vmem_specs(len(args)),
        out_specs=vmem_specs(len(outs)),
        scratch_shapes=scratch,
        compiler_params=pltpu.CompilerParams(collective_id=name_id, has_side_effects=True, vmem_limit_bytes=limit << 20),
        cost_estimate=pl.CostEstimate(flops=int(3e10), bytes_accessed=int(3e7), transcendentals=0),
    )(*args)


def node_pass(feats, agg, cot, w_in, w_out):
    feat_pair, agg_pair = split(feats), split(agg)
    pre = dot3(feat_pair, pair_at(w_in, pl.ds(0, FEAT))) + dot3(agg_pair, pair_at(w_in, pl.ds(FEAT, FEAT)))
    gate = sigmoid(pre)
    hidden = split(pre * gate)
    out_pair = (w_out[0][...], w_out[1][...])
    normed, scale = norm(dot3(hidden, out_pair))
    tail = split(norm_back(cot, normed, scale))
    grad_pre = split(dot3(tail, out_pair, NT) * (gate * (1.0 + pre * (1.0 - gate))))
    return feat_pair, agg_pair, hidden, tail, grad_pre


def node_kernel(*refs):
    agg_ref, fine_ref, cot_ref, few_ref, few_cot_ref, w_in_ref, w_out_ref = refs[:7]
    grad_agg_ref, own_ref, direct_ref, node_ref = refs[7:11]
    buf, got, sends, recvs, full, wi0, wi1, wo0, wo1, total = refs[11:]
    ring = Exchange(FOUR_PARTS, buf, got, full, sends, recvs)
    ring.greet()
    for part, spec in enumerate(FOUR_PARTS):
        for device in range(128):
            first = FINE + 8 * device
            if first < NEAR and 8 * device < COARSE:
                buf[part, position(device, spec), 0] = agg_ref[first : first + 8, part * 128 : (part + 1) * 128]
            else:
                buf[part, position(device, spec), 0] = jnp.zeros((8, 128), F32)
        ring.start(part)
    for part in range(4):
        ring.start_kept(part)

    wi, wo = (wi0, wi1), (wo0, wo1)
    keep = {}

    def cut_weights():
        wi0[...], wi1[...] = split(w_in_ref[...])
        wo0[...], wo1[...] = split(w_out_ref[...])

    def fine_pass():
        keep["fine"] = node_pass(fine_ref[...], agg_ref[:FINE, :], cot_ref[...], wi, wo)

    def fine_back():
        grad_pre = keep["fine"][4]
        own_ref[...] = cot_ref[...] + dot3(grad_pre, pair_at(wi, pl.ds(0, FEAT)), NT)
        grad_agg_ref[:FINE, :] = dot3(grad_pre, pair_at(wi, pl.ds(FEAT, FEAT)), NT)

    def nothing():
        pass

    ring.run(ring.REDUCE, [nothing, cut_weights, nothing, fine_pass, fine_back])

    few_agg = jnp.concatenate([buf[part, ring.spot[part]["last"], 0] for part in range(4)], axis=1)
    blank = jnp.zeros((8, FEAT), F32)
    few = node_pass(
        jnp.concatenate([few_ref[...], blank], axis=0),
        jnp.concatenate([few_agg, blank], axis=0),
        jnp.concatenate([few_cot_ref[...], blank], axis=0),
        wi,
        wo,
    )
    few_grad = dot3(few[4], pair_at(wi, pl.ds(FEAT, FEAT)), NT)[:8]
    for part in range(4):
        full[part, ring.spot[part]["last"], 0] = few_grad[:, part * 128 : (part + 1) * 128]

    def few_back():
        direct = few_cot_ref[...] + dot3(few[4], pair_at(wi, pl.ds(0, FEAT)), NT)[:8]
        for at in range(4):
            direct_ref[at] = direct[:, at * 128 : (at + 1) * 128]

    def weights_back(which, grad, first):
        def run():
            total[...] = dot3(keep["fine"][which], keep["fine"][grad], TN) + dot3(few[which], few[grad], TN)
            put_tiles(node_ref.at[pl.ds(first, 64)], total)

        return run

    beside = [nothing, few_back, weights_back(0, 4, 0), weights_back(1, 4, 64), weights_back(2, 3, 128)]
    ring.run(ring.GATHER, beside)
    for part, spec in enumerate(FOUR_PARTS):
        for device in range((NEAR - FINE) // 8):
            first = FINE + 8 * device
            grad_agg_ref[first : first + 8, part * 128 : (part + 1) * 128] = full[part, position(device, spec), 0]


def node_step(agg, fine, cot_fine, few, few_cot, w_in, w_out):
    half = pltpu.VMEM((2 * FEAT, FEAT), BF16)
    quarter = pltpu.VMEM((FEAT, FEAT), BF16)
    return remote_call(
        node_kernel,
        2,
        [f32_out(NEAR, FEAT), f32_out(FINE, FEAT), f32_out(4, 8, 128), f32_out(192, 4, 8, 128)],
        exchange_scratch(4, 1)
        + [pltpu.VMEM((4, 128, 1, 8, 128), F32), half, half, quarter, quarter, pltpu.VMEM((FEAT, FEAT), F32)],
        34,
        agg,
        fine,
        cot_fine,
        few,
        few_cot,
        w_in,
        w_out,
    )


CHIPS = 64


class Shuffle:
    def __init__(self, sends, recvs, core_sends, core_recvs):
        self.sends, self.recvs, self.core_sends, self.core_recvs = sends, recvs, core_sends, core_recvs
        self.me = lax.axis_index("patch")
        self.places, self.core = axis_places(self.me)
        self.chip = self.me // 2
        self.mate = self.me + 1 - 2 * self.core

    def other(self, step):
        z, x, y = ((place + step // span) % 4 for place, span in zip(self.places, (16, 4, 1)))
        return z * 16 + x * 4 + y

    def each(self, run):
        def body(step, carry):
            run(self.other(step))
            return carry

        lax.fori_loop(1, CHIPS, body, 0)

    def signal(self):
        barrier = pltpu.get_barrier_semaphore()

        def run(chip):
            pl.semaphore_signal(barrier, inc=1, device_id=(chip * 2 + self.core,), device_id_type=MESH)

        self.each(run)
        pl.semaphore_signal(barrier, inc=1, device_id=(self.mate,), device_id_type=MESH)

    def wait_signals(self):
        pl.semaphore_wait(pltpu.get_barrier_semaphore(), CHIPS)

    def copy(self, src, dst, sends, recvs, device):
        return pltpu.make_async_remote_copy(
            src_ref=src, dst_ref=dst, send_sem=sends, recv_sem=recvs, device_id=(device,), device_id_type=MESH
        )

    def send_chips(self, src, dst):
        def run(chip):
            self.copy(src.at[chip], dst.at[self.chip], self.sends, self.recvs, chip * 2 + self.core).start()

        self.each(run)
        dst[self.chip] = src[self.chip]

    def wait_chips(self, src, dst):
        most = pl.ds(0, CHIPS - 1)
        self.copy(src.at[most], dst.at[most], self.sends, self.recvs, self.mate).wait()

    def core_copy(self, src, dst):
        return self.copy(src, dst, self.core_sends, self.core_recvs, self.mate)


def front_kernel(*refs):
    fine_ref, near_ref, edge_ref, w_ref, w_out_ref, list_ref, send_ref, recv_ref = refs[:8]
    pre_ref, normed_ref, scale_ref, agg_ref = refs[8:12]
    outgoing, got, from_mate, p0, p1, q0, q1, h0, h1, n0, n1, rep, recv_rep = refs[12:25]
    shuffle = Shuffle(*refs[25:])
    shuffle.signal()
    w_send = split(w_ref[FEAT : 2 * FEAT, :])
    own = split(dot3(split(fine_ref[...]), w_send))
    p0[pl.ds(0, FINE), :], p1[pl.ds(0, FINE), :] = own
    rep[...] = spread(list_ref[...])

    def request(at, carry):
        rows = block_at(at)
        chips = pl.ds(at * (BLOCK // 16), BLOCK // 16)
        outgoing[chips] = dot2(hot_rows(rep[rows, :], 0, FINE), own).reshape(BLOCK // 16, 2, 8, FEAT)
        return carry

    lax.fori_loop(0, EDGE // BLOCK, request, 0)
    shuffle.wait_signals()
    shuffle.send_chips(outgoing, got)

    rep[...] = spread(send_ref[...])
    recv_rep[...] = spread(recv_ref[...])
    w_recv = split(w_ref[2 * FEAT :, :])
    put_pair((q0, q1), pl.ds(0, FINE), dot3(split(near_ref[:FINE, :]), w_recv))

    def project(at, carry):
        rows = block_at(at)
        feats = split(near_ref[rows, :])
        put_pair((p0, p1), rows, dot3(feats, w_send))
        put_pair((q0, q1), rows, dot3(feats, w_recv))
        return carry

    lax.fori_loop(1, NEAR // BLOCK, project, 0)
    w_edge = split(w_ref[:FEAT, :])

    def near_step(at, carry):
        rows = block_at(at)
        total = dot3(split(edge_ref[rows, :]), w_edge)
        total += dot2(hot_rows(recv_rep[rows, :], 0, NEAR), (q0[...], q1[...]))
        total += dot2(hot_rows(rep[rows, :], 0, NEAR), (p0[...], p1[...]))
        pre_ref[rows, :] = total
        return carry

    lax.fori_loop(0, EDGE // BLOCK, near_step, 0)

    shuffle.wait_chips(outgoing, got)
    swap = shuffle.core_copy(got.at[:, 1 - shuffle.core], from_mate)
    swap.start()
    half = CHIPS * 8
    put_pair((h0, h1), pl.ds(0, half), got[:, shuffle.core].reshape(half, FEAT))
    w_out = split(w_out_ref[...])
    swap.wait()
    put_pair((h0, h1), pl.ds(half, half), from_mate[...].reshape(half, FEAT))

    def edge_step(at, carry):
        rows = block_at(at)
        pre = pre_ref[rows, :] + dot2(hot_rows(rep[rows, :], NEAR, EDGE), (h0[...], h1[...]))
        pre_ref[rows, :] = pre
        normed, scale = norm(dot3(split(pre * sigmoid(pre)), w_out))
        normed_ref[rows, :] = normed
        scale_ref[rows, :] = jnp.broadcast_to(scale, (BLOCK, 128))
        put_pair((n0, n1), rows, edge_ref[rows, :] + normed)
        return carry

    lax.fori_loop(0, EDGE // BLOCK, edge_step, 0)

    def gather(at, carry):
        rows = block_at(at)
        agg_ref[rows, :] = dot2(hot_columns(recv_ref[...], at * BLOCK, BLOCK), (n0[...], n1[...]))
        return carry

    lax.fori_loop(0, NEAR // BLOCK, gather, 0)


def back_kernel(*refs):
    grad_agg_ref, cot_ref, pre_ref, normed_ref, scale_ref, w_out_ref, send_ref, recv_ref = refs[:8]
    edge_ref, near_ref, w_ref, list_ref, direct_ref = refs[8:13]
    grad_edges_ref, grad_fine_ref, in_edge_ref, out_ref, in_recv_ref, coarse_ref, in_send_ref = refs[13:20]
    t0, t1, d0, d1, a0, a1, recv_rep, for_mate, pack, back = refs[20:30]
    edge_total, tail_total, recv_total, send_total = refs[30:34]
    shuffle = Shuffle(*refs[34:])
    shuffle.signal()
    recv_rep[...] = spread(recv_ref[...])
    a0[...], a1[...] = split(grad_agg_ref[...])
    w_out = split(w_out_ref[...])

    def step(at, carry):
        rows = block_at(at)
        grad = cot_ref[rows, :] + dot2(hot_rows(recv_rep[rows, :], 0, NEAR), (a0[...], a1[...]))
        grad_edges_ref[rows, :] = grad
        tail = split(norm_back(grad, normed_ref[rows, :], scale_ref[rows, :1]))
        t0[rows, :], t1[rows, :] = tail
        pre = pre_ref[rows, :]
        gate = sigmoid(pre)
        put_pair((d0, d1), rows, dot3(tail, w_out, NT) * (gate * (1.0 + pre * (1.0 - gate))))
        return carry

    lax.fori_loop(0, EDGE // BLOCK, step, 0)

    def halo_rows(first, at):
        rows = dot2(hot_columns(send_ref[...], NEAR + first + at * BLOCK, BLOCK), (d0[...], d1[...]))
        return rows.reshape(BLOCK // 8, 8, FEAT)

    half = CHIPS * 8

    def to_mate(at, carry):
        for_mate[pl.ds(at * (BLOCK // 8), BLOCK // 8)] = halo_rows(half, at)
        return carry

    def to_pack(at, carry):
        pack[pl.ds(at * (BLOCK // 8), BLOCK // 8), 0] = halo_rows(0, at)
        return carry

    lax.fori_loop(0, half // BLOCK, to_mate, 0)
    shuffle.wait_signals()
    swap = shuffle.core_copy(for_mate, pack.at[:, 1])
    swap.start()
    lax.fori_loop(0, half // BLOCK, to_pack, 0)
    swap.wait()
    shuffle.send_chips(pack, back)

    edge_total[...] = jnp.zeros_like(edge_total)
    tail_total[...] = jnp.zeros_like(tail_total)
    w_edge = split(w_ref[:FEAT, :])

    def weight_step(at, carry):
        rows = block_at(at)
        grad_pre = (d0[rows, :], d1[rows, :])
        grad_edges_ref[rows, :] += dot3(grad_pre, w_edge, NT)
        edge_total[...] += dot3(split(edge_ref[rows, :]), grad_pre, TN)
        pre = pre_ref[rows, :]
        tail_total[...] += dot3(split(pre * sigmoid(pre)), (t0[rows, :], t1[rows, :]), TN)
        return carry

    lax.fori_loop(0, EDGE // BLOCK, weight_step, 0)
    put_tiles(in_edge_ref, edge_total)
    put_tiles(out_ref, tail_total)
    w_send = split(w_ref[FEAT : 2 * FEAT, :])
    w_recv = split(w_ref[2 * FEAT :, :])

    def sums(at):
        grad_pre = (d0[...], d1[...])
        sent = dot2(hot_columns(send_ref[...], at * BLOCK, BLOCK), grad_pre)
        return sent, split(dot2(hot_columns(recv_ref[...], at * BLOCK, BLOCK), grad_pre))

    fine_sent, received = sums(0)
    grad_fine_ref[...] = direct_ref[...] + dot3(received, w_recv, NT)
    recv_total[...] = dot3(split(near_ref[:FINE, :]), received, TN)
    send_total[...] = jnp.zeros_like(send_total)

    def coarse_step(at, carry):
        rows = block_at(at)
        sent, received = sums(at)
        sent = split(sent)
        value = dot3(sent, w_send, NT) + dot3(received, w_recv, NT)
        put_tiles(coarse_ref.at[pl.ds((at - 1) * (BLOCK // 8), BLOCK // 8)], value)
        feats = split(near_ref[rows, :])
        recv_total[...] += dot3(feats, received, TN)
        send_total[...] += dot3(feats, sent, TN)
        return carry

    lax.fori_loop(1, NEAR // BLOCK, coarse_step, 0)
    put_tiles(in_recv_ref, recv_total)

    shuffle.wait_chips(pack, back)
    returned = split(back[...].reshape(EDGE, FEAT))
    fine_sent = split(fine_sent + dot2(hot_columns(list_ref[...], 0, FINE), returned))
    grad_fine_ref[...] += dot3(fine_sent, w_send, NT)
    send_total[...] += dot3(split(near_ref[:FINE, :]), fine_sent, TN)
    put_tiles(in_send_ref, send_total)


OUT_ROW, EDGE_ROW, RECV_ROW, COARSE_ROW, SEND_ROW, ROWS = 192, 256, 320, 384, 480, 576


def sum_kernel(*refs):
    node_ref, out_ref, in_edge_ref, in_recv_ref, coarse_ref, in_send_ref, direct_ref = refs[:7]
    sum_ref, buf, got, sends, recvs = refs[7:]
    flat = buf.reshape(ROWS * 4, 8, 128)
    ring = Exchange(ALL_PARTS, buf, got, sum_ref, sends, recvs)
    ring.greet()
    started = 0
    row = 0
    for ref in (node_ref, out_ref, in_edge_ref, in_recv_ref, coarse_ref, in_send_ref):
        size = ref.shape[0]
        flat[row * 4 : (row + size) * 4] = ref[...].reshape(size * 4, 8, 128)
        if row == COARSE_ROW:
            flat[pl.ds(row * 4 + ring.me % 96 * 4, 4)] += direct_ref[...]
        row += size
        if row == SEND_ROW + 64:
            flat[row * 4 :] = jnp.zeros(((ROWS - row) * 4, 8, 128), F32)
            row = ROWS
        while started < LINKS and (started + 1) * (ROWS // LINKS) <= row:
            ring.start(started)
            started += 1
    for part in range(LINKS):
        ring.start_kept(part)
    ring.run(ring.SUM)


def put_rows(ref, tiles, scale):
    for at in range(FEAT // 128):
        ref[:, at * 128 : (at + 1) * 128] = (tiles[:, at] * scale).reshape(-1, 128)


def finish_kernel(edge_scale, node_scale, sum_ref, coarse_ref, in_ref, out_ref, node_in_ref, node_out_ref):
    tiles = sum_ref.reshape(ROWS, 4, 8, 128)
    for place, row in enumerate((EDGE_ROW, SEND_ROW, RECV_ROW)):
        put_rows(in_ref.at[pl.ds(place * FEAT, FEAT)], tiles[row : row + 64], edge_scale)
    put_rows(out_ref, tiles[OUT_ROW : OUT_ROW + 64], edge_scale)
    whole = COARSE // 8
    put_rows(coarse_ref.at[pl.ds(0, whole * 8)], tiles[COARSE_ROW : COARSE_ROW + whole], 1.0)
    for at in range(FEAT // 128):
        coarse_ref[whole * 8 :, at * 128 : (at + 1) * 128] = tiles[COARSE_ROW + whole, at][: COARSE - whole * 8]
    put_rows(node_in_ref, tiles[0:128], node_scale)
    put_rows(node_out_ref, tiles[128:192], node_scale)


def per_device(
    fine_nodes,
    coarse_nodes,
    edge_feats,
    senders,
    receivers,
    send_rows,
    w_edge_in,
    w_edge_out,
    w_node_in,
    w_node_out,
    cot_fine,
    cot_coarse,
    cot_edges,
):
    me = lax.axis_index("patch")
    peers = lax.axis_size("patch")
    core = me % 2
    near_count = FINE + COARSE
    send_list = send_rows.reshape(CHIPS, 2, 8)
    back_list = jnp.where(core == 1, send_list[:, ::-1], send_list).reshape(1, EDGE)
    send_list = send_list.reshape(1, EDGE)
    halo = senders - near_count
    source = halo // 8
    halo_at = NEAR + (source % 2 != core) * (EDGE // 2) + source // 2 * 8 + halo % 8
    send_at = jnp.where(senders < near_count, senders, halo_at).astype(jnp.int32).reshape(1, EDGE)
    recv_at = receivers.reshape(1, EDGE)
    half = pltpu.VMEM((EDGE, FEAT), BF16)
    index = pltpu.VMEM((EDGE, 128), jnp.int32)
    square = pltpu.VMEM((FEAT, FEAT), F32)
    chip_rows = pltpu.VMEM((CHIPS, 2, 8, FEAT), F32)
    core_rows = pltpu.VMEM((CHIPS, 8, FEAT), F32)
    sems = [pltpu.SemaphoreType.DMA] * 4
    wide = f32_out(EDGE, FEAT)
    fine_out = f32_out(FINE, FEAT)

    near = jnp.concatenate([fine_nodes, coarse_nodes, jnp.zeros((NEAR - near_count, FEAT), F32)], axis=0)
    pre, normed, scale, agg = remote_call(
        front_kernel,
        1,
        [wide, wide, f32_out(EDGE, 128), wide],
        [chip_rows, chip_rows, core_rows] + [half] * 8 + [index] * 2 + sems,
        FRONT_MIB,
        fine_nodes,
        near,
        edge_feats,
        w_edge_in,
        w_edge_out,
        send_list,
        send_at,
        recv_at,
    )
    blank = jnp.zeros((8 * peers - COARSE, FEAT), F32)
    few = lax.dynamic_slice(jnp.concatenate([coarse_nodes, blank], axis=0), (me * 8, 0), (8, FEAT))
    few_cot = lax.dynamic_slice(jnp.concatenate([cot_coarse, blank], axis=0), (me * 8, 0), (8, FEAT))
    grad_agg, direct, few_direct, node = node_step(agg, fine_nodes, cot_fine, few, few_cot, w_node_in, w_node_out)
    grad_edges, grad_fine, in_edge, edge_out, in_recv, coarse, in_send = remote_call(
        back_kernel,
        3,
        [wide, fine_out, TILES, TILES, TILES, f32_out(96, 4, 8, 128), TILES],
        [half] * 6 + [index, core_rows, chip_rows, chip_rows] + [square] * 4 + sems,
        BACK_MIB,
        grad_agg,
        cot_edges,
        pre,
        normed,
        scale,
        w_edge_out,
        send_at,
        recv_at,
        edge_feats,
        near,
        w_edge_in,
        back_list,
        direct,
    )
    (summed,) = remote_call(
        sum_kernel, 4, [sum_out(3)], exchange_scratch(LINKS, 3), SUM_MIB, node, edge_out, in_edge, in_recv, coarse, in_send, few_direct
    )
    grad_coarse, grad_in, grad_out, grad_node_in, grad_node_out = local_call(
        functools.partial(
            finish_kernel, 1.0 / math.sqrt(EDGE * peers), 1.0 / math.sqrt(FINE * peers + COARSE)
        ),
        [f32_out(COARSE, FEAT), f32_out(3 * FEAT, FEAT), f32_out(FEAT, FEAT), f32_out(2 * FEAT, FEAT), f32_out(FEAT, FEAT)],
        [],
        1e6,
        summed,
    )
    return grad_fine, grad_coarse, grad_edges, grad_in, grad_out, grad_node_in, grad_node_out


def solution(mesh):
    return jax.shard_map(
        per_device,
        mesh=mesh,
        in_specs=(
            P("patch", None),
            P(),
            P("patch", None),
            P("patch"),
            P("patch"),
            P("patch", None, None),
            P(),
            P(),
            P(),
            P(),
            P("patch", None),
            P(),
            P("patch", None),
        ),
        out_specs=(P("patch", None), P(), P("patch", None), P(), P(), P(), P()),
        check_vma=False,
    )
```

```python
import functools
import math

import jax
import jax.numpy as jnp
from jax import lax
from jax.experimental import pallas as pl
from jax.experimental.pallas import tpu as pltpu
from jax.sharding import PartitionSpec as P

MESH = pl.DeviceIdType.MESH
F32 = jnp.float32
BF16 = jnp.bfloat16
FEAT = 512
FINE = 256
COARSE = 642
NEAR = 1024
EDGE = 1024
BLOCK = 256
LINKS = 6
WIDE = 512
FRONT_MIB, BACK_MIB, SUM_MIB = 38, 42, 30

NN = (((1,), (0,)), ((), ()))
NT = (((1,), (1,)), ((), ()))
TN = (((0,), (0,)), ((), ()))


def split(value):
    high = value.astype(BF16)
    return high, (value - high.astype(F32)).astype(BF16)


def dot(left, right, dims=NN):
    return lax.dot_general(left, right, dims, preferred_element_type=F32)


def dot3(left, right, dims=NN):
    return dot(left[0], right[0], dims) + dot(left[0], right[1], dims) + dot(left[1], right[0], dims)


def dot2(left, right, dims=NN):
    return dot(left, right[0], dims) + dot(left, right[1], dims)


def block_at(step, size=BLOCK):
    return pl.ds(pl.multiple_of(step * size, size), size)


def pair_at(refs, rows):
    return refs[0][rows, :], refs[1][rows, :]


def put_pair(refs, rows, value):
    high, low = split(value)
    refs[0][rows, :] = high
    refs[1][rows, :] = low


def spread(index_row):
    return jnp.transpose(jnp.broadcast_to(index_row, (128, index_row.shape[1])))


def hot_rows(spread_block, first, width):
    lane = lax.broadcasted_iota(jnp.int32, (spread_block.shape[0], 128), 1)
    local = spread_block - first
    tiles = [jnp.where(local == lane + at, 1.0, 0.0).astype(BF16) for at in range(0, width, 128)]
    return jnp.concatenate(tiles, axis=1)


def hot_columns(index_row, first, height):
    row = lax.broadcasted_iota(jnp.int32, (height, index_row.shape[1]), 0) + first
    return jnp.where(row == index_row, 1.0, 0.0).astype(BF16)


def sigmoid(value):
    return 1.0 / (1.0 + jnp.exp(-value))


def mean(value):
    return jnp.sum(value, axis=1, keepdims=True) * (1.0 / FEAT)


def norm(value):
    center = value - mean(value)
    scale = lax.rsqrt(mean(center * center) + 1e-05)
    return center * scale, scale


def norm_back(grad, normed, scale):
    return scale * (grad - mean(grad) - normed * mean(grad * normed))


def put_tiles(ref, value):
    for at in range(FEAT // 128):
        ref[:, at] = value[:, at * 128 : (at + 1) * 128].reshape(-1, 8, 128)


def vmem_specs(count):
    return [pl.BlockSpec(memory_space=pltpu.VMEM)] * count


def f32_out(*shape):
    return jax.ShapeDtypeStruct(shape, F32)


def bf16_out(*shape):
    return jax.ShapeDtypeStruct(shape, BF16)


TILES = f32_out(64, 4, 8, 128)


STRIDES = (32, 8, 2)
ALL_PARTS = tuple((part % 3, part // 3) for part in range(6))
FOUR_PARTS = ALL_PARTS[:4]
GOT_CHUNKS = 127
SEM_COUNT = 24


def axis_places(device):
    return [(device // 32) % 4, (device // 8) % 4, (device // 2) % 4], device % 2


def axis_bits(place):
    return ((place + 1) // 2) % 2, place // 2


def position(device, spec):
    places, core = axis_places(device)
    first, flip = spec
    bits = axis_bits(places[first])
    spot = (core * 2 + bits[flip]) * 2 + bits[1 - flip]
    return (spot * 4 + places[(first + 1) % 3]) * 4 + places[(first + 2) % 3]


class Exchange:
    def __init__(self, specs, buf, got, out, sends, recvs):
        self.specs, self.buf, self.got, self.out, self.sends, self.recvs = specs, buf, got, out, sends, recvs
        self.me = lax.axis_index("patch")
        self.places, self.core = axis_places(self.me)
        self.mate = self.me + 1 - 2 * self.core
        self.bits = [axis_bits(place) for place in self.places]
        self.flying = {}
        self.spot = {}
        for part, (first, flip) in enumerate(specs):
            one, two = self.bits[first][flip], self.bits[first][1 - flip]
            third, fourth = self.places[(first + 1) % 3], self.places[(first + 2) % 3]
            at_core = self.core * 64
            at_one = at_core + one * 32
            at_two = at_one + two * 16
            at_three = at_two + third * 4
            self.spot[part] = dict(
                one=one, two=two, core=at_core, first=at_one, second=at_two, third=at_three, last=at_three + fourth
            )

    def greet(self):
        mates = [self.mate]
        mates += [self.peer(axis, shift) for axis in range(3) for shift in (1, 2, 3)]
        barrier = pltpu.get_barrier_semaphore()
        for mate in mates:
            pl.semaphore_signal(barrier, inc=1, device_id=(mate,), device_id_type=MESH)
        pl.semaphore_wait(barrier, len(mates))

    def peer(self, axis, shift):
        return self.me + ((self.places[axis] + shift) % 4 - self.places[axis]) * STRIDES[axis]

    def neighbour(self, axis, flip):
        place = self.places[axis]
        step = 3 - 2 * place if flip else 1 - 2 * (place % 2)
        return self.me + step * STRIDES[axis]

    def push(self, part, sem, src, dst, device):
        copy = pltpu.make_async_remote_copy(
            src_ref=src,
            dst_ref=dst,
            send_sem=self.sends.at[sem, part],
            recv_sem=self.recvs.at[sem, part],
            device_id=(device,),
            device_id_type=MESH,
        )
        copy.start()
        self.flying[part, sem] = copy

    def wait(self, part, *sems):
        for sem in sems:
            self.flying.pop((part, sem)).wait()

    def send_sum(self, part, sem, at, size, slot, device):
        self.push(part, sem, self.buf.at[part, pl.ds(at, size)], self.got.at[part, pl.ds(slot, size)], device)

    def add(self, part, at, size, *slots):
        total = self.buf[part, pl.ds(at, size)]
        for slot in slots:
            total += self.got[part, pl.ds(slot, size)]
        self.buf[part, pl.ds(at, size)] = total

    def send_block(self, part, sem, at, size, device):
        block = self.out.at[part, pl.ds(at, size)]
        self.push(part, sem, block, block, device)


    def start(self, part):
        spot = self.spot[part]
        other = 64 - spot["core"]
        self.send_sum(part, 0, other + (1 - spot["one"]) * 32, 32, 0, self.mate)

    def start_kept(self, part):
        spot = self.spot[part]
        other = 64 - spot["core"]
        self.send_sum(part, 1, other + spot["one"] * 32, 32, 32, self.mate)

    def reduce_first(self, part):
        spot = self.spot[part]
        first, flip = self.specs[part]
        away = spot["core"] + (1 - spot["one"]) * 32
        device = self.neighbour(first, flip)
        self.wait(part, 0)
        self.add(part, away, 32, 0)
        self.send_sum(part, 2, away + (1 - spot["two"]) * 16, 16, 64, device)
        self.send_sum(part, 3, away + spot["two"] * 16, 16, 80, device)

    def reduce_kept(self, part):
        self.wait(part, 1)
        self.add(part, self.spot[part]["first"], 32, 32)

    def reduce_second(self, part):
        spot = self.spot[part]
        first, flip = self.specs[part]
        away = spot["first"] + (1 - spot["two"]) * 16
        self.wait(part, 2)
        self.add(part, away, 16, 64)
        self.send_sum(part, 4, away, 16, 96, self.neighbour(first, 1 - flip))

    def reduce_third(self, part):
        spot = self.spot[part]
        axis = (self.specs[part][0] + 1) % 3
        self.wait(part, 3, 4)
        self.add(part, spot["second"], 16, 80, 96)
        for shift in (1, 2, 3):
            at = spot["second"] + (self.places[axis] + shift) % 4 * 4
            self.send_sum(part, 4 + shift, at, 4, 108 + 4 * shift, self.peer(axis, shift))

    def reduce_fourth(self, part):
        spot = self.spot[part]
        axis = (self.specs[part][0] + 2) % 3
        self.wait(part, 5, 6, 7)
        self.add(part, spot["third"], 4, 112, 116, 120)
        for shift in (1, 2, 3):
            at = spot["third"] + (self.places[axis] + shift) % 4
            self.send_sum(part, 7 + shift, at, 1, 123 + shift, self.peer(axis, shift))

    def reduce_last(self, part):
        self.wait(part, 8, 9, 10)
        self.add(part, self.spot[part]["last"], 1, 124, 125, 126)

    def gather_fourth(self, part):
        axis = (self.specs[part][0] + 2) % 3
        for shift in (1, 2, 3):
            self.send_block(part, 10 + shift, self.spot[part]["last"], 1, self.peer(axis, shift))

    def gather_third(self, part):
        axis = (self.specs[part][0] + 1) % 3
        self.wait(part, 11, 12, 13)
        for shift in (1, 2, 3):
            self.send_block(part, 13 + shift, self.spot[part]["third"], 4, self.peer(axis, shift))

    def gather_second(self, part):
        spot = self.spot[part]
        first, flip = self.specs[part]
        self.wait(part, 14, 15, 16)
        self.send_block(part, 17, spot["second"], 16, self.neighbour(first, 1 - flip))
        self.send_block(part, 20, spot["second"], 16, self.mate)

    def gather_first(self, part):
        spot = self.spot[part]
        first, flip = self.specs[part]
        device = self.neighbour(first, flip)
        self.wait(part, 17)
        self.send_block(part, 18, spot["first"], 16, device)
        self.send_block(part, 19, spot["first"] + 16, 16, device)
        self.send_block(part, 21, spot["first"] + (1 - spot["two"]) * 16, 16, self.mate)

    def gather_core(self, part):
        spot = self.spot[part]
        self.wait(part, 18)
        self.send_block(part, 22, spot["core"] + (1 - spot["one"]) * 32, 16, self.mate)

    def gather_rest(self, part):
        spot = self.spot[part]
        self.wait(part, 19)
        self.send_block(part, 23, spot["core"] + (1 - spot["one"]) * 32 + 16, 16, self.mate)

    def gather_last(self, part):
        self.wait(part, 20, 21, 22, 23)

    REDUCE = ("reduce_first", "reduce_kept", "reduce_second", "reduce_third", "reduce_fourth", "reduce_last")
    GATHER = ("gather_fourth", "gather_third", "gather_second", "gather_first", "gather_core", "gather_rest", "gather_last")

    def run(self, stages, beside=()):
        beside = list(beside)
        for stage in stages:
            if beside:
                beside.pop(0)()
            for part in range(len(self.specs)):
                getattr(self, stage)(part)
        for work in beside:
            work()

    def finish_sum(self, part):
        self.reduce_last(part)
        last = pl.ds(self.spot[part]["last"], 1)
        self.out[part, last] = self.buf[part, last]
        self.gather_fourth(part)

    SUM = REDUCE[:-1] + ("finish_sum",) + GATHER[1:]


def exchange_scratch(parts, units):
    sem = pltpu.SemaphoreType.DMA((SEM_COUNT, parts))
    return [
        pltpu.VMEM((parts, 128, units, 8, 128), F32),
        pltpu.VMEM((parts, GOT_CHUNKS, units, 8, 128), F32),
        sem,
        sem,
    ]


def sum_out(units):
    return f32_out(LINKS, 128, units, 8, 128)


def remote_call(kernel, name_id, outs, scratch, limit, *args):
    return pl.pallas_call(
        kernel,
        out_shape=outs,
        in_specs=vmem_specs(len(args)),
        out_specs=vmem_specs(len(outs)),
        scratch_shapes=scratch,
        compiler_params=pltpu.CompilerParams(collective_id=name_id, has_side_effects=True, vmem_limit_bytes=limit << 20),
        cost_estimate=pl.CostEstimate(flops=int(3e10), bytes_accessed=int(3e7), transcendentals=0),
    )(*args)


def few_dot3(left, right, dims=NN):
    count = left[0].shape[0]
    both = dot(jnp.concatenate(left, axis=0), right[0], dims)
    return both[:count] + both[count:] + dot(left[0], right[1], dims)


class NodePass:
    def __init__(self, product, w_in, w_out):
        self.product, self.w_in, self.w_out = product, w_in, w_out

    def first(self, feats, agg):
        self.feats, self.agg = split(feats), split(agg)
        pre = self.product(self.feats, pair_at(self.w_in, pl.ds(0, FEAT)))
        self.pre = pre + self.product(self.agg, pair_at(self.w_in, pl.ds(FEAT, FEAT)))
        self.gate = sigmoid(self.pre)
        self.hidden = split(self.pre * self.gate)

    def second(self):
        self.normed, self.scale = norm(self.product(self.hidden, pair_at(self.w_out, pl.ds(0, FEAT))))

    def third(self, cot):
        self.tail = split(norm_back(cot, self.normed, self.scale))
        grad = self.product(self.tail, pair_at(self.w_out, pl.ds(0, FEAT)), NT)
        self.grad = split(grad * (self.gate * (1.0 + self.pre * (1.0 - self.gate))))

    def back(self, first):
        return self.product(self.grad, pair_at(self.w_in, pl.ds(first, FEAT)), NT)


def node_kernel(*refs):
    agg_ref, fine_ref, cot_ref, few_ref, few_cot_ref, w_in_ref, w_out_ref = refs[:7]
    grad_agg_ref, own_ref, direct_ref, node_ref = refs[7:11]
    buf, got, sends, recvs, full, wi0, wi1, wo0, wo1, total = refs[11:]
    ring = Exchange(FOUR_PARTS, buf, got, full, sends, recvs)
    ring.greet()
    for part, spec in enumerate(FOUR_PARTS):
        for device in range(128):
            first = FINE + 8 * device
            if first < NEAR and 8 * device < COARSE:
                buf[part, position(device, spec), 0] = agg_ref[first : first + 8, part * 128 : (part + 1) * 128]
            else:
                buf[part, position(device, spec), 0] = jnp.zeros((8, 128), F32)
        ring.start(part)
    for part in range(4):
        ring.start_kept(part)

    wi, wo = (wi0, wi1), (wo0, wo1)
    fine = NodePass(dot3, wi, wo)
    few = NodePass(few_dot3, wi, wo)

    def cut_weights():
        wi0[...], wi1[...] = split(w_in_ref[...])
        wo0[...], wo1[...] = split(w_out_ref[...])

    def fine_first():
        fine.first(fine_ref[...], agg_ref[:FINE, :])

    def fine_third():
        fine.third(cot_ref[...])

    def fine_back():
        own_ref[...] = cot_ref[...] + fine.back(0)

    def fine_agg():
        grad_agg_ref[:FINE, :] = fine.back(FEAT)

    ring.run(ring.REDUCE, [cut_weights, fine_first, fine.second, fine_third, fine_back, fine_agg])

    few_agg = jnp.concatenate([buf[part, ring.spot[part]["last"], 0] for part in range(4)], axis=1)
    blank = jnp.zeros((8, FEAT), F32)
    few.first(jnp.concatenate([few_ref[...], blank], axis=0), jnp.concatenate([few_agg, blank], axis=0))
    few.second()
    few.third(jnp.concatenate([few_cot_ref[...], blank], axis=0))
    few_grad = few.back(FEAT)[:8]
    for part in range(4):
        full[part, ring.spot[part]["last"], 0] = few_grad[:, part * 128 : (part + 1) * 128]

    def few_back():
        direct = few_cot_ref[...] + few.back(0)[:8]
        for at in range(4):
            direct_ref[at] = direct[:, at * 128 : (at + 1) * 128]

    def weights_back(which, grad, first):
        def run():
            total[...] = dot3(getattr(fine, which), getattr(fine, grad), TN) + dot3(getattr(few, which), getattr(few, grad), TN)
            put_tiles(node_ref.at[pl.ds(first, 64)], total)

        return run

    def nothing():
        pass

    beside = [nothing, few_back]
    beside += [weights_back("feats", "grad", 0), weights_back("agg", "grad", 64), weights_back("hidden", "tail", 128)]
    ring.run(ring.GATHER, beside)
    for part, spec in enumerate(FOUR_PARTS):
        for device in range((NEAR - FINE) // 8):
            first = FINE + 8 * device
            grad_agg_ref[first : first + 8, part * 128 : (part + 1) * 128] = full[part, position(device, spec), 0]


def node_step(agg, fine, cot_fine, few, few_cot, w_in, w_out):
    half = pltpu.VMEM((2 * FEAT, FEAT), BF16)
    quarter = pltpu.VMEM((FEAT, FEAT), BF16)
    return remote_call(
        node_kernel,
        2,
        [f32_out(NEAR, FEAT), f32_out(FINE, FEAT), f32_out(4, 8, 128), f32_out(192, 4, 8, 128)],
        exchange_scratch(4, 1)
        + [pltpu.VMEM((4, 128, 1, 8, 128), F32), half, half, quarter, quarter, pltpu.VMEM((FEAT, FEAT), F32)],
        34,
        agg,
        fine,
        cot_fine,
        few,
        few_cot,
        w_in,
        w_out,
    )


CHIPS = 64


class Shuffle:
    def __init__(self, sends, recvs, core_sends, core_recvs):
        self.sends, self.recvs, self.core_sends, self.core_recvs = sends, recvs, core_sends, core_recvs
        self.me = lax.axis_index("patch")
        self.places, self.core = axis_places(self.me)
        self.chip = self.me // 2
        self.mate = self.me + 1 - 2 * self.core

    def other(self, step):
        z, x, y = ((place + step // span) % 4 for place, span in zip(self.places, (16, 4, 1)))
        return z * 16 + x * 4 + y

    def each(self, run):
        def body(step, carry):
            run(self.other(step))
            return carry

        lax.fori_loop(1, CHIPS, body, 0)

    def signal(self):
        barrier = pltpu.get_barrier_semaphore()

        def run(chip):
            pl.semaphore_signal(barrier, inc=1, device_id=(chip * 2 + self.core,), device_id_type=MESH)

        self.each(run)
        pl.semaphore_signal(barrier, inc=1, device_id=(self.mate,), device_id_type=MESH)

    def wait_signals(self):
        pl.semaphore_wait(pltpu.get_barrier_semaphore(), CHIPS)

    def copy(self, src, dst, sends, recvs, device):
        return pltpu.make_async_remote_copy(
            src_ref=src, dst_ref=dst, send_sem=sends, recv_sem=recvs, device_id=(device,), device_id_type=MESH
        )

    def send_chips(self, src, dst):
        def run(chip):
            self.copy(src.at[chip], dst.at[self.chip], self.sends, self.recvs, chip * 2 + self.core).start()

        self.each(run)
        dst[self.chip] = src[self.chip]

    def wait_chips(self, src, dst):
        most = pl.ds(0, CHIPS - 1)
        self.copy(src.at[most], dst.at[most], self.sends, self.recvs, self.mate).wait()

    def core_copy(self, src, dst):
        return self.copy(src, dst, self.core_sends, self.core_recvs, self.mate)


def front_kernel(*refs):
    fine_ref, near_ref, edge_ref, w_ref, w_out_ref, list_ref, send_ref, recv_ref = refs[:8]
    pre_ref, normed_ref, scale_ref, agg_ref = refs[8:12]
    outgoing, got, from_mate, p0, p1, q0, q1, h0, h1, n0, n1, rep, recv_rep = refs[12:25]
    shuffle = Shuffle(*refs[25:])
    shuffle.signal()
    w_send = split(w_ref[FEAT : 2 * FEAT, :])
    own = split(dot3(split(fine_ref[...]), w_send))
    rep[...] = spread(list_ref[...])

    def request(at, carry):
        rows = block_at(at, WIDE)
        chips = pl.ds(at * (WIDE // 16), WIDE // 16)
        outgoing[chips] = dot2(hot_rows(rep[rows, :], 0, FINE), own).reshape(WIDE // 16, 2, 8, FEAT)
        return carry

    lax.fori_loop(0, EDGE // WIDE, request, 0)
    shuffle.wait_signals()
    shuffle.send_chips(outgoing, got)

    rep[...] = spread(send_ref[...])
    recv_rep[...] = spread(recv_ref[...])
    w_recv = split(w_ref[2 * FEAT :, :])

    def project(at, carry):
        rows = block_at(at, WIDE)
        feats = split(near_ref[rows, :])
        put_pair((p0, p1), rows, dot3(feats, w_send))
        put_pair((q0, q1), rows, dot3(feats, w_recv))
        return carry

    lax.fori_loop(0, NEAR // WIDE, project, 0)
    w_edge = split(w_ref[:FEAT, :])

    def near_step(at, carry):
        rows = block_at(at, WIDE)
        total = dot3(split(edge_ref[rows, :]), w_edge)
        total += dot2(hot_rows(recv_rep[rows, :], 0, NEAR), (q0[...], q1[...]))
        total += dot2(hot_rows(rep[rows, :], 0, NEAR), (p0[...], p1[...]))
        pre_ref[rows, :] = total
        return carry

    lax.fori_loop(0, EDGE // WIDE, near_step, 0)

    shuffle.wait_chips(outgoing, got)
    swap = shuffle.core_copy(got.at[:, 1 - shuffle.core], from_mate)
    swap.start()
    half = CHIPS * 8
    put_pair((h0, h1), pl.ds(0, half), got[:, shuffle.core].reshape(half, FEAT))
    w_out = split(w_out_ref[...])

    def halo_step(at, carry):
        rows = block_at(at, WIDE)
        pre_ref[rows, :] += dot2(hot_rows(rep[rows, :], NEAR, half), pair_at((h0, h1), pl.ds(0, half)))
        return carry

    lax.fori_loop(0, EDGE // WIDE, halo_step, 0)
    swap.wait()
    put_pair((h0, h1), pl.ds(half, half), from_mate[...].reshape(half, FEAT))

    def edge_step(at, carry):
        rows = block_at(at, WIDE)
        pre = pre_ref[rows, :] + dot2(hot_rows(rep[rows, :], NEAR + half, half), pair_at((h0, h1), pl.ds(half, half)))
        pre_ref[rows, :] = pre
        normed, scale = norm(dot3(split(pre * sigmoid(pre)), w_out))
        normed_ref[rows, :] = normed
        scale_ref[rows, :] = jnp.broadcast_to(scale, (WIDE, 128))
        put_pair((n0, n1), rows, edge_ref[rows, :] + normed)
        return carry

    lax.fori_loop(0, EDGE // WIDE, edge_step, 0)

    def gather(at, carry):
        rows = block_at(at, WIDE)
        agg_ref[rows, :] = dot2(hot_columns(recv_ref[...], at * WIDE, WIDE), (n0[...], n1[...]))
        return carry

    lax.fori_loop(0, NEAR // WIDE, gather, 0)


def back_kernel(*refs):
    grad_agg_ref, cot_ref, pre_ref, normed_ref, scale_ref, w_out_ref, send_ref, recv_ref = refs[:8]
    edge_ref, near_ref, w_ref, list_ref, direct_ref = refs[8:13]
    grad_edges_ref, grad_fine_ref, in_edge_ref, out_ref, in_recv_ref, coarse_ref, in_send_ref = refs[13:20]
    t0, t1, d0, d1, a0, a1, recv_rep, for_mate, pack, back = refs[20:30]
    edge_total, tail_total, recv_total, send_total = refs[30:34]
    shuffle = Shuffle(*refs[34:])
    shuffle.signal()
    recv_rep[...] = spread(recv_ref[...])
    a0[...], a1[...] = split(grad_agg_ref[...])
    w_out = split(w_out_ref[...])

    def step(at, carry):
        rows = block_at(at, WIDE)
        grad = cot_ref[rows, :] + dot2(hot_rows(recv_rep[rows, :], 0, NEAR), (a0[...], a1[...]))
        grad_edges_ref[rows, :] = grad
        tail = split(norm_back(grad, normed_ref[rows, :], scale_ref[rows, :1]))
        t0[rows, :], t1[rows, :] = tail
        pre = pre_ref[rows, :]
        gate = sigmoid(pre)
        put_pair((d0, d1), rows, dot3(tail, w_out, NT) * (gate * (1.0 + pre * (1.0 - gate))))
        return carry

    lax.fori_loop(0, EDGE // WIDE, step, 0)

    half = CHIPS * 8

    def halo_rows(first):
        rows = dot2(hot_columns(send_ref[...], NEAR + first, half), (d0[...], d1[...]))
        return rows.reshape(CHIPS, 8, FEAT)

    for_mate[...] = halo_rows(half)
    shuffle.wait_signals()
    swap = shuffle.core_copy(for_mate, pack.at[:, 1])
    swap.start()
    pack[:, 0] = halo_rows(0)
    swap.wait()
    shuffle.send_chips(pack, back)

    edge_total[...] = jnp.zeros_like(edge_total)
    tail_total[...] = jnp.zeros_like(tail_total)
    w_edge = split(w_ref[:FEAT, :])

    def weight_step(at, carry):
        rows = block_at(at)
        grad_pre = (d0[rows, :], d1[rows, :])
        grad_edges_ref[rows, :] += dot3(grad_pre, w_edge, NT)
        edge_total[...] += dot3(split(edge_ref[rows, :]), grad_pre, TN)
        pre = pre_ref[rows, :]
        tail_total[...] += dot3(split(pre * sigmoid(pre)), (t0[rows, :], t1[rows, :]), TN)
        return carry

    lax.fori_loop(0, EDGE // BLOCK, weight_step, 0)
    put_tiles(in_edge_ref, edge_total)
    put_tiles(out_ref, tail_total)
    w_send = split(w_ref[FEAT : 2 * FEAT, :])
    w_recv = split(w_ref[2 * FEAT :, :])

    def sums(at):
        grad_pre = (d0[...], d1[...])
        sent = dot2(hot_columns(send_ref[...], at * BLOCK, BLOCK), grad_pre)
        return sent, split(dot2(hot_columns(recv_ref[...], at * BLOCK, BLOCK), grad_pre))

    fine_sent, received = sums(0)
    grad_fine_ref[...] = direct_ref[...] + dot3(received, w_recv, NT)
    recv_total[...] = dot3(split(near_ref[:FINE, :]), received, TN)
    send_total[...] = jnp.zeros_like(send_total)

    def coarse_step(at, carry):
        rows = block_at(at)
        sent, received = sums(at)
        sent = split(sent)
        value = dot3(sent, w_send, NT) + dot3(received, w_recv, NT)
        put_tiles(coarse_ref.at[pl.ds((at - 1) * (BLOCK // 8), BLOCK // 8)], value)
        feats = split(near_ref[rows, :])
        recv_total[...] += dot3(feats, received, TN)
        send_total[...] += dot3(feats, sent, TN)
        return carry

    lax.fori_loop(1, NEAR // BLOCK, coarse_step, 0)
    put_tiles(in_recv_ref, recv_total)

    shuffle.wait_chips(pack, back)
    returned = split(back[...].reshape(EDGE, FEAT))
    fine_sent = split(fine_sent + dot2(hot_columns(list_ref[...], 0, FINE), returned))
    grad_fine_ref[...] += dot3(fine_sent, w_send, NT)
    send_total[...] += dot3(split(near_ref[:FINE, :]), fine_sent, TN)
    put_tiles(in_send_ref, send_total)


OUT_ROW, EDGE_ROW, RECV_ROW, COARSE_ROW, SEND_ROW, ROWS = 192, 256, 320, 384, 480, 576


def sum_kernel(*refs):
    node_ref, out_ref, in_edge_ref, in_recv_ref, coarse_ref, in_send_ref, direct_ref = refs[:7]
    sum_ref, buf, got, sends, recvs = refs[7:]
    flat = buf.reshape(ROWS * 4, 8, 128)
    ring = Exchange(ALL_PARTS, buf, got, sum_ref, sends, recvs)
    ring.greet()
    started = 0
    row = 0
    for ref in (node_ref, out_ref, in_edge_ref, in_recv_ref, coarse_ref, in_send_ref):
        size = ref.shape[0]
        flat[row * 4 : (row + size) * 4] = ref[...].reshape(size * 4, 8, 128)
        if row == COARSE_ROW:
            flat[pl.ds(row * 4 + ring.me % 96 * 4, 4)] += direct_ref[...]
        row += size
        if row == SEND_ROW + 64:
            flat[row * 4 :] = jnp.zeros(((ROWS - row) * 4, 8, 128), F32)
            row = ROWS
        while started < LINKS and (started + 1) * (ROWS // LINKS) <= row:
            ring.start(started)
            started += 1
    for part in range(LINKS):
        ring.start_kept(part)
    ring.run(ring.SUM)


def finish_kernel(pieces, sum_ref, coarse_ref, in_ref, out_ref, node_in_ref, node_out_ref, *rest):
    rows, stores = rest[:-1], rest[-1]
    outs = (coarse_ref, in_ref, out_ref, node_in_ref, node_out_ref)
    tiles = sum_ref.reshape(ROWS, 4, 8, 128)
    puts = []
    for at, (first, count, which, to, scale) in enumerate(pieces):
        for column in range(FEAT // 128):
            lanes = slice(column * 128, (column + 1) * 128)
            whole = min(count, (outs[which].shape[0] - to) // 8)
            value = tiles[first : first + whole, column] * scale
            rows[which][to : to + whole * 8, lanes] = value.reshape(whole * 8, 128)
            if whole < count:
                rows[which][to + whole * 8 :, lanes] = tiles[first + whole, column][: COARSE - whole * 8] * scale
        src, dst = rows[which], outs[which]
        if count * 8 < src.shape[0]:
            src, dst = src.at[pl.ds(to, count * 8)], dst.at[pl.ds(to, count * 8)]
        puts.append(pltpu.make_async_copy(src, dst, stores.at[at]))
        puts[-1].start()
    for put in puts:
        put.wait()


def finish(summed, edge_scale, node_scale):
    pieces = [
        (0, 64, 3, 0, node_scale),
        (64, 64, 3, FEAT, node_scale),
        (128, 64, 4, 0, node_scale),
        (OUT_ROW, 64, 2, 0, edge_scale),
        (EDGE_ROW, 64, 1, 0, edge_scale),
        (RECV_ROW, 64, 1, 2 * FEAT, edge_scale),
        (COARSE_ROW, 81, 0, 0, 1.0),
        (SEND_ROW, 64, 1, FEAT, edge_scale),
    ]
    any_spec = pl.BlockSpec(memory_space=pl.ANY)
    sizes = (COARSE, 3 * FEAT, FEAT, 2 * FEAT, FEAT)
    sem = pltpu.SemaphoreType.DMA((len(pieces),))
    return pl.pallas_call(
        functools.partial(finish_kernel, pieces),
        out_shape=[f32_out(size, FEAT) for size in sizes],
        in_specs=vmem_specs(1),
        out_specs=[any_spec] * 5,
        scratch_shapes=[pltpu.VMEM((size, FEAT), F32) for size in sizes] + [sem],
        compiler_params=pltpu.CompilerParams(vmem_limit_bytes=24 << 20),
    )(summed)


def per_device(
    fine_nodes,
    coarse_nodes,
    edge_feats,
    senders,
    receivers,
    send_rows,
    w_edge_in,
    w_edge_out,
    w_node_in,
    w_node_out,
    cot_fine,
    cot_coarse,
    cot_edges,
):
    me = lax.axis_index("patch")
    peers = lax.axis_size("patch")
    core = me % 2
    near_count = FINE + COARSE
    send_list = send_rows.reshape(CHIPS, 2, 8)
    back_list = jnp.where(core == 1, send_list[:, ::-1], send_list).reshape(1, EDGE)
    send_list = send_list.reshape(1, EDGE)
    halo = senders - near_count
    source = halo // 8
    halo_at = NEAR + (source % 2 != core) * (EDGE // 2) + source // 2 * 8 + halo % 8
    send_at = jnp.where(senders < near_count, senders, halo_at).astype(jnp.int32).reshape(1, EDGE)
    recv_at = receivers.reshape(1, EDGE)
    half = pltpu.VMEM((EDGE, FEAT), BF16)
    index = pltpu.VMEM((EDGE, 128), jnp.int32)
    square = pltpu.VMEM((FEAT, FEAT), F32)
    chip_rows = pltpu.VMEM((CHIPS, 2, 8, FEAT), F32)
    core_rows = pltpu.VMEM((CHIPS, 8, FEAT), F32)
    sems = [pltpu.SemaphoreType.DMA] * 4
    wide = f32_out(EDGE, FEAT)
    fine_out = f32_out(FINE, FEAT)

    near = jnp.concatenate([fine_nodes, coarse_nodes, jnp.zeros((NEAR - near_count, FEAT), F32)], axis=0)
    pre, normed, scale, agg = remote_call(
        front_kernel,
        1,
        [wide, wide, f32_out(EDGE, 128), wide],
        [chip_rows, chip_rows, core_rows] + [half] * 8 + [index] * 2 + sems,
        FRONT_MIB,
        fine_nodes,
        near,
        edge_feats,
        w_edge_in,
        w_edge_out,
        send_list,
        send_at,
        recv_at,
    )
    blank = jnp.zeros((8 * peers - COARSE, FEAT), F32)
    few = lax.dynamic_slice(jnp.concatenate([coarse_nodes, blank], axis=0), (me * 8, 0), (8, FEAT))
    few_cot = lax.dynamic_slice(jnp.concatenate([cot_coarse, blank], axis=0), (me * 8, 0), (8, FEAT))
    grad_agg, direct, few_direct, node = node_step(agg, fine_nodes, cot_fine, few, few_cot, w_node_in, w_node_out)
    grad_edges, grad_fine, in_edge, edge_out, in_recv, coarse, in_send = remote_call(
        back_kernel,
        3,
        [wide, fine_out, TILES, TILES, TILES, f32_out(96, 4, 8, 128), TILES],
        [half] * 6 + [index, core_rows, chip_rows, chip_rows] + [square] * 4 + sems,
        BACK_MIB,
        grad_agg,
        cot_edges,
        pre,
        normed,
        scale,
        w_edge_out,
        send_at,
        recv_at,
        edge_feats,
        near,
        w_edge_in,
        back_list,
        direct,
    )
    (summed,) = remote_call(
        sum_kernel, 4, [sum_out(3)], exchange_scratch(LINKS, 3), SUM_MIB, node, edge_out, in_edge, in_recv, coarse, in_send, few_direct
    )
    edge_scale = 1.0 / math.sqrt(EDGE * peers)
    node_scale = 1.0 / math.sqrt(FINE * peers + COARSE)
    grad_coarse, grad_in, grad_out, grad_node_in, grad_node_out = finish(summed, edge_scale, node_scale)
    return grad_fine, grad_coarse, grad_edges, grad_in, grad_out, grad_node_in, grad_node_out


def solution(mesh):
    return jax.shard_map(
        per_device,
        mesh=mesh,
        in_specs=(
            P("patch", None),
            P(),
            P("patch", None),
            P("patch"),
            P("patch"),
            P("patch", None, None),
            P(),
            P(),
            P(),
            P(),
            P("patch", None),
            P(),
            P("patch", None),
        ),
        out_specs=(P("patch", None), P(), P("patch", None), P(), P(), P(), P()),
        check_vma=False,
    )
```

```python
import functools
import math

import jax
import jax.numpy as jnp
from jax import lax
from jax.experimental import pallas as pl
from jax.experimental.pallas import tpu as pltpu
from jax.sharding import PartitionSpec as P

MESH = pl.DeviceIdType.MESH
F32 = jnp.float32
BF16 = jnp.bfloat16
FEAT = 512
FINE = 256
COARSE = 642
NEAR = 1024
EDGE = 1024
BLOCK = 256
LINKS = 6
WIDE = 512
FRONT_MIB, BACK_MIB, SUM_MIB = 42, 42, 30

NN = (((1,), (0,)), ((), ()))
NT = (((1,), (1,)), ((), ()))
TN = (((0,), (0,)), ((), ()))


def split(value):
    high = value.astype(BF16)
    return high, (value - high.astype(F32)).astype(BF16)


def dot(left, right, dims=NN):
    return lax.dot_general(left, right, dims, preferred_element_type=F32)


def dot3(left, right, dims=NN):
    return dot(left[0], right[0], dims) + dot(left[0], right[1], dims) + dot(left[1], right[0], dims)


def dot2(left, right, dims=NN):
    return dot(left, right[0], dims) + dot(left, right[1], dims)


def block_at(step, size=BLOCK):
    return pl.ds(pl.multiple_of(step * size, size), size)


def pair_at(refs, rows):
    return refs[0][rows, :], refs[1][rows, :]


def put_pair(refs, rows, value):
    high, low = split(value)
    refs[0][rows, :] = high
    refs[1][rows, :] = low


def spread(index_row):
    return jnp.transpose(jnp.broadcast_to(index_row, (128, index_row.shape[1])))


def hot_rows(spread_block, first, width):
    lane = lax.broadcasted_iota(jnp.int32, (spread_block.shape[0], 128), 1)
    local = spread_block - first
    tiles = [jnp.where(local == lane + at, 1.0, 0.0).astype(BF16) for at in range(0, width, 128)]
    return jnp.concatenate(tiles, axis=1)


def hot_columns(index_row, first, height):
    row = lax.broadcasted_iota(jnp.int32, (height, index_row.shape[1]), 0) + first
    return jnp.where(row == index_row, 1.0, 0.0).astype(BF16)


def sigmoid(value):
    return 1.0 / (1.0 + jnp.exp(-value))


def mean(value):
    return jnp.sum(value, axis=1, keepdims=True) * (1.0 / FEAT)


def norm(value):
    center = value - mean(value)
    scale = lax.rsqrt(mean(center * center) + 1e-05)
    return center * scale, scale


def norm_back(grad, normed, scale):
    return scale * (grad - mean(grad) - normed * mean(grad * normed))


def put_tiles(ref, value):
    for at in range(FEAT // 128):
        ref[:, at] = value[:, at * 128 : (at + 1) * 128].reshape(-1, 8, 128)


def vmem_specs(count):
    return [pl.BlockSpec(memory_space=pltpu.VMEM)] * count


def f32_out(*shape):
    return jax.ShapeDtypeStruct(shape, F32)


def bf16_out(*shape):
    return jax.ShapeDtypeStruct(shape, BF16)


TILES = f32_out(64, 4, 8, 128)


STRIDES = (32, 8, 2)
ALL_PARTS = tuple((part % 3, part // 3) for part in range(6))
FOUR_PARTS = ALL_PARTS[:4]
GOT_CHUNKS = 127
SEM_COUNT = 24


def axis_places(device):
    return [(device // 32) % 4, (device // 8) % 4, (device // 2) % 4], device % 2


def axis_bits(place):
    return ((place + 1) // 2) % 2, place // 2


def position(device, spec):
    places, core = axis_places(device)
    first, flip = spec
    bits = axis_bits(places[first])
    spot = (core * 2 + bits[flip]) * 2 + bits[1 - flip]
    return (spot * 4 + places[(first + 1) % 3]) * 4 + places[(first + 2) % 3]


class Exchange:
    def __init__(self, specs, buf, got, out, sends, recvs):
        self.specs, self.buf, self.got, self.out, self.sends, self.recvs = specs, buf, got, out, sends, recvs
        self.me = lax.axis_index("patch")
        self.places, self.core = axis_places(self.me)
        self.mate = self.me + 1 - 2 * self.core
        self.bits = [axis_bits(place) for place in self.places]
        self.flying = {}
        self.spot = {}
        for part, (first, flip) in enumerate(specs):
            one, two = self.bits[first][flip], self.bits[first][1 - flip]
            third, fourth = self.places[(first + 1) % 3], self.places[(first + 2) % 3]
            at_core = self.core * 64
            at_one = at_core + one * 32
            at_two = at_one + two * 16
            at_three = at_two + third * 4
            self.spot[part] = dict(
                one=one, two=two, core=at_core, first=at_one, second=at_two, third=at_three, last=at_three + fourth
            )

    def signal(self):
        mates = [self.mate]
        mates += [self.peer(axis, shift) for axis in range(3) for shift in (1, 2, 3)]
        barrier = pltpu.get_barrier_semaphore()
        for mate in mates:
            pl.semaphore_signal(barrier, inc=1, device_id=(mate,), device_id_type=MESH)

    def wait_signals(self):
        pl.semaphore_wait(pltpu.get_barrier_semaphore(), 10)

    def peer(self, axis, shift):
        return self.me + ((self.places[axis] + shift) % 4 - self.places[axis]) * STRIDES[axis]

    def neighbour(self, axis, flip):
        place = self.places[axis]
        step = 3 - 2 * place if flip else 1 - 2 * (place % 2)
        return self.me + step * STRIDES[axis]

    def push(self, part, sem, src, dst, device):
        copy = pltpu.make_async_remote_copy(
            src_ref=src,
            dst_ref=dst,
            send_sem=self.sends.at[sem, part],
            recv_sem=self.recvs.at[sem, part],
            device_id=(device,),
            device_id_type=MESH,
        )
        copy.start()
        self.flying[part, sem] = copy

    def wait(self, part, *sems):
        for sem in sems:
            self.flying.pop((part, sem)).wait()

    def send_sum(self, part, sem, at, size, slot, device):
        self.push(part, sem, self.buf.at[part, pl.ds(at, size)], self.got.at[part, pl.ds(slot, size)], device)

    def add(self, part, at, size, *slots):
        total = self.buf[part, pl.ds(at, size)]
        for slot in slots:
            total += self.got[part, pl.ds(slot, size)]
        self.buf[part, pl.ds(at, size)] = total

    def send_block(self, part, sem, at, size, device):
        block = self.out.at[part, pl.ds(at, size)]
        self.push(part, sem, block, block, device)


    def start(self, part):
        spot = self.spot[part]
        other = 64 - spot["core"]
        self.send_sum(part, 0, other + (1 - spot["one"]) * 32, 32, 0, self.mate)

    def start_kept(self, part):
        spot = self.spot[part]
        other = 64 - spot["core"]
        self.send_sum(part, 1, other + spot["one"] * 32, 32, 32, self.mate)

    def reduce_first(self, part):
        spot = self.spot[part]
        first, flip = self.specs[part]
        away = spot["core"] + (1 - spot["one"]) * 32
        device = self.neighbour(first, flip)
        self.wait(part, 0)
        self.add(part, away, 32, 0)
        self.send_sum(part, 2, away + (1 - spot["two"]) * 16, 16, 64, device)
        self.send_sum(part, 3, away + spot["two"] * 16, 16, 80, device)

    def reduce_kept(self, part):
        self.wait(part, 1)
        self.add(part, self.spot[part]["first"], 32, 32)

    def reduce_second(self, part):
        spot = self.spot[part]
        first, flip = self.specs[part]
        away = spot["first"] + (1 - spot["two"]) * 16
        self.wait(part, 2)
        self.add(part, away, 16, 64)
        self.send_sum(part, 4, away, 16, 96, self.neighbour(first, 1 - flip))

    def reduce_third(self, part):
        spot = self.spot[part]
        axis = (self.specs[part][0] + 1) % 3
        self.wait(part, 3, 4)
        self.add(part, spot["second"], 16, 80, 96)
        for shift in (1, 2, 3):
            at = spot["second"] + (self.places[axis] + shift) % 4 * 4
            self.send_sum(part, 4 + shift, at, 4, 108 + 4 * shift, self.peer(axis, shift))

    def reduce_fourth(self, part):
        spot = self.spot[part]
        axis = (self.specs[part][0] + 2) % 3
        self.wait(part, 5, 6, 7)
        self.add(part, spot["third"], 4, 112, 116, 120)
        for shift in (1, 2, 3):
            at = spot["third"] + (self.places[axis] + shift) % 4
            self.send_sum(part, 7 + shift, at, 1, 123 + shift, self.peer(axis, shift))

    def reduce_last(self, part):
        self.wait(part, 8, 9, 10)
        self.add(part, self.spot[part]["last"], 1, 124, 125, 126)

    def gather_fourth(self, part):
        axis = (self.specs[part][0] + 2) % 3
        for shift in (1, 2, 3):
            self.send_block(part, 10 + shift, self.spot[part]["last"], 1, self.peer(axis, shift))

    def gather_third(self, part):
        axis = (self.specs[part][0] + 1) % 3
        self.wait(part, 11, 12, 13)
        for shift in (1, 2, 3):
            self.send_block(part, 13 + shift, self.spot[part]["third"], 4, self.peer(axis, shift))

    def gather_second(self, part):
        spot = self.spot[part]
        first, flip = self.specs[part]
        self.wait(part, 14, 15, 16)
        self.send_block(part, 17, spot["second"], 16, self.neighbour(first, 1 - flip))
        self.send_block(part, 20, spot["second"], 16, self.mate)

    def gather_first(self, part):
        spot = self.spot[part]
        first, flip = self.specs[part]
        device = self.neighbour(first, flip)
        self.wait(part, 17)
        self.send_block(part, 18, spot["first"], 16, device)
        self.send_block(part, 19, spot["first"] + 16, 16, device)
        self.send_block(part, 21, spot["first"] + (1 - spot["two"]) * 16, 16, self.mate)

    def gather_core(self, part):
        spot = self.spot[part]
        self.wait(part, 18)
        self.send_block(part, 22, spot["core"] + (1 - spot["one"]) * 32, 16, self.mate)

    def gather_rest(self, part):
        spot = self.spot[part]
        self.wait(part, 19)
        self.send_block(part, 23, spot["core"] + (1 - spot["one"]) * 32 + 16, 16, self.mate)

    def gather_last(self, part):
        self.wait(part, 20, 21, 22, 23)

    REDUCE = ("reduce_first", "reduce_kept", "reduce_second", "reduce_third", "reduce_fourth", "reduce_last")
    GATHER = ("gather_fourth", "gather_third", "gather_second", "gather_first", "gather_core", "gather_rest", "gather_last")

    def stage(self, stage, *parts):
        for part in parts:
            getattr(self, stage)(part)

    def run(self, stages, beside=()):
        beside = list(beside)
        for stage in stages:
            if beside:
                beside.pop(0)()
            self.stage(stage, *range(len(self.specs)))
        for work in beside:
            work()

    def finish_sum(self, part):
        self.reduce_last(part)
        last = pl.ds(self.spot[part]["last"], 1)
        self.out[part, last] = self.buf[part, last]
        self.gather_fourth(part)

    SUM = REDUCE[:-1] + ("finish_sum",) + GATHER[1:]


def exchange_scratch(parts, units):
    sem = pltpu.SemaphoreType.DMA((SEM_COUNT, parts))
    return [
        pltpu.VMEM((parts, 128, units, 8, 128), F32),
        pltpu.VMEM((parts, GOT_CHUNKS, units, 8, 128), F32),
        sem,
        sem,
    ]


def sum_out(units):
    return f32_out(LINKS, 128, units, 8, 128)


def remote_call(kernel, name_id, outs, scratch, limit, *args):
    return pl.pallas_call(
        kernel,
        out_shape=outs,
        in_specs=vmem_specs(len(args)),
        out_specs=vmem_specs(len(outs)),
        scratch_shapes=scratch,
        compiler_params=pltpu.CompilerParams(collective_id=name_id, has_side_effects=True, vmem_limit_bytes=limit << 20),
        cost_estimate=pl.CostEstimate(flops=int(3e10), bytes_accessed=int(3e7), transcendentals=0),
    )(*args)


def few_dot3(left, right, dims=NN):
    count = left[0].shape[0]
    both = dot(jnp.concatenate(left, axis=0), right[0], dims)
    return both[:count] + both[count:] + dot(left[0], right[1], dims)


class NodePass:
    def __init__(self, product, w_in, w_out):
        self.product, self.w_in, self.w_out = product, w_in, w_out

    def first(self, feats, agg):
        self.feats, self.agg = split(feats), split(agg)
        pre = self.product(self.feats, pair_at(self.w_in, pl.ds(0, FEAT)))
        self.pre = pre + self.product(self.agg, pair_at(self.w_in, pl.ds(FEAT, FEAT)))
        self.gate = sigmoid(self.pre)
        self.hidden = split(self.pre * self.gate)

    def second(self):
        self.normed, self.scale = norm(self.product(self.hidden, pair_at(self.w_out, pl.ds(0, FEAT))))

    def third(self, cot):
        self.tail = split(norm_back(cot, self.normed, self.scale))
        grad = self.product(self.tail, pair_at(self.w_out, pl.ds(0, FEAT)), NT)
        self.grad = split(grad * (self.gate * (1.0 + self.pre * (1.0 - self.gate))))

    def back(self, first):
        return self.product(self.grad, pair_at(self.w_in, pl.ds(first, FEAT)), NT)


def few_rows(ref, me):
    whole = COARSE // 8
    rows = ref[pl.ds(pl.multiple_of(me % whole * 8, 8), 8), :]
    rest = jnp.concatenate([ref[whole * 8 :, :], jnp.zeros((8 - COARSE % 8, FEAT), F32)], axis=0)
    return jnp.where(me < whole, rows, jnp.where(me == whole, rest, 0.0))


def node_kernel(*refs):
    agg_ref, fine_ref, cot_ref, coarse_ref, coarse_cot_ref, w_in_ref, w_out_ref = refs[:7]
    grad_agg_ref, own_ref, direct_ref, node_ref = refs[7:11]
    buf, got, sends, recvs, full, wi0, wi1, wo0, wo1, total = refs[11:]
    ring = Exchange(FOUR_PARTS, buf, got, full, sends, recvs)
    ring.signal()
    for part, spec in enumerate(FOUR_PARTS):
        for device in range(128):
            first = FINE + 8 * device
            if first < NEAR and 8 * device < COARSE:
                buf[part, position(device, spec), 0] = agg_ref[first : first + 8, part * 128 : (part + 1) * 128]
            else:
                buf[part, position(device, spec), 0] = jnp.zeros((8, 128), F32)
    ring.wait_signals()
    ring.stage("start", *range(4))
    ring.stage("start_kept", *range(4))

    wi, wo = (wi0, wi1), (wo0, wo1)
    fine = NodePass(dot3, wi, wo)
    few = NodePass(few_dot3, wi, wo)
    few_feats, few_cot = few_rows(coarse_ref, ring.me), few_rows(coarse_cot_ref, ring.me)

    def cut_weights():
        wi0[...], wi1[...] = split(w_in_ref[...])
        wo0[...], wo1[...] = split(w_out_ref[...])

    def fine_first():
        fine.first(fine_ref[...], agg_ref[:FINE, :])

    def fine_third():
        fine.third(cot_ref[...])

    def fine_back():
        own_ref[...] = cot_ref[...] + fine.back(0)

    def fine_agg():
        grad_agg_ref[:FINE, :] = fine.back(FEAT)

    ring.run(ring.REDUCE, [cut_weights, fine_first, fine.second, fine_third, fine_back, fine_agg])

    few_agg = jnp.concatenate([buf[part, ring.spot[part]["last"], 0] for part in range(4)], axis=1)
    blank = jnp.zeros((8, FEAT), F32)
    few.first(jnp.concatenate([few_feats, blank], axis=0), jnp.concatenate([few_agg, blank], axis=0))
    few.second()
    few.third(jnp.concatenate([few_cot, blank], axis=0))
    few_grad = few.back(FEAT)[:8]
    for part in range(4):
        full[part, ring.spot[part]["last"], 0] = few_grad[:, part * 128 : (part + 1) * 128]

    def few_back():
        direct = few_cot + few.back(0)[:8]
        for at in range(4):
            direct_ref[at] = direct[:, at * 128 : (at + 1) * 128]

    def weights_back(which, grad, first):
        def run():
            total[...] = dot3(getattr(fine, which), getattr(fine, grad), TN) + dot3(getattr(few, which), getattr(few, grad), TN)
            put_tiles(node_ref.at[pl.ds(first, 64)], total)

        return run

    def nothing():
        pass

    beside = [nothing, few_back]
    beside += [weights_back("feats", "grad", 0), weights_back("agg", "grad", 64), weights_back("hidden", "tail", 128)]
    ring.run(ring.GATHER, beside)
    for part, spec in enumerate(FOUR_PARTS):
        for device in range((NEAR - FINE) // 8):
            first = FINE + 8 * device
            grad_agg_ref[first : first + 8, part * 128 : (part + 1) * 128] = full[part, position(device, spec), 0]


def node_step(agg, fine, cot_fine, coarse, cot_coarse, w_in, w_out):
    half = pltpu.VMEM((2 * FEAT, FEAT), BF16)
    quarter = pltpu.VMEM((FEAT, FEAT), BF16)
    return remote_call(
        node_kernel,
        2,
        [f32_out(NEAR, FEAT), f32_out(FINE, FEAT), f32_out(4, 8, 128), f32_out(192, 4, 8, 128)],
        exchange_scratch(4, 1)
        + [pltpu.VMEM((4, 128, 1, 8, 128), F32), half, half, quarter, quarter, pltpu.VMEM((FEAT, FEAT), F32)],
        34,
        agg,
        fine,
        cot_fine,
        coarse,
        cot_coarse,
        w_in,
        w_out,
    )


CHIPS = 64


class Shuffle:
    def __init__(self, sends, recvs, core_sends, core_recvs):
        self.sends, self.recvs, self.core_sends, self.core_recvs = sends, recvs, core_sends, core_recvs
        self.me = lax.axis_index("patch")
        self.places, self.core = axis_places(self.me)
        self.chip = self.me // 2
        self.mate = self.me + 1 - 2 * self.core

    def other(self, step):
        z, x, y = ((place + step // span) % 4 for place, span in zip(self.places, (16, 4, 1)))
        return z * 16 + x * 4 + y

    def each(self, run):
        def body(step, carry):
            run(self.other(step))
            return carry

        lax.fori_loop(1, CHIPS, body, 0)

    def signal(self):
        barrier = pltpu.get_barrier_semaphore()

        def run(chip):
            pl.semaphore_signal(barrier, inc=1, device_id=(chip * 2 + self.core,), device_id_type=MESH)

        self.each(run)
        pl.semaphore_signal(barrier, inc=1, device_id=(self.mate,), device_id_type=MESH)

    def wait_signals(self):
        pl.semaphore_wait(pltpu.get_barrier_semaphore(), CHIPS)

    def copy(self, src, dst, sends, recvs, device):
        return pltpu.make_async_remote_copy(
            src_ref=src, dst_ref=dst, send_sem=sends, recv_sem=recvs, device_id=(device,), device_id_type=MESH
        )

    def send_chips(self, src, dst):
        def run(chip):
            self.copy(src.at[chip], dst.at[self.chip], self.sends, self.recvs, chip * 2 + self.core).start()

        self.each(run)
        dst[self.chip] = src[self.chip]

    def wait_chips(self, src, dst):
        most = pl.ds(0, CHIPS - 1)
        self.copy(src.at[most], dst.at[most], self.sends, self.recvs, self.mate).wait()

    def core_copy(self, src, dst):
        return self.copy(src, dst, self.core_sends, self.core_recvs, self.mate)


def halo_place(senders, core):
    halo = senders - (FINE + COARSE)
    source = jnp.right_shift(halo, 3)
    kind = jnp.bitwise_and(source + core, 1)
    place = NEAR + kind * (EDGE // 2) + jnp.right_shift(source, 1) * 8 + jnp.bitwise_and(halo, 7)
    return jnp.where(halo < 0, senders, place)


def front_kernel(*refs):
    list_ref, sender_ref, recv_ref = refs[:3]
    far_in, agg_ref, far_out = refs[3:8], refs[8], refs[9:13]
    outgoing, got, from_mate, p0, p1, q0, q1, h0, h1, n0, n1, rep, recv_rep = refs[13:26]
    near_ref, coarse_ref, w_ref, edge_ref, w_out_ref, pre_ref, normed_ref, scale_ref, send_ref, loads, stores = refs[26:37]
    shuffle = Shuffle(*refs[37:])
    places = (near_ref.at[pl.ds(0, FINE)], w_ref, coarse_ref, edge_ref, w_out_ref)
    fetch = [pltpu.make_async_copy(src, dst, loads.at[at]) for at, (src, dst) in enumerate(zip(far_in, places))]
    for copy in fetch:
        copy.start()
    results = (pre_ref, normed_ref, scale_ref, near_ref)
    keep = [pltpu.make_async_copy(src, dst, stores.at[at]) for at, (src, dst) in enumerate(zip(results, far_out))]
    shuffle.signal()
    rep[...] = spread(list_ref[...])
    send_ref[...] = halo_place(sender_ref[...], shuffle.core)
    for copy in fetch[:2]:
        copy.wait()
    w_send = split(w_ref[FEAT : 2 * FEAT, :])
    own = split(dot3(split(near_ref[:FINE, :]), w_send))

    def request(at, carry):
        rows = block_at(at, WIDE)
        chips = pl.ds(at * (WIDE // 16), WIDE // 16)
        outgoing[chips] = dot2(hot_rows(rep[rows, :], 0, FINE), own).reshape(WIDE // 16, 2, 8, FEAT)
        return carry

    lax.fori_loop(0, EDGE // WIDE, request, 0)
    shuffle.wait_signals()
    shuffle.send_chips(outgoing, got)

    rep[...] = spread(send_ref[...])
    recv_rep[...] = spread(recv_ref[...])
    w_recv = split(w_ref[2 * FEAT :, :])
    whole = COARSE // 8 * 8
    for copy in fetch[2:]:
        copy.wait()
    near_ref[FINE : FINE + whole, :] = coarse_ref[:whole, :]
    near_ref[FINE + whole :, :] = jnp.zeros((NEAR - FINE - whole, FEAT), F32)
    near_ref[FINE + whole : FINE + COARSE, :] = coarse_ref[whole:, :]
    keep[3].start()

    def project(at, carry):
        rows = block_at(at, WIDE)
        feats = split(near_ref[rows, :])
        put_pair((p0, p1), rows, dot3(feats, w_send))
        put_pair((q0, q1), rows, dot3(feats, w_recv))
        return carry

    lax.fori_loop(0, NEAR // WIDE, project, 0)
    w_edge = split(w_ref[:FEAT, :])

    def near_step(at, carry):
        rows = block_at(at, WIDE)
        total = dot3(split(edge_ref[rows, :]), w_edge)
        total += dot2(hot_rows(recv_rep[rows, :], 0, NEAR), (q0[...], q1[...]))
        total += dot2(hot_rows(rep[rows, :], 0, NEAR), (p0[...], p1[...]))
        pre_ref[rows, :] = total
        return carry

    lax.fori_loop(0, EDGE // WIDE, near_step, 0)

    shuffle.wait_chips(outgoing, got)
    swap = shuffle.core_copy(got.at[:, 1 - shuffle.core], from_mate)
    swap.start()
    half = CHIPS * 8
    put_pair((h0, h1), pl.ds(0, half), got[:, shuffle.core].reshape(half, FEAT))
    w_out = split(w_out_ref[...])

    def halo_step(at, carry):
        rows = block_at(at, WIDE)
        pre_ref[rows, :] += dot2(hot_rows(rep[rows, :], NEAR, half), pair_at((h0, h1), pl.ds(0, half)))
        return carry

    lax.fori_loop(0, EDGE // WIDE, halo_step, 0)
    swap.wait()
    put_pair((h0, h1), pl.ds(half, half), from_mate[...].reshape(half, FEAT))

    def edge_step(at, carry):
        rows = block_at(at, WIDE)
        pre = pre_ref[rows, :] + dot2(hot_rows(rep[rows, :], NEAR + half, half), pair_at((h0, h1), pl.ds(half, half)))
        pre_ref[rows, :] = pre
        normed, scale = norm(dot3(split(pre * sigmoid(pre)), w_out))
        normed_ref[rows, :] = normed
        scale_ref[rows, :] = jnp.broadcast_to(scale, (WIDE, 128))
        put_pair((n0, n1), rows, edge_ref[rows, :] + normed)
        return carry

    lax.fori_loop(0, EDGE // WIDE, edge_step, 0)
    for copy in keep[:3]:
        copy.start()

    def gather(at, carry):
        rows = block_at(at, WIDE)
        agg_ref[rows, :] = dot2(hot_columns(recv_ref[...], at * WIDE, WIDE), (n0[...], n1[...]))
        return carry

    lax.fori_loop(0, NEAR // WIDE, gather, 0)
    for copy in keep:
        copy.wait()


def back_kernel(*refs):
    grad_agg_ref, cot_ref, pre_ref, normed_ref, scale_ref, w_out_ref, sender_ref, recv_ref = refs[:8]
    edge_ref, near_ref, w_ref, list_ref, direct_ref = refs[8:13]
    grad_edges_ref, grad_fine_ref, in_edge_ref, out_ref, in_recv_ref, coarse_ref, in_send_ref = refs[13:20]
    t0, t1, d0, d1, a0, a1, recv_rep, for_mate, pack, back = refs[20:30]
    edge_total, tail_total, recv_total, send_total, send_ref = refs[30:35]
    shuffle = Shuffle(*refs[35:])
    shuffle.signal()
    send_ref[...] = halo_place(sender_ref[...], shuffle.core)
    recv_rep[...] = spread(recv_ref[...])
    a0[...], a1[...] = split(grad_agg_ref[...])
    w_out = split(w_out_ref[...])

    def step(at, carry):
        rows = block_at(at, WIDE)
        grad = cot_ref[rows, :] + dot2(hot_rows(recv_rep[rows, :], 0, NEAR), (a0[...], a1[...]))
        grad_edges_ref[rows, :] = grad
        tail = split(norm_back(grad, normed_ref[rows, :], scale_ref[rows, :1]))
        t0[rows, :], t1[rows, :] = tail
        pre = pre_ref[rows, :]
        gate = sigmoid(pre)
        put_pair((d0, d1), rows, dot3(tail, w_out, NT) * (gate * (1.0 + pre * (1.0 - gate))))
        return carry

    lax.fori_loop(0, EDGE // WIDE, step, 0)

    half = CHIPS * 8

    def halo_rows(first):
        rows = dot2(hot_columns(send_ref[...], NEAR + first, half), (d0[...], d1[...]))
        return rows.reshape(CHIPS, 8, FEAT)

    for_mate[...] = halo_rows(half)
    shuffle.wait_signals()
    swap = shuffle.core_copy(for_mate, pack.at[:, 1])
    swap.start()
    pack[:, 0] = halo_rows(0)
    swap.wait()
    shuffle.send_chips(pack, back)

    edge_total[...] = jnp.zeros_like(edge_total)
    tail_total[...] = jnp.zeros_like(tail_total)
    w_edge = split(w_ref[:FEAT, :])

    def weight_step(at, carry):
        rows = block_at(at)
        grad_pre = (d0[rows, :], d1[rows, :])
        grad_edges_ref[rows, :] += dot3(grad_pre, w_edge, NT)
        edge_total[...] += dot3(split(edge_ref[rows, :]), grad_pre, TN)
        pre = pre_ref[rows, :]
        tail_total[...] += dot3(split(pre * sigmoid(pre)), (t0[rows, :], t1[rows, :]), TN)
        return carry

    lax.fori_loop(0, EDGE // BLOCK, weight_step, 0)
    put_tiles(in_edge_ref, edge_total)
    put_tiles(out_ref, tail_total)
    w_send = split(w_ref[FEAT : 2 * FEAT, :])
    w_recv = split(w_ref[2 * FEAT :, :])

    def sums(at):
        grad_pre = (d0[...], d1[...])
        sent = dot2(hot_columns(send_ref[...], at * BLOCK, BLOCK), grad_pre)
        return sent, split(dot2(hot_columns(recv_ref[...], at * BLOCK, BLOCK), grad_pre))

    fine_sent, received = sums(0)
    grad_fine_ref[...] = direct_ref[...] + dot3(received, w_recv, NT)
    recv_total[...] = dot3(split(near_ref[:FINE, :]), received, TN)
    send_total[...] = jnp.zeros_like(send_total)

    def coarse_step(at, carry):
        rows = block_at(at)
        sent, received = sums(at)
        sent = split(sent)
        value = dot3(sent, w_send, NT) + dot3(received, w_recv, NT)
        put_tiles(coarse_ref.at[pl.ds((at - 1) * (BLOCK // 8), BLOCK // 8)], value)
        feats = split(near_ref[rows, :])
        recv_total[...] += dot3(feats, received, TN)
        send_total[...] += dot3(feats, sent, TN)
        return carry

    lax.fori_loop(1, NEAR // BLOCK, coarse_step, 0)
    put_tiles(in_recv_ref, recv_total)

    shuffle.wait_chips(pack, back)
    pack[:, 0] = back[:, shuffle.core]
    pack[:, 1] = back[:, 1 - shuffle.core]
    returned = split(pack[...].reshape(EDGE, FEAT))
    fine_sent = split(fine_sent + dot2(hot_columns(list_ref[...], 0, FINE), returned))
    grad_fine_ref[...] += dot3(fine_sent, w_send, NT)
    send_total[...] += dot3(split(near_ref[:FINE, :]), fine_sent, TN)
    put_tiles(in_send_ref, send_total)


OUT_ROW, EDGE_ROW, RECV_ROW, COARSE_ROW, SEND_ROW, ROWS = 192, 256, 320, 384, 480, 576


def sum_kernel(*refs):
    node_ref, out_ref, in_edge_ref, in_recv_ref, coarse_ref, in_send_ref, direct_ref = refs[:7]
    sum_ref, buf, got, sends, recvs = refs[7:]
    flat = buf.reshape(ROWS * 4, 8, 128)
    ring = Exchange(ALL_PARTS, buf, got, sum_ref, sends, recvs)
    ring.signal()
    row = 0
    for ref in (node_ref, out_ref, in_edge_ref, in_recv_ref, coarse_ref, in_send_ref):
        size = ref.shape[0]
        flat[row * 4 : (row + size) * 4] = ref[...].reshape(size * 4, 8, 128)
        if row == COARSE_ROW:
            flat[pl.ds(row * 4 + ring.me % 96 * 4, 4)] += direct_ref[...]
        row += size
        if row == SEND_ROW + 64:
            flat[row * 4 :] = jnp.zeros(((ROWS - row) * 4, 8, 128), F32)
            row = ROWS
    ring.wait_signals()
    ring.stage("start", *range(LINKS))
    ring.stage("start_kept", *range(LINKS))
    ring.run(ring.SUM)


def finish_kernel(pieces, sum_ref, coarse_ref, in_ref, out_ref, node_in_ref, node_out_ref, *rest):
    rows, stores = rest[:-1], rest[-1]
    outs = (coarse_ref, in_ref, out_ref, node_in_ref, node_out_ref)
    tiles = sum_ref.reshape(ROWS, 4, 8, 128)
    puts = []
    for at, (first, count, which, to, scale) in enumerate(pieces):
        for column in range(FEAT // 128):
            lanes = slice(column * 128, (column + 1) * 128)
            whole = min(count, (outs[which].shape[0] - to) // 8)
            value = tiles[first : first + whole, column] * scale
            rows[which][to : to + whole * 8, lanes] = value.reshape(whole * 8, 128)
            if whole < count:
                rows[which][to + whole * 8 :, lanes] = tiles[first + whole, column][: COARSE - whole * 8] * scale
        src, dst = rows[which], outs[which]
        if count * 8 < src.shape[0]:
            src, dst = src.at[pl.ds(to, count * 8)], dst.at[pl.ds(to, count * 8)]
        puts.append(pltpu.make_async_copy(src, dst, stores.at[at]))
        puts[-1].start()
    for put in puts:
        put.wait()


def finish(summed, edge_scale, node_scale):
    pieces = [
        (0, 64, 3, 0, node_scale),
        (64, 64, 3, FEAT, node_scale),
        (128, 64, 4, 0, node_scale),
        (OUT_ROW, 64, 2, 0, edge_scale),
        (EDGE_ROW, 64, 1, 0, edge_scale),
        (RECV_ROW, 64, 1, 2 * FEAT, edge_scale),
        (COARSE_ROW, 81, 0, 0, 1.0),
        (SEND_ROW, 64, 1, FEAT, edge_scale),
    ]
    any_spec = pl.BlockSpec(memory_space=pl.ANY)
    sizes = (COARSE, 3 * FEAT, FEAT, 2 * FEAT, FEAT)
    sem = pltpu.SemaphoreType.DMA((len(pieces),))
    return pl.pallas_call(
        functools.partial(finish_kernel, pieces),
        out_shape=[f32_out(size, FEAT) for size in sizes],
        in_specs=vmem_specs(1),
        out_specs=[any_spec] * 5,
        scratch_shapes=[pltpu.VMEM((size, FEAT), F32) for size in sizes] + [sem],
        compiler_params=pltpu.CompilerParams(vmem_limit_bytes=24 << 20),
    )(summed)


def per_device(
    fine_nodes,
    coarse_nodes,
    edge_feats,
    senders,
    receivers,
    send_rows,
    w_edge_in,
    w_edge_out,
    w_node_in,
    w_node_out,
    cot_fine,
    cot_coarse,
    cot_edges,
):
    peers = lax.axis_size("patch")
    send_list = send_rows.reshape(1, EDGE)
    send_at = senders.reshape(1, EDGE)
    recv_at = receivers.reshape(1, EDGE)
    half = pltpu.VMEM((EDGE, FEAT), BF16)
    index = pltpu.VMEM((EDGE, 128), jnp.int32)
    square = pltpu.VMEM((FEAT, FEAT), F32)
    chip_rows = pltpu.VMEM((CHIPS, 2, 8, FEAT), F32)
    core_rows = pltpu.VMEM((CHIPS, 8, FEAT), F32)
    sems = [pltpu.SemaphoreType.DMA] * 4
    wide = f32_out(EDGE, FEAT)
    fine_out = f32_out(FINE, FEAT)

    rows = pltpu.VMEM((EDGE, FEAT), F32)
    rep_out = f32_out(EDGE, 128)
    row_index = pltpu.VMEM((1, EDGE), jnp.int32)
    hbm = pl.BlockSpec(memory_space=pltpu.HBM)
    agg, pre, normed, scale, near = pl.pallas_call(
        front_kernel,
        out_shape=[wide, wide, wide, rep_out, wide],
        in_specs=vmem_specs(3) + [hbm] * 5,
        out_specs=vmem_specs(1) + [hbm] * 4,
        scratch_shapes=[chip_rows, chip_rows, core_rows]
        + [half] * 8
        + [index] * 2
        + [rows, pltpu.VMEM((COARSE, FEAT), F32), pltpu.VMEM((3 * FEAT, FEAT), F32), rows, square]
        + [rows, rows, pltpu.VMEM((EDGE, 128), F32), row_index]
        + [pltpu.SemaphoreType.DMA((5,)), pltpu.SemaphoreType.DMA((4,))]
        + sems,
        compiler_params=pltpu.CompilerParams(collective_id=1, has_side_effects=True, vmem_limit_bytes=FRONT_MIB << 20),
    )(send_list, send_at, recv_at, fine_nodes, w_edge_in, coarse_nodes, edge_feats, w_edge_out)
    grad_agg, direct, few_direct, node = node_step(
        agg, fine_nodes, cot_fine, coarse_nodes, cot_coarse, w_node_in, w_node_out
    )
    grad_edges, grad_fine, in_edge, edge_out, in_recv, coarse, in_send = remote_call(
        back_kernel,
        3,
        [wide, fine_out, TILES, TILES, TILES, f32_out(96, 4, 8, 128), TILES],
        [half] * 6 + [index, core_rows, chip_rows, chip_rows] + [square] * 4 + [row_index] + sems,
        BACK_MIB,
        grad_agg,
        cot_edges,
        pre,
        normed,
        scale,
        w_edge_out,
        send_at,
        recv_at,
        edge_feats,
        near,
        w_edge_in,
        send_list,
        direct,
    )
    (summed,) = remote_call(
        sum_kernel, 4, [sum_out(3)], exchange_scratch(LINKS, 3), SUM_MIB, node, edge_out, in_edge, in_recv, coarse, in_send, few_direct
    )
    edge_scale = 1.0 / math.sqrt(EDGE * peers)
    node_scale = 1.0 / math.sqrt(FINE * peers + COARSE)
    grad_coarse, grad_in, grad_out, grad_node_in, grad_node_out = finish(summed, edge_scale, node_scale)
    return grad_fine, grad_coarse, grad_edges, grad_in, grad_out, grad_node_in, grad_node_out


def solution(mesh):
    return jax.shard_map(
        per_device,
        mesh=mesh,
        in_specs=(
            P("patch", None),
            P(),
            P("patch", None),
            P("patch"),
            P("patch"),
            P("patch", None, None),
            P(),
            P(),
            P(),
            P(),
            P("patch", None),
            P(),
            P("patch", None),
        ),
        out_specs=(P("patch", None), P(), P("patch", None), P(), P(), P(), P()),
        check_vma=False,
    )
```

```python
import functools
import math

import jax
import jax.numpy as jnp
from jax import lax
from jax.experimental import pallas as pl
from jax.experimental.pallas import tpu as pltpu
from jax.sharding import PartitionSpec as P

MESH = pl.DeviceIdType.MESH
F32 = jnp.float32
BF16 = jnp.bfloat16
FEAT = 512
FINE = 256
COARSE = 642
NEAR = 1024
EDGE = 1024
BLOCK = 256
LINKS = 6
WIDE = 512
FRONT_MIB, BACK_MIB, SUM_MIB = 60, 42, 30

NN = (((1,), (0,)), ((), ()))
NT = (((1,), (1,)), ((), ()))
TN = (((0,), (0,)), ((), ()))


def split(value):
    high = value.astype(BF16)
    return high, (value - high.astype(F32)).astype(BF16)


def dot(left, right, dims=NN):
    return lax.dot_general(left, right, dims, preferred_element_type=F32)


def dot3(left, right, dims=NN):
    return dot(left[0], right[0], dims) + dot(left[0], right[1], dims) + dot(left[1], right[0], dims)


def dot2(left, right, dims=NN):
    return dot(left, right[0], dims) + dot(left, right[1], dims)


def block_at(step, size=BLOCK):
    return pl.ds(pl.multiple_of(step * size, size), size)


def pair_at(refs, rows):
    return refs[0][rows, :], refs[1][rows, :]


def put_pair(refs, rows, value):
    high, low = split(value)
    refs[0][rows, :] = high
    refs[1][rows, :] = low


def spread(index_row):
    return jnp.transpose(jnp.broadcast_to(index_row, (128, index_row.shape[1])))


def hot_rows(spread_block, first, width):
    lane = lax.broadcasted_iota(jnp.int32, (spread_block.shape[0], 128), 1)
    local = spread_block - first
    tiles = [jnp.where(local == lane + at, 1.0, 0.0).astype(BF16) for at in range(0, width, 128)]
    return jnp.concatenate(tiles, axis=1)


def hot_columns(index_row, first, height):
    row = lax.broadcasted_iota(jnp.int32, (height, index_row.shape[1]), 0) + first
    return jnp.where(row == index_row, 1.0, 0.0).astype(BF16)


def sigmoid(value):
    return 1.0 / (1.0 + jnp.exp(-value))


def mean(value):
    return jnp.sum(value, axis=1, keepdims=True) * (1.0 / FEAT)


def norm(value):
    center = value - mean(value)
    scale = lax.rsqrt(mean(center * center) + 1e-05)
    return center * scale, scale


def norm_back(grad, normed, scale):
    return scale * (grad - mean(grad) - normed * mean(grad * normed))


def put_tiles(ref, value):
    for at in range(FEAT // 128):
        ref[:, at] = value[:, at * 128 : (at + 1) * 128].reshape(-1, 8, 128)


def vmem_specs(count):
    return [pl.BlockSpec(memory_space=pltpu.VMEM)] * count


def f32_out(*shape):
    return jax.ShapeDtypeStruct(shape, F32)


def bf16_out(*shape):
    return jax.ShapeDtypeStruct(shape, BF16)


TILES = f32_out(64, 4, 8, 128)


STRIDES = (32, 8, 2)
ALL_PARTS = tuple((part % 3, part // 3) for part in range(6))
FOUR_PARTS = ALL_PARTS[:4]
GOT_CHUNKS = 127
SEM_COUNT = 24


def axis_places(device):
    return [(device // 32) % 4, (device // 8) % 4, (device // 2) % 4], device % 2


def axis_bits(place):
    return ((place + 1) // 2) % 2, place // 2


def position(device, spec):
    places, core = axis_places(device)
    first, flip = spec
    bits = axis_bits(places[first])
    spot = (core * 2 + bits[flip]) * 2 + bits[1 - flip]
    return (spot * 4 + places[(first + 1) % 3]) * 4 + places[(first + 2) % 3]


class Exchange:
    def __init__(self, specs, buf, got, out, sends, recvs):
        self.specs, self.buf, self.got, self.out, self.sends, self.recvs = specs, buf, got, out, sends, recvs
        self.me = lax.axis_index("patch")
        self.places, self.core = axis_places(self.me)
        self.mate = self.me + 1 - 2 * self.core
        self.bits = [axis_bits(place) for place in self.places]
        self.flying = {}
        self.spot = {}
        for part, (first, flip) in enumerate(specs):
            one, two = self.bits[first][flip], self.bits[first][1 - flip]
            third, fourth = self.places[(first + 1) % 3], self.places[(first + 2) % 3]
            at_core = self.core * 64
            at_one = at_core + one * 32
            at_two = at_one + two * 16
            at_three = at_two + third * 4
            self.spot[part] = dict(
                one=one, two=two, core=at_core, first=at_one, second=at_two, third=at_three, last=at_three + fourth
            )

    def signal(self):
        mates = [self.mate]
        mates += [self.peer(axis, shift) for axis in range(3) for shift in (1, 2, 3)]
        barrier = pltpu.get_barrier_semaphore()
        for mate in mates:
            pl.semaphore_signal(barrier, inc=1, device_id=(mate,), device_id_type=MESH)

    def wait_signals(self):
        pl.semaphore_wait(pltpu.get_barrier_semaphore(), 10)

    def peer(self, axis, shift):
        return self.me + ((self.places[axis] + shift) % 4 - self.places[axis]) * STRIDES[axis]

    def neighbour(self, axis, flip):
        place = self.places[axis]
        step = 3 - 2 * place if flip else 1 - 2 * (place % 2)
        return self.me + step * STRIDES[axis]

    def push(self, part, sem, src, dst, device):
        copy = pltpu.make_async_remote_copy(
            src_ref=src,
            dst_ref=dst,
            send_sem=self.sends.at[sem, part],
            recv_sem=self.recvs.at[sem, part],
            device_id=(device,),
            device_id_type=MESH,
        )
        copy.start()
        self.flying[part, sem] = copy

    def wait(self, part, *sems):
        for sem in sems:
            self.flying.pop((part, sem)).wait()

    def send_sum(self, part, sem, at, size, slot, device):
        self.push(part, sem, self.buf.at[part, pl.ds(at, size)], self.got.at[part, pl.ds(slot, size)], device)

    def add(self, part, at, size, *slots):
        total = self.buf[part, pl.ds(at, size)]
        for slot in slots:
            total += self.got[part, pl.ds(slot, size)]
        self.buf[part, pl.ds(at, size)] = total

    def send_block(self, part, sem, at, size, device):
        block = self.out.at[part, pl.ds(at, size)]
        self.push(part, sem, block, block, device)


    def start(self, part):
        spot = self.spot[part]
        other = 64 - spot["core"]
        self.send_sum(part, 0, other + (1 - spot["one"]) * 32, 32, 0, self.mate)

    def start_kept(self, part):
        spot = self.spot[part]
        other = 64 - spot["core"]
        self.send_sum(part, 1, other + spot["one"] * 32, 32, 32, self.mate)

    def reduce_first(self, part):
        spot = self.spot[part]
        first, flip = self.specs[part]
        away = spot["core"] + (1 - spot["one"]) * 32
        device = self.neighbour(first, flip)
        self.wait(part, 0)
        self.add(part, away, 32, 0)
        self.send_sum(part, 2, away + (1 - spot["two"]) * 16, 16, 64, device)
        self.send_sum(part, 3, away + spot["two"] * 16, 16, 80, device)

    def reduce_kept(self, part):
        self.wait(part, 1)
        self.add(part, self.spot[part]["first"], 32, 32)

    def reduce_second(self, part):
        spot = self.spot[part]
        first, flip = self.specs[part]
        away = spot["first"] + (1 - spot["two"]) * 16
        self.wait(part, 2)
        self.add(part, away, 16, 64)
        self.send_sum(part, 4, away, 16, 96, self.neighbour(first, 1 - flip))

    def reduce_third(self, part):
        spot = self.spot[part]
        axis = (self.specs[part][0] + 1) % 3
        self.wait(part, 3, 4)
        self.add(part, spot["second"], 16, 80, 96)
        for shift in (1, 2, 3):
            at = spot["second"] + (self.places[axis] + shift) % 4 * 4
            self.send_sum(part, 4 + shift, at, 4, 108 + 4 * shift, self.peer(axis, shift))

    def reduce_fourth(self, part):
        spot = self.spot[part]
        axis = (self.specs[part][0] + 2) % 3
        self.wait(part, 5, 6, 7)
        self.add(part, spot["third"], 4, 112, 116, 120)
        for shift in (1, 2, 3):
            at = spot["third"] + (self.places[axis] + shift) % 4
            self.send_sum(part, 7 + shift, at, 1, 123 + shift, self.peer(axis, shift))

    def reduce_last(self, part):
        self.wait(part, 8, 9, 10)
        self.add(part, self.spot[part]["last"], 1, 124, 125, 126)

    def gather_fourth(self, part):
        axis = (self.specs[part][0] + 2) % 3
        for shift in (1, 2, 3):
            self.send_block(part, 10 + shift, self.spot[part]["last"], 1, self.peer(axis, shift))

    def gather_third(self, part):
        axis = (self.specs[part][0] + 1) % 3
        self.wait(part, 11, 12, 13)
        for shift in (1, 2, 3):
            self.send_block(part, 13 + shift, self.spot[part]["third"], 4, self.peer(axis, shift))

    def gather_second(self, part):
        spot = self.spot[part]
        first, flip = self.specs[part]
        self.wait(part, 14, 15, 16)
        self.send_block(part, 17, spot["second"], 16, self.neighbour(first, 1 - flip))
        self.send_block(part, 20, spot["second"], 16, self.mate)

    def gather_first(self, part):
        spot = self.spot[part]
        first, flip = self.specs[part]
        device = self.neighbour(first, flip)
        self.wait(part, 17)
        self.send_block(part, 18, spot["first"], 16, device)
        self.send_block(part, 19, spot["first"] + 16, 16, device)
        self.send_block(part, 21, spot["first"] + (1 - spot["two"]) * 16, 16, self.mate)

    def gather_core(self, part):
        spot = self.spot[part]
        self.wait(part, 18)
        self.send_block(part, 22, spot["core"] + (1 - spot["one"]) * 32, 16, self.mate)

    def gather_rest(self, part):
        spot = self.spot[part]
        self.wait(part, 19)
        self.send_block(part, 23, spot["core"] + (1 - spot["one"]) * 32 + 16, 16, self.mate)

    def gather_last(self, part):
        self.wait(part, 20, 21, 22, 23)

    REDUCE = ("reduce_first", "reduce_kept", "reduce_second", "reduce_third", "reduce_fourth", "reduce_last")
    GATHER = ("gather_fourth", "gather_third", "gather_second", "gather_first", "gather_core", "gather_rest", "gather_last")

    def stage(self, stage, *parts):
        for part in parts:
            getattr(self, stage)(part)

    def run(self, stages, beside=()):
        beside = list(beside)
        for stage in stages:
            if beside:
                beside.pop(0)()
            self.stage(stage, *range(len(self.specs)))
        for work in beside:
            work()

    def finish_sum(self, part):
        self.reduce_last(part)
        last = pl.ds(self.spot[part]["last"], 1)
        self.out[part, last] = self.buf[part, last]
        self.gather_fourth(part)

    SUM = REDUCE[:-1] + ("finish_sum",) + GATHER[1:]


def exchange_scratch(parts, units):
    sem = pltpu.SemaphoreType.DMA((SEM_COUNT, parts))
    return [
        pltpu.VMEM((parts, 128, units, 8, 128), F32),
        pltpu.VMEM((parts, GOT_CHUNKS, units, 8, 128), F32),
        sem,
        sem,
    ]


def sum_out(units):
    return f32_out(LINKS, 128, units, 8, 128)


def remote_call(kernel, name_id, outs, scratch, limit, *args):
    return pl.pallas_call(
        kernel,
        out_shape=outs,
        in_specs=vmem_specs(len(args)),
        out_specs=vmem_specs(len(outs)),
        scratch_shapes=scratch,
        compiler_params=pltpu.CompilerParams(collective_id=name_id, has_side_effects=True, vmem_limit_bytes=limit << 20),
        cost_estimate=pl.CostEstimate(flops=int(3e10), bytes_accessed=int(3e7), transcendentals=0),
    )(*args)


def few_dot3(left, right, dims=NN):
    count = left[0].shape[0]
    both = dot(jnp.concatenate(left, axis=0), right[0], dims)
    return both[:count] + both[count:] + dot(left[0], right[1], dims)


class NodePass:
    def __init__(self, product, w_in, w_out):
        self.product, self.w_in, self.w_out = product, w_in, w_out

    def first(self, feats, agg):
        self.feats, self.agg = split(feats), split(agg)
        pre = self.product(self.feats, pair_at(self.w_in, pl.ds(0, FEAT)))
        self.pre = pre + self.product(self.agg, pair_at(self.w_in, pl.ds(FEAT, FEAT)))
        self.gate = sigmoid(self.pre)
        self.hidden = split(self.pre * self.gate)

    def second(self):
        self.normed, self.scale = norm(self.product(self.hidden, pair_at(self.w_out, pl.ds(0, FEAT))))

    def third(self, cot):
        self.tail = split(norm_back(cot, self.normed, self.scale))
        grad = self.product(self.tail, pair_at(self.w_out, pl.ds(0, FEAT)), NT)
        self.grad = split(grad * (self.gate * (1.0 + self.pre * (1.0 - self.gate))))

    def back(self, first):
        return self.product(self.grad, pair_at(self.w_in, pl.ds(first, FEAT)), NT)


def few_rows(ref, me):
    whole = COARSE // 8
    rows = ref[pl.ds(pl.multiple_of(me % whole * 8, 8), 8), :]
    rest = jnp.concatenate([ref[whole * 8 :, :], jnp.zeros((8 - COARSE % 8, FEAT), F32)], axis=0)
    return jnp.where(me < whole, rows, jnp.where(me == whole, rest, 0.0))


def node_kernel(*refs):
    agg_ref, fine_ref, cot_ref, coarse_ref, coarse_cot_ref, w_in_ref, w_out_ref = refs[:7]
    grad_agg_ref, own_ref, direct_ref, node_ref = refs[7:11]
    buf, got, sends, recvs, full, wi0, wi1, wo0, wo1, total = refs[11:]
    ring = Exchange(FOUR_PARTS, buf, got, full, sends, recvs)
    ring.signal()
    for part, spec in enumerate(FOUR_PARTS):
        for device in range(128):
            first = FINE + 8 * device
            if first < NEAR and 8 * device < COARSE:
                buf[part, position(device, spec), 0] = agg_ref[first : first + 8, part * 128 : (part + 1) * 128]
            else:
                buf[part, position(device, spec), 0] = jnp.zeros((8, 128), F32)
    ring.wait_signals()
    ring.stage("start", *range(4))
    ring.stage("start_kept", *range(4))

    wi, wo = (wi0, wi1), (wo0, wo1)
    fine = NodePass(dot3, wi, wo)
    few = NodePass(few_dot3, wi, wo)
    few_feats, few_cot = few_rows(coarse_ref, ring.me), few_rows(coarse_cot_ref, ring.me)

    def cut_weights():
        wi0[...], wi1[...] = split(w_in_ref[...])
        wo0[...], wo1[...] = split(w_out_ref[...])

    def fine_first():
        fine.first(fine_ref[...], agg_ref[:FINE, :])

    def fine_third():
        fine.third(cot_ref[...])

    def fine_back():
        own_ref[...] = cot_ref[...] + fine.back(0)

    def fine_agg():
        grad_agg_ref[:FINE, :] = fine.back(FEAT)

    ring.run(ring.REDUCE, [cut_weights, fine_first, fine.second, fine_third, fine_back, fine_agg])

    few_agg = jnp.concatenate([buf[part, ring.spot[part]["last"], 0] for part in range(4)], axis=1)
    blank = jnp.zeros((8, FEAT), F32)
    few.first(jnp.concatenate([few_feats, blank], axis=0), jnp.concatenate([few_agg, blank], axis=0))
    few.second()
    few.third(jnp.concatenate([few_cot, blank], axis=0))
    few_grad = few.back(FEAT)[:8]
    for part in range(4):
        full[part, ring.spot[part]["last"], 0] = few_grad[:, part * 128 : (part + 1) * 128]

    def few_back():
        direct = few_cot + few.back(0)[:8]
        for at in range(4):
            direct_ref[at] = direct[:, at * 128 : (at + 1) * 128]

    def weights_back(which, grad, first):
        def run():
            total[...] = dot3(getattr(fine, which), getattr(fine, grad), TN) + dot3(getattr(few, which), getattr(few, grad), TN)
            put_tiles(node_ref.at[pl.ds(first, 64)], total)

        return run

    def nothing():
        pass

    beside = [nothing, few_back]
    beside += [weights_back("feats", "grad", 0), weights_back("agg", "grad", 64), weights_back("hidden", "tail", 128)]
    ring.run(ring.GATHER, beside)
    for part, spec in enumerate(FOUR_PARTS):
        for device in range((NEAR - FINE) // 8):
            first = FINE + 8 * device
            grad_agg_ref[first : first + 8, part * 128 : (part + 1) * 128] = full[part, position(device, spec), 0]


def node_step(agg, fine, cot_fine, coarse, cot_coarse, w_in, w_out):
    half = pltpu.VMEM((2 * FEAT, FEAT), BF16)
    quarter = pltpu.VMEM((FEAT, FEAT), BF16)
    return remote_call(
        node_kernel,
        2,
        [f32_out(NEAR, FEAT), f32_out(FINE, FEAT), f32_out(4, 8, 128), f32_out(192, 4, 8, 128)],
        exchange_scratch(4, 1)
        + [pltpu.VMEM((4, 128, 1, 8, 128), F32), half, half, quarter, quarter, pltpu.VMEM((FEAT, FEAT), F32)],
        34,
        agg,
        fine,
        cot_fine,
        coarse,
        cot_coarse,
        w_in,
        w_out,
    )


CHIPS = 64


class Shuffle:
    def __init__(self, sends, recvs, core_sends, core_recvs):
        self.sends, self.recvs, self.core_sends, self.core_recvs = sends, recvs, core_sends, core_recvs
        self.me = lax.axis_index("patch")
        self.places, self.core = axis_places(self.me)
        self.chip = self.me // 2
        self.mate = self.me + 1 - 2 * self.core

    def other(self, step):
        z, x, y = ((place + step // span) % 4 for place, span in zip(self.places, (16, 4, 1)))
        return z * 16 + x * 4 + y

    def each(self, run):
        def body(step, carry):
            run(self.other(step))
            return carry

        lax.fori_loop(1, CHIPS, body, 0)

    def signal(self):
        barrier = pltpu.get_barrier_semaphore()

        def run(chip):
            pl.semaphore_signal(barrier, inc=1, device_id=(chip * 2 + self.core,), device_id_type=MESH)

        self.each(run)
        pl.semaphore_signal(barrier, inc=1, device_id=(self.mate,), device_id_type=MESH)

    def wait_signals(self):
        pl.semaphore_wait(pltpu.get_barrier_semaphore(), CHIPS)

    def copy(self, src, dst, sends, recvs, device):
        return pltpu.make_async_remote_copy(
            src_ref=src, dst_ref=dst, send_sem=sends, recv_sem=recvs, device_id=(device,), device_id_type=MESH
        )

    def send_chips(self, src, dst):
        def run(chip):
            self.copy(src.at[chip], dst.at[self.chip], self.sends, self.recvs, chip * 2 + self.core).start()

        self.each(run)
        dst[self.chip] = src[self.chip]

    def wait_chips(self, src, dst):
        most = pl.ds(0, CHIPS - 1)
        self.copy(src.at[most], dst.at[most], self.sends, self.recvs, self.mate).wait()

    def core_copy(self, src, dst):
        return self.copy(src, dst, self.core_sends, self.core_recvs, self.mate)


def halo_place(senders, core):
    halo = senders - (FINE + COARSE)
    source = jnp.right_shift(halo, 3)
    kind = jnp.bitwise_and(source + core, 1)
    place = NEAR + kind * (EDGE // 2) + jnp.right_shift(source, 1) * 8 + jnp.bitwise_and(halo, 7)
    return jnp.where(halo < 0, senders, place)


def front_kernel(*refs):
    list_ref, sender_ref, recv_ref = refs[:3]
    far_in, agg_ref, far_out = refs[3:8], refs[8], refs[9:13]
    outgoing, got, from_mate, p0, p1, q0, q1, h0, h1, n0, n1, rep, recv_rep = refs[13:26]
    near_ref, coarse_ref, w_ref, edge_ref, w_out_ref, pre_ref, normed_ref, scale_ref, send_ref, loads, stores = refs[26:37]
    shuffle = Shuffle(*refs[37:])
    places = (near_ref.at[pl.ds(0, FINE)], w_ref, coarse_ref, edge_ref, w_out_ref)
    fetch = [pltpu.make_async_copy(src, dst, loads.at[at]) for at, (src, dst) in enumerate(zip(far_in, places))]
    for copy in fetch:
        copy.start()
    results = (pre_ref, normed_ref, scale_ref, near_ref)
    keep = [pltpu.make_async_copy(src, dst, stores.at[at]) for at, (src, dst) in enumerate(zip(results, far_out))]
    shuffle.signal()
    rep[...] = spread(list_ref[...])
    send_ref[...] = halo_place(sender_ref[...], shuffle.core)
    for copy in fetch[:2]:
        copy.wait()
    w_send = split(w_ref[FEAT : 2 * FEAT, :])
    own = split(dot3(split(near_ref[:FINE, :]), w_send))

    def request(at, carry):
        rows = block_at(at, WIDE)
        chips = pl.ds(at * (WIDE // 16), WIDE // 16)
        outgoing[chips] = dot2(hot_rows(rep[rows, :], 0, FINE), own).reshape(WIDE // 16, 2, 8, FEAT)
        return carry

    lax.fori_loop(0, EDGE // WIDE, request, 0)
    shuffle.wait_signals()
    shuffle.send_chips(outgoing, got)

    rep[...] = spread(send_ref[...])
    recv_rep[...] = spread(recv_ref[...])
    w_recv = split(w_ref[2 * FEAT :, :])
    whole = COARSE // 8 * 8
    for copy in fetch[2:]:
        copy.wait()
    near_ref[FINE : FINE + whole, :] = coarse_ref[:whole, :]
    near_ref[FINE + whole :, :] = jnp.zeros((NEAR - FINE - whole, FEAT), F32)
    near_ref[FINE + whole : FINE + COARSE, :] = coarse_ref[whole:, :]
    keep[3].start()

    def project(at, carry):
        rows = block_at(at, WIDE)
        feats = split(near_ref[rows, :])
        put_pair((p0, p1), rows, dot3(feats, w_send))
        put_pair((q0, q1), rows, dot3(feats, w_recv))
        return carry

    lax.fori_loop(0, NEAR // WIDE, project, 0)
    w_edge = split(w_ref[:FEAT, :])

    def near_step(at, carry):
        rows = block_at(at, WIDE)
        total = dot3(split(edge_ref[rows, :]), w_edge)
        total += dot2(hot_rows(recv_rep[rows, :], 0, NEAR), (q0[...], q1[...]))
        total += dot2(hot_rows(rep[rows, :], 0, NEAR), (p0[...], p1[...]))
        pre_ref[rows, :] = total
        return carry

    lax.fori_loop(0, EDGE // WIDE, near_step, 0)

    shuffle.wait_chips(outgoing, got)
    swap = shuffle.core_copy(got.at[:, 1 - shuffle.core], from_mate)
    swap.start()
    half = CHIPS * 8
    put_pair((h0, h1), pl.ds(0, half), got[:, shuffle.core].reshape(half, FEAT))
    w_out = split(w_out_ref[...])

    def halo_step(at, carry):
        rows = block_at(at, WIDE)
        pre_ref[rows, :] += dot2(hot_rows(rep[rows, :], NEAR, half), pair_at((h0, h1), pl.ds(0, half)))
        return carry

    lax.fori_loop(0, EDGE // WIDE, halo_step, 0)
    swap.wait()
    put_pair((h0, h1), pl.ds(half, half), from_mate[...].reshape(half, FEAT))

    def edge_step(at, carry):
        rows = block_at(at, WIDE)
        pre = pre_ref[rows, :] + dot2(hot_rows(rep[rows, :], NEAR + half, half), pair_at((h0, h1), pl.ds(half, half)))
        pre_ref[rows, :] = pre
        normed, scale = norm(dot3(split(pre * sigmoid(pre)), w_out))
        normed_ref[rows, :] = normed
        scale_ref[rows, :] = jnp.broadcast_to(scale, (WIDE, 128))
        put_pair((n0, n1), rows, edge_ref[rows, :] + normed)
        return carry

    lax.fori_loop(0, EDGE // WIDE, edge_step, 0)
    for copy in keep[:3]:
        copy.start()

    def gather(at, carry):
        rows = block_at(at, WIDE)
        agg_ref[rows, :] = dot2(hot_columns(recv_ref[...], at * WIDE, WIDE), (n0[...], n1[...]))
        return carry

    lax.fori_loop(0, NEAR // WIDE, gather, 0)
    for copy in keep:
        copy.wait()


def back_kernel(*refs):
    grad_agg_ref, cot_ref, pre_ref, normed_ref, scale_ref, w_out_ref, sender_ref, recv_ref = refs[:8]
    edge_ref, near_ref, w_ref, list_ref, direct_ref = refs[8:13]
    grad_edges_ref, grad_fine_ref, in_edge_ref, out_ref, in_recv_ref, coarse_ref, in_send_ref = refs[13:20]
    t0, t1, d0, d1, a0, a1, recv_rep, for_mate, pack, back = refs[20:30]
    edge_total, tail_total, recv_total, send_total, send_ref = refs[30:35]
    shuffle = Shuffle(*refs[35:])
    shuffle.signal()
    send_ref[...] = halo_place(sender_ref[...], shuffle.core)
    recv_rep[...] = spread(recv_ref[...])
    a0[...], a1[...] = split(grad_agg_ref[...])
    w_out = split(w_out_ref[...])

    def step(at, carry):
        rows = block_at(at, WIDE)
        grad = cot_ref[rows, :] + dot2(hot_rows(recv_rep[rows, :], 0, NEAR), (a0[...], a1[...]))
        grad_edges_ref[rows, :] = grad
        tail = split(norm_back(grad, normed_ref[rows, :], scale_ref[rows, :1]))
        t0[rows, :], t1[rows, :] = tail
        pre = pre_ref[rows, :]
        gate = sigmoid(pre)
        put_pair((d0, d1), rows, dot3(tail, w_out, NT) * (gate * (1.0 + pre * (1.0 - gate))))
        return carry

    lax.fori_loop(0, EDGE // WIDE, step, 0)

    half = CHIPS * 8

    def halo_rows(first):
        rows = dot2(hot_columns(send_ref[...], NEAR + first, half), (d0[...], d1[...]))
        return rows.reshape(CHIPS, 8, FEAT)

    for_mate[...] = halo_rows(half)
    shuffle.wait_signals()
    swap = shuffle.core_copy(for_mate, pack.at[:, 1])
    swap.start()
    pack[:, 0] = halo_rows(0)
    swap.wait()
    shuffle.send_chips(pack, back)

    edge_total[...] = jnp.zeros_like(edge_total)
    tail_total[...] = jnp.zeros_like(tail_total)
    w_edge = split(w_ref[:FEAT, :])

    def weight_step(at, carry):
        rows = block_at(at)
        grad_pre = (d0[rows, :], d1[rows, :])
        grad_edges_ref[rows, :] += dot3(grad_pre, w_edge, NT)
        edge_total[...] += dot3(split(edge_ref[rows, :]), grad_pre, TN)
        pre = pre_ref[rows, :]
        tail_total[...] += dot3(split(pre * sigmoid(pre)), (t0[rows, :], t1[rows, :]), TN)
        return carry

    lax.fori_loop(0, EDGE // BLOCK, weight_step, 0)
    put_tiles(in_edge_ref, edge_total)
    put_tiles(out_ref, tail_total)
    w_send = split(w_ref[FEAT : 2 * FEAT, :])
    w_recv = split(w_ref[2 * FEAT :, :])

    def sums(at):
        grad_pre = (d0[...], d1[...])
        sent = dot2(hot_columns(send_ref[...], at * BLOCK, BLOCK), grad_pre)
        return sent, split(dot2(hot_columns(recv_ref[...], at * BLOCK, BLOCK), grad_pre))

    fine_sent, received = sums(0)
    grad_fine_ref[...] = direct_ref[...] + dot3(received, w_recv, NT)
    recv_total[...] = dot3(split(near_ref[:FINE, :]), received, TN)
    send_total[...] = jnp.zeros_like(send_total)

    def coarse_step(at, carry):
        rows = block_at(at)
        sent, received = sums(at)
        sent = split(sent)
        value = dot3(sent, w_send, NT) + dot3(received, w_recv, NT)
        put_tiles(coarse_ref.at[pl.ds((at - 1) * (BLOCK // 8), BLOCK // 8)], value)
        feats = split(near_ref[rows, :])
        recv_total[...] += dot3(feats, received, TN)
        send_total[...] += dot3(feats, sent, TN)
        return carry

    lax.fori_loop(1, NEAR // BLOCK, coarse_step, 0)
    put_tiles(in_recv_ref, recv_total)

    shuffle.wait_chips(pack, back)
    pack[:, 0] = back[:, shuffle.core]
    pack[:, 1] = back[:, 1 - shuffle.core]
    returned = split(pack[...].reshape(EDGE, FEAT))
    fine_sent = split(fine_sent + dot2(hot_columns(list_ref[...], 0, FINE), returned))
    grad_fine_ref[...] += dot3(fine_sent, w_send, NT)
    send_total[...] += dot3(split(near_ref[:FINE, :]), fine_sent, TN)
    put_tiles(in_send_ref, send_total)


OUT_ROW, EDGE_ROW, RECV_ROW, COARSE_ROW, SEND_ROW, ROWS = 192, 256, 320, 384, 480, 576


def sum_kernel(*refs):
    node_ref, out_ref, in_edge_ref, in_recv_ref, coarse_ref, in_send_ref, direct_ref = refs[:7]
    sum_ref, buf, got, sends, recvs = refs[7:]
    flat = buf.reshape(ROWS * 4, 8, 128)
    ring = Exchange(ALL_PARTS, buf, got, sum_ref, sends, recvs)
    ring.signal()
    row = 0
    for ref in (node_ref, out_ref, in_edge_ref, in_recv_ref, coarse_ref, in_send_ref):
        size = ref.shape[0]
        flat[row * 4 : (row + size) * 4] = ref[...].reshape(size * 4, 8, 128)
        if row == COARSE_ROW:
            flat[pl.ds(row * 4 + ring.me % 96 * 4, 4)] += direct_ref[...]
        row += size
        if row == SEND_ROW + 64:
            flat[row * 4 :] = jnp.zeros(((ROWS - row) * 4, 8, 128), F32)
            row = ROWS
    ring.wait_signals()
    ring.stage("start", *range(LINKS))
    ring.stage("start_kept", *range(LINKS))
    ring.run(ring.SUM)


def finish_kernel(pieces, sum_ref, edges_ref, fine_ref, coarse_ref, in_ref, out_ref, node_in_ref, node_out_ref, edges_out, fine_out, *rest):
    rows, stores, passes = rest[:-2], rest[-2], rest[-1]
    outs = (coarse_ref, in_ref, out_ref, node_in_ref, node_out_ref)
    tiles = sum_ref.reshape(ROWS, 4, 8, 128)
    puts = [
        pltpu.make_async_copy(edges_ref, edges_out, passes.at[0]),
        pltpu.make_async_copy(fine_ref, fine_out, passes.at[1]),
    ]
    for put in puts:
        put.start()
    for at, (first, count, which, to, scale) in enumerate(pieces):
        for column in range(FEAT // 128):
            lanes = slice(column * 128, (column + 1) * 128)
            whole = min(count, (outs[which].shape[0] - to) // 8)
            value = tiles[first : first + whole, column] * scale
            rows[which][to : to + whole * 8, lanes] = value.reshape(whole * 8, 128)
            if whole < count:
                rows[which][to + whole * 8 :, lanes] = tiles[first + whole, column][: COARSE - whole * 8] * scale
        src, dst = rows[which], outs[which]
        if count * 8 < src.shape[0]:
            src, dst = src.at[pl.ds(to, count * 8)], dst.at[pl.ds(to, count * 8)]
        puts.append(pltpu.make_async_copy(src, dst, stores.at[at]))
        puts[-1].start()
    for put in puts:
        put.wait()


def finish(summed, grad_edges, grad_fine, edge_scale, node_scale):
    pieces = [
        (0, 64, 3, 0, node_scale),
        (64, 64, 3, FEAT, node_scale),
        (128, 64, 4, 0, node_scale),
        (OUT_ROW, 64, 2, 0, edge_scale),
        (EDGE_ROW, 64, 1, 0, edge_scale),
        (RECV_ROW, 64, 1, 2 * FEAT, edge_scale),
        (COARSE_ROW, 81, 0, 0, 1.0),
        (SEND_ROW, 64, 1, FEAT, edge_scale),
    ]
    any_spec = pl.BlockSpec(memory_space=pl.ANY)
    sizes = (COARSE, 3 * FEAT, FEAT, 2 * FEAT, FEAT)
    sem = pltpu.SemaphoreType.DMA((len(pieces),))
    return pl.pallas_call(
        functools.partial(finish_kernel, pieces),
        out_shape=[f32_out(size, FEAT) for size in sizes + (EDGE, FINE)],
        in_specs=vmem_specs(1) + [any_spec] * 2,
        out_specs=[any_spec] * 7,
        scratch_shapes=[pltpu.VMEM((size, FEAT), F32) for size in sizes] + [sem, pltpu.SemaphoreType.DMA((2,))],
        compiler_params=pltpu.CompilerParams(vmem_limit_bytes=24 << 20),
    )(summed, grad_edges, grad_fine)


def per_device(
    fine_nodes,
    coarse_nodes,
    edge_feats,
    senders,
    receivers,
    send_rows,
    w_edge_in,
    w_edge_out,
    w_node_in,
    w_node_out,
    cot_fine,
    cot_coarse,
    cot_edges,
):
    peers = lax.axis_size("patch")
    send_list = send_rows.reshape(1, EDGE)
    send_at = senders.reshape(1, EDGE)
    recv_at = receivers.reshape(1, EDGE)
    half = pltpu.VMEM((EDGE, FEAT), BF16)
    index = pltpu.VMEM((EDGE, 128), jnp.int32)
    square = pltpu.VMEM((FEAT, FEAT), F32)
    chip_rows = pltpu.VMEM((CHIPS, 2, 8, FEAT), F32)
    core_rows = pltpu.VMEM((CHIPS, 8, FEAT), F32)
    sems = [pltpu.SemaphoreType.DMA] * 4
    wide = f32_out(EDGE, FEAT)
    fine_out = f32_out(FINE, FEAT)

    rows = pltpu.VMEM((EDGE, FEAT), F32)
    rep_out = f32_out(EDGE, 128)
    row_index = pltpu.VMEM((1, EDGE), jnp.int32)
    hbm = pl.BlockSpec(memory_space=pltpu.HBM)
    agg, pre, normed, scale, near = pl.pallas_call(
        front_kernel,
        out_shape=[wide, wide, wide, rep_out, wide],
        in_specs=vmem_specs(3) + [hbm] * 5,
        out_specs=vmem_specs(1) + [hbm] * 4,
        scratch_shapes=[chip_rows, chip_rows, core_rows]
        + [half] * 8
        + [index] * 2
        + [rows, pltpu.VMEM((COARSE, FEAT), F32), pltpu.VMEM((3 * FEAT, FEAT), F32), rows, square]
        + [rows, rows, pltpu.VMEM((EDGE, 128), F32), row_index]
        + [pltpu.SemaphoreType.DMA((5,)), pltpu.SemaphoreType.DMA((4,))]
        + sems,
        compiler_params=pltpu.CompilerParams(collective_id=1, has_side_effects=True, vmem_limit_bytes=FRONT_MIB << 20),
    )(send_list, send_at, recv_at, fine_nodes, w_edge_in, coarse_nodes, edge_feats, w_edge_out)
    grad_agg, direct, few_direct, node = node_step(
        agg, fine_nodes, cot_fine, coarse_nodes, cot_coarse, w_node_in, w_node_out
    )
    grad_edges, grad_fine, in_edge, edge_out, in_recv, coarse, in_send = remote_call(
        back_kernel,
        3,
        [wide, fine_out, TILES, TILES, TILES, f32_out(96, 4, 8, 128), TILES],
        [half] * 6 + [index, core_rows, chip_rows, chip_rows] + [square] * 4 + [row_index] + sems,
        BACK_MIB,
        grad_agg,
        cot_edges,
        pre,
        normed,
        scale,
        w_edge_out,
        send_at,
        recv_at,
        edge_feats,
        near,
        w_edge_in,
        send_list,
        direct,
    )
    (summed,) = remote_call(
        sum_kernel, 4, [sum_out(3)], exchange_scratch(LINKS, 3), SUM_MIB, node, edge_out, in_edge, in_recv, coarse, in_send, few_direct
    )
    edge_scale = 1.0 / math.sqrt(EDGE * peers)
    node_scale = 1.0 / math.sqrt(FINE * peers + COARSE)
    grad_coarse, grad_in, grad_out, grad_node_in, grad_node_out, grad_edges, grad_fine = finish(
        summed, grad_edges, grad_fine, edge_scale, node_scale
    )
    return grad_fine, grad_coarse, grad_edges, grad_in, grad_out, grad_node_in, grad_node_out


def solution(mesh):
    return jax.shard_map(
        per_device,
        mesh=mesh,
        in_specs=(
            P("patch", None),
            P(),
            P("patch", None),
            P("patch"),
            P("patch"),
            P("patch", None, None),
            P(),
            P(),
            P(),
            P(),
            P("patch", None),
            P(),
            P("patch", None),
        ),
        out_specs=(P("patch", None), P(), P("patch", None), P(), P(), P(), P()),
        check_vma=False,
    )
```

```python
import functools
import math

import jax
import jax.numpy as jnp
from jax import lax
from jax.experimental import pallas as pl
from jax.experimental.pallas import tpu as pltpu
from jax.sharding import PartitionSpec as P

MESH = pl.DeviceIdType.MESH
F32 = jnp.float32
BF16 = jnp.bfloat16
FEAT = 512
FINE = 256
COARSE = 642
NEAR = 1024
EDGE = 1024
BLOCK = 256
LINKS = 6
WIDE = 512
FRONT_MIB, BACK_MIB, SUM_MIB = 57, 41, 30

NN = (((1,), (0,)), ((), ()))
NT = (((1,), (1,)), ((), ()))
TN = (((0,), (0,)), ((), ()))


def split(value):
    high = value.astype(BF16)
    return high, (value - high.astype(F32)).astype(BF16)


def dot(left, right, dims=NN):
    return lax.dot_general(left, right, dims, preferred_element_type=F32)


def dot3(left, right, dims=NN):
    return dot(left[0], right[0], dims) + dot(left[0], right[1], dims) + dot(left[1], right[0], dims)


def dot2(left, right, dims=NN):
    return dot(left, right[0], dims) + dot(left, right[1], dims)


def block_at(step, size=BLOCK):
    return pl.ds(pl.multiple_of(step * size, size), size)


def pair_at(refs, rows):
    return refs[0][rows, :], refs[1][rows, :]


def put_pair(refs, rows, value):
    high, low = split(value)
    refs[0][rows, :] = high
    refs[1][rows, :] = low


def spread(index_row):
    return jnp.transpose(jnp.broadcast_to(index_row, (128, index_row.shape[1])))


def hot_rows(spread_block, first, width):
    lane = lax.broadcasted_iota(jnp.int32, (spread_block.shape[0], 128), 1)
    local = spread_block - first
    tiles = [jnp.where(local == lane + at, 1.0, 0.0).astype(BF16) for at in range(0, width, 128)]
    return jnp.concatenate(tiles, axis=1)


def hot_columns(index_row, first, height):
    row = lax.broadcasted_iota(jnp.int32, (height, index_row.shape[1]), 0) + first
    return jnp.where(row == index_row, 1.0, 0.0).astype(BF16)


def sigmoid(value):
    return 1.0 / (1.0 + jnp.exp(-value))


def mean(value):
    return jnp.sum(value, axis=1, keepdims=True) * (1.0 / FEAT)


def norm(value):
    center = value - mean(value)
    scale = lax.rsqrt(mean(center * center) + 1e-05)
    return center * scale, scale


def norm_back(grad, normed, scale):
    return scale * (grad - mean(grad) - normed * mean(grad * normed))


def put_tiles(ref, value):
    for at in range(FEAT // 128):
        ref[:, at] = value[:, at * 128 : (at + 1) * 128].reshape(-1, 8, 128)


def vmem_specs(count):
    return [pl.BlockSpec(memory_space=pltpu.VMEM)] * count


def f32_out(*shape):
    return jax.ShapeDtypeStruct(shape, F32)


def bf16_out(*shape):
    return jax.ShapeDtypeStruct(shape, BF16)


TILES = f32_out(64, 4, 8, 128)


STRIDES = (32, 8, 2)
ALL_PARTS = tuple((part % 3, part // 3) for part in range(6))
FOUR_PARTS = ALL_PARTS[:4]
GOT_CHUNKS = 127
SEM_COUNT = 24


def axis_places(device):
    return [(device // 32) % 4, (device // 8) % 4, (device // 2) % 4], device % 2


def axis_bits(place):
    return ((place + 1) // 2) % 2, place // 2


def position(device, spec):
    places, core = axis_places(device)
    first, flip = spec
    bits = axis_bits(places[first])
    spot = (core * 2 + bits[flip]) * 2 + bits[1 - flip]
    return (spot * 4 + places[(first + 1) % 3]) * 4 + places[(first + 2) % 3]


class Exchange:
    def __init__(self, specs, buf, got, out, sends, recvs):
        self.specs, self.buf, self.got, self.out, self.sends, self.recvs = specs, buf, got, out, sends, recvs
        self.me = lax.axis_index("patch")
        self.places, self.core = axis_places(self.me)
        self.mate = self.me + 1 - 2 * self.core
        self.bits = [axis_bits(place) for place in self.places]
        self.flying = {}
        self.spot = {}
        for part, (first, flip) in enumerate(specs):
            one, two = self.bits[first][flip], self.bits[first][1 - flip]
            third, fourth = self.places[(first + 1) % 3], self.places[(first + 2) % 3]
            at_core = self.core * 64
            at_one = at_core + one * 32
            at_two = at_one + two * 16
            at_three = at_two + third * 4
            self.spot[part] = dict(
                one=one, two=two, core=at_core, first=at_one, second=at_two, third=at_three, last=at_three + fourth
            )

    def signal(self):
        mates = [self.mate]
        mates += [self.peer(axis, shift) for axis in range(3) for shift in (1, 2, 3)]
        barrier = pltpu.get_barrier_semaphore()
        for mate in mates:
            pl.semaphore_signal(barrier, inc=1, device_id=(mate,), device_id_type=MESH)

    def wait_signals(self):
        pl.semaphore_wait(pltpu.get_barrier_semaphore(), 10)

    def peer(self, axis, shift):
        return self.me + ((self.places[axis] + shift) % 4 - self.places[axis]) * STRIDES[axis]

    def neighbour(self, axis, flip):
        place = self.places[axis]
        step = 3 - 2 * place if flip else 1 - 2 * (place % 2)
        return self.me + step * STRIDES[axis]

    def push(self, part, sem, src, dst, device):
        copy = pltpu.make_async_remote_copy(
            src_ref=src,
            dst_ref=dst,
            send_sem=self.sends.at[sem, part],
            recv_sem=self.recvs.at[sem, part],
            device_id=(device,),
            device_id_type=MESH,
        )
        copy.start()
        self.flying[part, sem] = copy

    def wait(self, part, *sems):
        for sem in sems:
            self.flying.pop((part, sem)).wait()

    def send_sum(self, part, sem, at, size, slot, device):
        self.push(part, sem, self.buf.at[part, pl.ds(at, size)], self.got.at[part, pl.ds(slot, size)], device)

    def add(self, part, at, size, *slots):
        total = self.buf[part, pl.ds(at, size)]
        for slot in slots:
            total += self.got[part, pl.ds(slot, size)]
        self.buf[part, pl.ds(at, size)] = total

    def send_block(self, part, sem, at, size, device):
        block = self.out.at[part, pl.ds(at, size)]
        self.push(part, sem, block, block, device)


    def start(self, part):
        spot = self.spot[part]
        other = 64 - spot["core"]
        self.send_sum(part, 0, other + (1 - spot["one"]) * 32, 32, 0, self.mate)

    def start_kept(self, part):
        spot = self.spot[part]
        other = 64 - spot["core"]
        self.send_sum(part, 1, other + spot["one"] * 32, 32, 32, self.mate)

    def reduce_first(self, part):
        spot = self.spot[part]
        first, flip = self.specs[part]
        away = spot["core"] + (1 - spot["one"]) * 32
        device = self.neighbour(first, flip)
        self.wait(part, 0)
        self.add(part, away, 32, 0)
        self.send_sum(part, 2, away + (1 - spot["two"]) * 16, 16, 64, device)
        self.send_sum(part, 3, away + spot["two"] * 16, 16, 80, device)

    def reduce_kept(self, part):
        self.wait(part, 1)
        self.add(part, self.spot[part]["first"], 32, 32)

    def reduce_second(self, part):
        spot = self.spot[part]
        first, flip = self.specs[part]
        away = spot["first"] + (1 - spot["two"]) * 16
        self.wait(part, 2)
        self.add(part, away, 16, 64)
        self.send_sum(part, 4, away, 16, 96, self.neighbour(first, 1 - flip))

    def reduce_third(self, part):
        spot = self.spot[part]
        axis = (self.specs[part][0] + 1) % 3
        self.wait(part, 3, 4)
        self.add(part, spot["second"], 16, 80, 96)
        for shift in (1, 2, 3):
            at = spot["second"] + (self.places[axis] + shift) % 4 * 4
            self.send_sum(part, 4 + shift, at, 4, 108 + 4 * shift, self.peer(axis, shift))

    def reduce_fourth(self, part):
        spot = self.spot[part]
        axis = (self.specs[part][0] + 2) % 3
        self.wait(part, 5, 6, 7)
        self.add(part, spot["third"], 4, 112, 116, 120)
        for shift in (1, 2, 3):
            at = spot["third"] + (self.places[axis] + shift) % 4
            self.send_sum(part, 7 + shift, at, 1, 123 + shift, self.peer(axis, shift))

    def reduce_last(self, part):
        self.wait(part, 8, 9, 10)
        self.add(part, self.spot[part]["last"], 1, 124, 125, 126)

    def gather_fourth(self, part):
        axis = (self.specs[part][0] + 2) % 3
        for shift in (1, 2, 3):
            self.send_block(part, 10 + shift, self.spot[part]["last"], 1, self.peer(axis, shift))

    def gather_third(self, part):
        axis = (self.specs[part][0] + 1) % 3
        self.wait(part, 11, 12, 13)
        for shift in (1, 2, 3):
            self.send_block(part, 13 + shift, self.spot[part]["third"], 4, self.peer(axis, shift))

    def gather_second(self, part):
        spot = self.spot[part]
        first, flip = self.specs[part]
        self.wait(part, 14, 15, 16)
        self.send_block(part, 17, spot["second"], 16, self.neighbour(first, 1 - flip))
        self.send_block(part, 20, spot["second"], 16, self.mate)

    def gather_first(self, part):
        spot = self.spot[part]
        first, flip = self.specs[part]
        device = self.neighbour(first, flip)
        self.wait(part, 17)
        self.send_block(part, 18, spot["first"], 16, device)
        self.send_block(part, 19, spot["first"] + 16, 16, device)
        self.send_block(part, 21, spot["first"] + (1 - spot["two"]) * 16, 16, self.mate)

    def gather_core(self, part):
        spot = self.spot[part]
        self.wait(part, 18)
        self.send_block(part, 22, spot["core"] + (1 - spot["one"]) * 32, 16, self.mate)

    def gather_rest(self, part):
        spot = self.spot[part]
        self.wait(part, 19)
        self.send_block(part, 23, spot["core"] + (1 - spot["one"]) * 32 + 16, 16, self.mate)

    def gather_last(self, part):
        self.wait(part, 20, 21, 22, 23)

    REDUCE = ("reduce_first", "reduce_kept", "reduce_second", "reduce_third", "reduce_fourth", "reduce_last")
    GATHER = ("gather_fourth", "gather_third", "gather_second", "gather_first", "gather_core", "gather_rest", "gather_last")

    def stage(self, stage, *parts):
        for part in parts:
            getattr(self, stage)(part)

    def run(self, stages, beside=()):
        beside = list(beside)
        for stage in stages:
            if beside:
                beside.pop(0)()
            self.stage(stage, *range(len(self.specs)))
        for work in beside:
            work()

    def finish_sum(self, part):
        self.reduce_last(part)
        last = pl.ds(self.spot[part]["last"], 1)
        self.out[part, last] = self.buf[part, last]
        self.gather_fourth(part)

    SUM = REDUCE[:-1] + ("finish_sum",) + GATHER[1:]


def exchange_scratch(parts, units):
    sem = pltpu.SemaphoreType.DMA((SEM_COUNT, parts))
    return [
        pltpu.VMEM((parts, 128, units, 8, 128), F32),
        pltpu.VMEM((parts, GOT_CHUNKS, units, 8, 128), F32),
        sem,
        sem,
    ]


def sum_out(units):
    return f32_out(LINKS, 128, units, 8, 128)


def remote_call(kernel, name_id, outs, scratch, limit, *args):
    return pl.pallas_call(
        kernel,
        out_shape=outs,
        in_specs=vmem_specs(len(args)),
        out_specs=vmem_specs(len(outs)),
        scratch_shapes=scratch,
        compiler_params=pltpu.CompilerParams(collective_id=name_id, has_side_effects=True, vmem_limit_bytes=limit << 20),
        cost_estimate=pl.CostEstimate(flops=int(3e10), bytes_accessed=int(3e7), transcendentals=0),
    )(*args)


def few_dot3(left, right, dims=NN):
    count = left[0].shape[0]
    both = dot(jnp.concatenate(left, axis=0), right[0], dims)
    return both[:count] + both[count:] + dot(left[0], right[1], dims)


class NodePass:
    def __init__(self, product, w_in, w_out):
        self.product, self.w_in, self.w_out = product, w_in, w_out

    def first(self, feats, agg):
        self.feats, self.agg = split(feats), split(agg)
        pre = self.product(self.feats, pair_at(self.w_in, pl.ds(0, FEAT)))
        self.pre = pre + self.product(self.agg, pair_at(self.w_in, pl.ds(FEAT, FEAT)))
        self.gate = sigmoid(self.pre)
        self.hidden = split(self.pre * self.gate)

    def second(self):
        self.normed, self.scale = norm(self.product(self.hidden, pair_at(self.w_out, pl.ds(0, FEAT))))

    def third(self, cot):
        self.tail = split(norm_back(cot, self.normed, self.scale))
        grad = self.product(self.tail, pair_at(self.w_out, pl.ds(0, FEAT)), NT)
        self.grad = split(grad * (self.gate * (1.0 + self.pre * (1.0 - self.gate))))

    def back(self, first):
        return self.product(self.grad, pair_at(self.w_in, pl.ds(first, FEAT)), NT)


def few_rows(ref, me):
    whole = COARSE // 8
    rows = ref[pl.ds(pl.multiple_of(me % whole * 8, 8), 8), :]
    rest = jnp.concatenate([ref[whole * 8 :, :], jnp.zeros((8 - COARSE % 8, FEAT), F32)], axis=0)
    return jnp.where(me < whole, rows, jnp.where(me == whole, rest, 0.0))


def node_kernel(*refs):
    agg_ref, fine_ref, cot_ref, coarse_ref, coarse_cot_ref, w_in_ref, w_out_ref = refs[:7]
    grad_agg_ref, own_ref, direct_ref, node_ref = refs[7:11]
    buf, got, sends, recvs, full, wi0, wi1, wo0, wo1, total = refs[11:]
    ring = Exchange(FOUR_PARTS, buf, got, full, sends, recvs)
    ring.signal()
    for part, spec in enumerate(FOUR_PARTS):
        for device in range(128):
            first = FINE + 8 * device
            if first < NEAR and 8 * device < COARSE:
                buf[part, position(device, spec), 0] = agg_ref[first : first + 8, part * 128 : (part + 1) * 128]
            else:
                buf[part, position(device, spec), 0] = jnp.zeros((8, 128), F32)
    ring.wait_signals()
    ring.stage("start", *range(4))
    ring.stage("start_kept", *range(4))

    wi, wo = (wi0, wi1), (wo0, wo1)
    fine = NodePass(dot3, wi, wo)
    few = NodePass(few_dot3, wi, wo)
    few_feats, few_cot = few_rows(coarse_ref, ring.me), few_rows(coarse_cot_ref, ring.me)

    def cut_weights():
        wi0[...], wi1[...] = split(w_in_ref[...])
        wo0[...], wo1[...] = split(w_out_ref[...])

    def fine_first():
        fine.first(fine_ref[...], agg_ref[:FINE, :])

    def fine_third():
        fine.third(cot_ref[...])

    def fine_back():
        own_ref[...] = cot_ref[...] + fine.back(0)

    def fine_agg():
        grad_agg_ref[:FINE, :] = fine.back(FEAT)

    ring.run(ring.REDUCE, [cut_weights, fine_first, fine.second, fine_third, fine_back, fine_agg])

    few_agg = jnp.concatenate([buf[part, ring.spot[part]["last"], 0] for part in range(4)], axis=1)
    blank = jnp.zeros((8, FEAT), F32)
    few.first(jnp.concatenate([few_feats, blank], axis=0), jnp.concatenate([few_agg, blank], axis=0))
    few.second()
    few.third(jnp.concatenate([few_cot, blank], axis=0))
    few_grad = few.back(FEAT)[:8]
    for part in range(4):
        full[part, ring.spot[part]["last"], 0] = few_grad[:, part * 128 : (part + 1) * 128]

    def few_back():
        direct = few_cot + few.back(0)[:8]
        for at in range(4):
            direct_ref[at] = direct[:, at * 128 : (at + 1) * 128]

    def weights_back(which, grad, first):
        def run():
            total[...] = dot3(getattr(fine, which), getattr(fine, grad), TN) + dot3(getattr(few, which), getattr(few, grad), TN)
            put_tiles(node_ref.at[pl.ds(first, 64)], total)

        return run

    def nothing():
        pass

    beside = [nothing, few_back]
    beside += [weights_back("feats", "grad", 0), weights_back("agg", "grad", 64), weights_back("hidden", "tail", 128)]
    ring.run(ring.GATHER, beside)
    for part, spec in enumerate(FOUR_PARTS):
        for device in range((NEAR - FINE) // 8):
            first = FINE + 8 * device
            grad_agg_ref[first : first + 8, part * 128 : (part + 1) * 128] = full[part, position(device, spec), 0]


def node_step(agg, fine, cot_fine, coarse, cot_coarse, w_in, w_out):
    half = pltpu.VMEM((2 * FEAT, FEAT), BF16)
    quarter = pltpu.VMEM((FEAT, FEAT), BF16)
    return remote_call(
        node_kernel,
        2,
        [f32_out(NEAR, FEAT), f32_out(FINE, FEAT), f32_out(4, 8, 128), f32_out(192, 4, 8, 128)],
        exchange_scratch(4, 1)
        + [pltpu.VMEM((4, 128, 1, 8, 128), F32), half, half, quarter, quarter, pltpu.VMEM((FEAT, FEAT), F32)],
        34,
        agg,
        fine,
        cot_fine,
        coarse,
        cot_coarse,
        w_in,
        w_out,
    )


CHIPS = 64


class Shuffle:
    def __init__(self, sends, recvs, core_sends, core_recvs):
        self.sends, self.recvs, self.core_sends, self.core_recvs = sends, recvs, core_sends, core_recvs
        self.me = lax.axis_index("patch")
        self.places, self.core = axis_places(self.me)
        self.chip = self.me // 2
        self.mate = self.me + 1 - 2 * self.core

    def other(self, step):
        step = step * 27 % CHIPS
        z, x, y = ((place + step // span) % 4 for place, span in zip(self.places, (16, 4, 1)))
        return z * 16 + x * 4 + y

    def each(self, run):
        def body(step, carry):
            run(self.other(step))
            return carry

        lax.fori_loop(1, CHIPS, body, 0)

    def signal(self):
        barrier = pltpu.get_barrier_semaphore()

        def run(chip):
            pl.semaphore_signal(barrier, inc=1, device_id=(chip * 2 + self.core,), device_id_type=MESH)

        self.each(run)
        pl.semaphore_signal(barrier, inc=1, device_id=(self.mate,), device_id_type=MESH)

    def wait_signals(self):
        pl.semaphore_wait(pltpu.get_barrier_semaphore(), CHIPS)

    def copy(self, src, dst, sends, recvs, device):
        return pltpu.make_async_remote_copy(
            src_ref=src, dst_ref=dst, send_sem=sends, recv_sem=recvs, device_id=(device,), device_id_type=MESH
        )

    def send_chips(self, src, dst):
        def run(chip):
            self.copy(src.at[chip], dst.at[self.chip], self.sends, self.recvs, chip * 2 + self.core).start()

        self.each(run)
        dst[self.chip] = src[self.chip]

    def wait_chips(self, src, dst):
        most = pl.ds(0, CHIPS - 1)
        self.copy(src.at[most], dst.at[most], self.sends, self.recvs, self.mate).wait()

    def core_copy(self, src, dst):
        return self.copy(src, dst, self.core_sends, self.core_recvs, self.mate)


def halo_place(senders, core):
    halo = senders - (FINE + COARSE)
    source = jnp.right_shift(halo, 3)
    kind = jnp.bitwise_and(source + core, 1)
    place = NEAR + kind * (EDGE // 2) + jnp.right_shift(source, 1) * 8 + jnp.bitwise_and(halo, 7)
    return jnp.where(halo < 0, senders, place)


def front_kernel(*refs):
    list_ref, sender_ref, recv_ref = refs[:3]
    far_in, agg_ref, far_out = refs[3:8], refs[8], refs[9:13]
    outgoing, got, from_mate, p0, p1, q0, q1, h0, h1, n0, n1, rep, recv_rep = refs[13:26]
    near_ref, coarse_ref, w_ref, edge_ref, w_out_ref, pre_ref, normed_ref, scale_ref, send_ref, loads, stores = refs[26:37]
    shuffle = Shuffle(*refs[37:])
    places = (near_ref.at[pl.ds(0, FINE)], w_ref, coarse_ref, edge_ref, w_out_ref)
    fetch = [pltpu.make_async_copy(src, dst, loads.at[at]) for at, (src, dst) in enumerate(zip(far_in, places))]
    for copy in fetch:
        copy.start()
    results = (pre_ref, normed_ref, scale_ref, near_ref)
    keep = [pltpu.make_async_copy(src, dst, stores.at[at]) for at, (src, dst) in enumerate(zip(results, far_out))]
    shuffle.signal()
    rep[...] = spread(list_ref[...])
    send_ref[...] = halo_place(sender_ref[...], shuffle.core)
    for copy in fetch[:2]:
        copy.wait()
    w_send = split(w_ref[FEAT : 2 * FEAT, :])
    own = split(dot3(split(near_ref[:FINE, :]), w_send))

    def request(at, carry):
        rows = block_at(at, WIDE)
        chips = pl.ds(at * (WIDE // 16), WIDE // 16)
        outgoing[chips] = dot2(hot_rows(rep[rows, :], 0, FINE), own).reshape(WIDE // 16, 2, 8, FEAT)
        return carry

    lax.fori_loop(0, EDGE // WIDE, request, 0)
    shuffle.wait_signals()
    shuffle.send_chips(outgoing, got)

    rep[...] = spread(send_ref[...])
    recv_rep[...] = spread(recv_ref[...])
    w_recv = split(w_ref[2 * FEAT :, :])
    whole = COARSE // 8 * 8
    for copy in fetch[2:]:
        copy.wait()
    near_ref[FINE : FINE + whole, :] = coarse_ref[:whole, :]
    near_ref[FINE + whole :, :] = jnp.zeros((NEAR - FINE - whole, FEAT), F32)
    near_ref[FINE + whole : FINE + COARSE, :] = coarse_ref[whole:, :]
    keep[3].start()

    def project(at, carry):
        rows = block_at(at, WIDE)
        feats = split(near_ref[rows, :])
        put_pair((p0, p1), rows, dot3(feats, w_send))
        put_pair((q0, q1), rows, dot3(feats, w_recv))
        return carry

    lax.fori_loop(0, NEAR // WIDE, project, 0)
    w_edge = split(w_ref[:FEAT, :])

    def near_step(at, carry):
        rows = block_at(at, WIDE)
        total = dot3(split(edge_ref[rows, :]), w_edge)
        total += dot2(hot_rows(recv_rep[rows, :], 0, NEAR), (q0[...], q1[...]))
        total += dot2(hot_rows(rep[rows, :], 0, NEAR), (p0[...], p1[...]))
        pre_ref[rows, :] = total
        return carry

    lax.fori_loop(0, EDGE // WIDE, near_step, 0)

    shuffle.wait_chips(outgoing, got)
    swap = shuffle.core_copy(got.at[:, 1 - shuffle.core], from_mate)
    swap.start()
    half = CHIPS * 8
    put_pair((h0, h1), pl.ds(0, half), got[:, shuffle.core].reshape(half, FEAT))
    w_out = split(w_out_ref[...])

    def halo_step(at, carry):
        rows = block_at(at, WIDE)
        pre_ref[rows, :] += dot2(hot_rows(rep[rows, :], NEAR, half), pair_at((h0, h1), pl.ds(0, half)))
        return carry

    lax.fori_loop(0, EDGE // WIDE, halo_step, 0)
    swap.wait()
    put_pair((h0, h1), pl.ds(half, half), from_mate[...].reshape(half, FEAT))

    def edge_step(at, carry):
        rows = block_at(at, WIDE)
        pre = pre_ref[rows, :] + dot2(hot_rows(rep[rows, :], NEAR + half, half), pair_at((h0, h1), pl.ds(half, half)))
        pre_ref[rows, :] = pre
        normed, scale = norm(dot3(split(pre * sigmoid(pre)), w_out))
        normed_ref[rows, :] = normed
        scale_ref[rows, :] = jnp.broadcast_to(scale, (WIDE, 128))
        put_pair((n0, n1), rows, edge_ref[rows, :] + normed)
        return carry

    lax.fori_loop(0, EDGE // WIDE, edge_step, 0)
    for copy in keep[:3]:
        copy.start()

    def gather(at, carry):
        rows = block_at(at, WIDE)
        agg_ref[rows, :] = dot2(hot_columns(recv_ref[...], at * WIDE, WIDE), (n0[...], n1[...]))
        return carry

    lax.fori_loop(0, NEAR // WIDE, gather, 0)
    for copy in keep:
        copy.wait()


def back_kernel(*refs):
    grad_agg_ref, cot_ref, pre_ref, normed_ref, scale_ref, w_out_ref, sender_ref, recv_ref = refs[:8]
    edge_ref, near_ref, w_ref, list_ref, direct_ref = refs[8:13]
    grad_edges_ref, grad_fine_ref, in_edge_ref, out_ref, in_recv_ref, coarse_ref, in_send_ref = refs[13:20]
    t0, t1, d0, d1, a0, a1, recv_rep, for_mate, pack, back = refs[20:30]
    edge_total, tail_total, recv_total, send_total, send_ref = refs[30:35]
    shuffle = Shuffle(*refs[35:])
    shuffle.signal()
    send_ref[...] = halo_place(sender_ref[...], shuffle.core)
    recv_rep[...] = spread(recv_ref[...])
    a0[...], a1[...] = split(grad_agg_ref[...])
    w_out = split(w_out_ref[...])

    def step(at, carry):
        rows = block_at(at, WIDE)
        grad = cot_ref[rows, :] + dot2(hot_rows(recv_rep[rows, :], 0, NEAR), (a0[...], a1[...]))
        grad_edges_ref[rows, :] = grad
        tail = split(norm_back(grad, normed_ref[rows, :], scale_ref[rows, :1]))
        t0[rows, :], t1[rows, :] = tail
        pre = pre_ref[rows, :]
        gate = sigmoid(pre)
        put_pair((d0, d1), rows, dot3(tail, w_out, NT) * (gate * (1.0 + pre * (1.0 - gate))))
        return carry

    lax.fori_loop(0, EDGE // WIDE, step, 0)

    half = CHIPS * 8

    def halo_rows(first):
        rows = dot2(hot_columns(send_ref[...], NEAR + first, half), (d0[...], d1[...]))
        return rows.reshape(CHIPS, 8, FEAT)

    for_mate[...] = halo_rows(half)
    shuffle.wait_signals()
    swap = shuffle.core_copy(for_mate, pack.at[:, 1])
    swap.start()
    pack[:, 0] = halo_rows(0)
    swap.wait()
    shuffle.send_chips(pack, back)

    edge_total[...] = jnp.zeros_like(edge_total)
    tail_total[...] = jnp.zeros_like(tail_total)
    w_edge = split(w_ref[:FEAT, :])

    def weight_step(at, carry):
        rows = block_at(at)
        grad_pre = (d0[rows, :], d1[rows, :])
        grad_edges_ref[rows, :] += dot3(grad_pre, w_edge, NT)
        edge_total[...] += dot3(split(edge_ref[rows, :]), grad_pre, TN)
        pre = pre_ref[rows, :]
        tail_total[...] += dot3(split(pre * sigmoid(pre)), (t0[rows, :], t1[rows, :]), TN)
        return carry

    lax.fori_loop(0, EDGE // BLOCK, weight_step, 0)
    put_tiles(in_edge_ref, edge_total)
    put_tiles(out_ref, tail_total)
    w_send = split(w_ref[FEAT : 2 * FEAT, :])
    w_recv = split(w_ref[2 * FEAT :, :])

    def sums(at):
        grad_pre = (d0[...], d1[...])
        sent = dot2(hot_columns(send_ref[...], at * BLOCK, BLOCK), grad_pre)
        return sent, split(dot2(hot_columns(recv_ref[...], at * BLOCK, BLOCK), grad_pre))

    fine_sent, received = sums(0)
    grad_fine_ref[...] = direct_ref[...] + dot3(received, w_recv, NT)
    recv_total[...] = dot3(split(near_ref[:FINE, :]), received, TN)
    send_total[...] = jnp.zeros_like(send_total)

    def coarse_step(at, carry):
        rows = block_at(at)
        sent, received = sums(at)
        sent = split(sent)
        value = dot3(sent, w_send, NT) + dot3(received, w_recv, NT)
        put_tiles(coarse_ref.at[pl.ds((at - 1) * (BLOCK // 8), BLOCK // 8)], value)
        feats = split(near_ref[rows, :])
        recv_total[...] += dot3(feats, received, TN)
        send_total[...] += dot3(feats, sent, TN)
        return carry

    lax.fori_loop(1, NEAR // BLOCK, coarse_step, 0)
    put_tiles(in_recv_ref, recv_total)

    shuffle.wait_chips(pack, back)
    pack[:, 0] = back[:, shuffle.core]
    pack[:, 1] = back[:, 1 - shuffle.core]
    returned = split(pack[...].reshape(EDGE, FEAT))
    fine_sent = split(fine_sent + dot2(hot_columns(list_ref[...], 0, FINE), returned))
    grad_fine_ref[...] += dot3(fine_sent, w_send, NT)
    send_total[...] += dot3(split(near_ref[:FINE, :]), fine_sent, TN)
    put_tiles(in_send_ref, send_total)


OUT_ROW, EDGE_ROW, RECV_ROW, COARSE_ROW, SEND_ROW, ROWS = 192, 256, 320, 384, 480, 576


def sum_kernel(*refs):
    node_ref, out_ref, in_edge_ref, in_recv_ref, coarse_ref, in_send_ref, direct_ref = refs[:7]
    sum_ref, buf, got, sends, recvs = refs[7:]
    flat = buf.reshape(ROWS * 4, 8, 128)
    ring = Exchange(ALL_PARTS, buf, got, sum_ref, sends, recvs)
    ring.signal()
    row = 0
    for ref in (node_ref, out_ref, in_edge_ref, in_recv_ref, coarse_ref, in_send_ref):
        size = ref.shape[0]
        flat[row * 4 : (row + size) * 4] = ref[...].reshape(size * 4, 8, 128)
        if row == COARSE_ROW:
            flat[pl.ds(row * 4 + ring.me % 96 * 4, 4)] += direct_ref[...]
        row += size
        if row == SEND_ROW + 64:
            flat[row * 4 :] = jnp.zeros(((ROWS - row) * 4, 8, 128), F32)
            row = ROWS
    ring.wait_signals()
    ring.stage("start", *range(LINKS))
    ring.stage("start_kept", *range(LINKS))
    ring.run(ring.SUM)


def finish_kernel(pieces, sum_ref, edges_ref, fine_ref, coarse_ref, in_ref, out_ref, node_in_ref, node_out_ref, edges_out, fine_out, *rest):
    rows, stores, passes = rest[:-2], rest[-2], rest[-1]
    outs = (coarse_ref, in_ref, out_ref, node_in_ref, node_out_ref)
    tiles = sum_ref.reshape(ROWS, 4, 8, 128)
    puts = [
        pltpu.make_async_copy(edges_ref, edges_out, passes.at[0]),
        pltpu.make_async_copy(fine_ref, fine_out, passes.at[1]),
    ]
    for put in puts:
        put.start()
    for at, (first, count, which, to, scale) in enumerate(pieces):
        for column in range(FEAT // 128):
            lanes = slice(column * 128, (column + 1) * 128)
            whole = min(count, (outs[which].shape[0] - to) // 8)
            value = tiles[first : first + whole, column] * scale
            rows[which][to : to + whole * 8, lanes] = value.reshape(whole * 8, 128)
            if whole < count:
                rows[which][to + whole * 8 :, lanes] = tiles[first + whole, column][: COARSE - whole * 8] * scale
        src, dst = rows[which], outs[which]
        if count * 8 < src.shape[0]:
            src, dst = src.at[pl.ds(to, count * 8)], dst.at[pl.ds(to, count * 8)]
        puts.append(pltpu.make_async_copy(src, dst, stores.at[at]))
        puts[-1].start()
    for put in puts:
        put.wait()


def finish(summed, grad_edges, grad_fine, edge_scale, node_scale):
    pieces = [
        (0, 64, 3, 0, node_scale),
        (64, 64, 3, FEAT, node_scale),
        (128, 64, 4, 0, node_scale),
        (OUT_ROW, 64, 2, 0, edge_scale),
        (EDGE_ROW, 64, 1, 0, edge_scale),
        (RECV_ROW, 64, 1, 2 * FEAT, edge_scale),
        (COARSE_ROW, 81, 0, 0, 1.0),
        (SEND_ROW, 64, 1, FEAT, edge_scale),
    ]
    any_spec = pl.BlockSpec(memory_space=pl.ANY)
    sizes = (COARSE, 3 * FEAT, FEAT, 2 * FEAT, FEAT)
    sem = pltpu.SemaphoreType.DMA((len(pieces),))
    return pl.pallas_call(
        functools.partial(finish_kernel, pieces),
        out_shape=[f32_out(size, FEAT) for size in sizes + (EDGE, FINE)],
        in_specs=vmem_specs(1) + [any_spec] * 2,
        out_specs=[any_spec] * 7,
        scratch_shapes=[pltpu.VMEM((size, FEAT), F32) for size in sizes] + [sem, pltpu.SemaphoreType.DMA((2,))],
        compiler_params=pltpu.CompilerParams(vmem_limit_bytes=24 << 20),
    )(summed, grad_edges, grad_fine)


def per_device(
    fine_nodes,
    coarse_nodes,
    edge_feats,
    senders,
    receivers,
    send_rows,
    w_edge_in,
    w_edge_out,
    w_node_in,
    w_node_out,
    cot_fine,
    cot_coarse,
    cot_edges,
):
    peers = lax.axis_size("patch")
    send_list = send_rows.reshape(1, EDGE)
    send_at = senders.reshape(1, EDGE)
    recv_at = receivers.reshape(1, EDGE)
    half = pltpu.VMEM((EDGE, FEAT), BF16)
    index = pltpu.VMEM((EDGE, 128), jnp.int32)
    square = pltpu.VMEM((FEAT, FEAT), F32)
    chip_rows = pltpu.VMEM((CHIPS, 2, 8, FEAT), F32)
    core_rows = pltpu.VMEM((CHIPS, 8, FEAT), F32)
    sems = [pltpu.SemaphoreType.DMA] * 4
    wide = f32_out(EDGE, FEAT)
    fine_out = f32_out(FINE, FEAT)

    rows = pltpu.VMEM((EDGE, FEAT), F32)
    rep_out = f32_out(EDGE, 128)
    row_index = pltpu.VMEM((1, EDGE), jnp.int32)
    hbm = pl.BlockSpec(memory_space=pltpu.HBM)
    agg, pre, normed, scale, near = pl.pallas_call(
        front_kernel,
        out_shape=[wide, wide, wide, rep_out, wide],
        in_specs=vmem_specs(3) + [hbm] * 5,
        out_specs=vmem_specs(1) + [hbm] * 4,
        scratch_shapes=[chip_rows, chip_rows, core_rows]
        + [half] * 8
        + [index] * 2
        + [rows, pltpu.VMEM((COARSE, FEAT), F32), pltpu.VMEM((3 * FEAT, FEAT), F32), rows, square]
        + [rows, rows, pltpu.VMEM((EDGE, 128), F32), row_index]
        + [pltpu.SemaphoreType.DMA((5,)), pltpu.SemaphoreType.DMA((4,))]
        + sems,
        compiler_params=pltpu.CompilerParams(collective_id=1, has_side_effects=True, vmem_limit_bytes=FRONT_MIB << 20),
    )(send_list, send_at, recv_at, fine_nodes, w_edge_in, coarse_nodes, edge_feats, w_edge_out)
    grad_agg, direct, few_direct, node = node_step(
        agg, fine_nodes, cot_fine, coarse_nodes, cot_coarse, w_node_in, w_node_out
    )
    grad_edges, grad_fine, in_edge, edge_out, in_recv, coarse, in_send = remote_call(
        back_kernel,
        3,
        [wide, fine_out, TILES, TILES, TILES, f32_out(96, 4, 8, 128), TILES],
        [half] * 6 + [index, core_rows, chip_rows, chip_rows] + [square] * 4 + [row_index] + sems,
        BACK_MIB,
        grad_agg,
        cot_edges,
        pre,
        normed,
        scale,
        w_edge_out,
        send_at,
        recv_at,
        edge_feats,
        near,
        w_edge_in,
        send_list,
        direct,
    )
    (summed,) = remote_call(
        sum_kernel, 4, [sum_out(3)], exchange_scratch(LINKS, 3), SUM_MIB, node, edge_out, in_edge, in_recv, coarse, in_send, few_direct
    )
    edge_scale = 1.0 / math.sqrt(EDGE * peers)
    node_scale = 1.0 / math.sqrt(FINE * peers + COARSE)
    grad_coarse, grad_in, grad_out, grad_node_in, grad_node_out, grad_edges, grad_fine = finish(
        summed, grad_edges, grad_fine, edge_scale, node_scale
    )
    return grad_fine, grad_coarse, grad_edges, grad_in, grad_out, grad_node_in, grad_node_out


def solution(mesh):
    return jax.shard_map(
        per_device,
        mesh=mesh,
        in_specs=(
            P("patch", None),
            P(),
            P("patch", None),
            P("patch"),
            P("patch"),
            P("patch", None, None),
            P(),
            P(),
            P(),
            P(),
            P("patch", None),
            P(),
            P("patch", None),
        ),
        out_specs=(P("patch", None), P(), P("patch", None), P(), P(), P(), P()),
        check_vma=False,
    )
```

```python
import functools
import math

import jax
import jax.numpy as jnp
from jax import lax
from jax.experimental import pallas as pl
from jax.experimental.pallas import tpu as pltpu
from jax.sharding import PartitionSpec as P

MESH = pl.DeviceIdType.MESH
F32 = jnp.float32
BF16 = jnp.bfloat16
FEAT = 512
FINE = 256
COARSE = 642
NEAR = 1024
EDGE = 1024
BLOCK = 256
LINKS = 6
WIDE = 512
FRONT_MIB, BACK_MIB, SUM_MIB = 57, 41, 30

NN = (((1,), (0,)), ((), ()))
NT = (((1,), (1,)), ((), ()))
TN = (((0,), (0,)), ((), ()))


def split(value):
    high = value.astype(BF16)
    return high, (value - high.astype(F32)).astype(BF16)


def dot(left, right, dims=NN):
    return lax.dot_general(left, right, dims, preferred_element_type=F32)


def dot3(left, right, dims=NN):
    return dot(left[0], right[0], dims) + dot(left[0], right[1], dims) + dot(left[1], right[0], dims)


def dot2(left, right, dims=NN):
    return dot(left, right[0], dims) + dot(left, right[1], dims)


def block_at(step, size=BLOCK):
    return pl.ds(pl.multiple_of(step * size, size), size)


def pair_at(refs, rows):
    return refs[0][rows, :], refs[1][rows, :]


def put_pair(refs, rows, value):
    high, low = split(value)
    refs[0][rows, :] = high
    refs[1][rows, :] = low


def spread(index_row):
    return jnp.transpose(jnp.broadcast_to(index_row, (128, index_row.shape[1])))


def hot_rows(spread_block, first, width):
    lane = lax.broadcasted_iota(jnp.int32, (spread_block.shape[0], 128), 1)
    local = spread_block - first
    tiles = [jnp.where(local == lane + at, 1.0, 0.0).astype(BF16) for at in range(0, width, 128)]
    return jnp.concatenate(tiles, axis=1)


def hot_columns(index_row, first, height):
    row = lax.broadcasted_iota(jnp.int32, (height, index_row.shape[1]), 0) + first
    return jnp.where(row == index_row, 1.0, 0.0).astype(BF16)


def sigmoid(value):
    return 1.0 / (1.0 + jnp.exp(-value))


def mean(value):
    return jnp.sum(value, axis=1, keepdims=True) * (1.0 / FEAT)


def norm(value):
    center = value - mean(value)
    scale = lax.rsqrt(mean(center * center) + 1e-05)
    return center * scale, scale


def norm_back(grad, normed, scale):
    return scale * (grad - mean(grad) - normed * mean(grad * normed))


def put_tiles(ref, value):
    for at in range(FEAT // 128):
        ref[:, at] = value[:, at * 128 : (at + 1) * 128].reshape(-1, 8, 128)


def vmem_specs(count):
    return [pl.BlockSpec(memory_space=pltpu.VMEM)] * count


def f32_out(*shape):
    return jax.ShapeDtypeStruct(shape, F32)


def bf16_out(*shape):
    return jax.ShapeDtypeStruct(shape, BF16)


TILES = f32_out(64, 4, 8, 128)


STRIDES = (32, 8, 2)
ALL_PARTS = tuple((part % 3, part // 3) for part in range(6))
FOUR_PARTS = ALL_PARTS[:4]
GOT_CHUNKS = 127
SEM_COUNT = 24


def axis_places(device):
    return [(device // 32) % 4, (device // 8) % 4, (device // 2) % 4], device % 2


def axis_bits(place):
    return ((place + 1) // 2) % 2, place // 2


def position(device, spec):
    places, core = axis_places(device)
    first, flip = spec
    bits = axis_bits(places[first])
    spot = (core * 2 + bits[flip]) * 2 + bits[1 - flip]
    return (spot * 4 + places[(first + 1) % 3]) * 4 + places[(first + 2) % 3]


class Exchange:
    def __init__(self, specs, buf, got, out, sends, recvs):
        self.specs, self.buf, self.got, self.out, self.sends, self.recvs = specs, buf, got, out, sends, recvs
        self.me = lax.axis_index("patch")
        self.places, self.core = axis_places(self.me)
        self.mate = self.me + 1 - 2 * self.core
        self.bits = [axis_bits(place) for place in self.places]
        self.flying = {}
        self.spot = {}
        for part, (first, flip) in enumerate(specs):
            one, two = self.bits[first][flip], self.bits[first][1 - flip]
            third, fourth = self.places[(first + 1) % 3], self.places[(first + 2) % 3]
            at_core = self.core * 64
            at_one = at_core + one * 32
            at_two = at_one + two * 16
            at_three = at_two + third * 4
            self.spot[part] = dict(
                one=one, two=two, core=at_core, first=at_one, second=at_two, third=at_three, last=at_three + fourth
            )

    def signal(self):
        mates = [self.mate]
        mates += [self.peer(axis, shift) for axis in range(3) for shift in (1, 2, 3)]
        barrier = pltpu.get_barrier_semaphore()
        for mate in mates:
            pl.semaphore_signal(barrier, inc=1, device_id=(mate,), device_id_type=MESH)

    def wait_signals(self):
        pl.semaphore_wait(pltpu.get_barrier_semaphore(), 10)

    def peer(self, axis, shift):
        return self.me + ((self.places[axis] + shift) % 4 - self.places[axis]) * STRIDES[axis]

    def neighbour(self, axis, flip):
        place = self.places[axis]
        step = 3 - 2 * place if flip else 1 - 2 * (place % 2)
        return self.me + step * STRIDES[axis]

    def push(self, part, sem, src, dst, device):
        copy = pltpu.make_async_remote_copy(
            src_ref=src,
            dst_ref=dst,
            send_sem=self.sends.at[sem, part],
            recv_sem=self.recvs.at[sem, part],
            device_id=(device,),
            device_id_type=MESH,
        )
        copy.start()
        self.flying[part, sem] = copy

    def wait(self, part, *sems):
        for sem in sems:
            self.flying.pop((part, sem)).wait()

    def send_sum(self, part, sem, at, size, slot, device):
        self.push(part, sem, self.buf.at[part, pl.ds(at, size)], self.got.at[part, pl.ds(slot, size)], device)

    def add(self, part, at, size, *slots):
        total = self.buf[part, pl.ds(at, size)]
        for slot in slots:
            total += self.got[part, pl.ds(slot, size)]
        self.buf[part, pl.ds(at, size)] = total

    def send_block(self, part, sem, at, size, device):
        block = self.out.at[part, pl.ds(at, size)]
        self.push(part, sem, block, block, device)


    def start(self, part):
        spot = self.spot[part]
        other = 64 - spot["core"]
        self.send_sum(part, 0, other + (1 - spot["one"]) * 32, 32, 0, self.mate)

    def start_kept(self, part):
        spot = self.spot[part]
        other = 64 - spot["core"]
        self.send_sum(part, 1, other + spot["one"] * 32, 32, 32, self.mate)

    def reduce_first(self, part):
        spot = self.spot[part]
        first, flip = self.specs[part]
        away = spot["core"] + (1 - spot["one"]) * 32
        device = self.neighbour(first, flip)
        self.wait(part, 0)
        self.add(part, away, 32, 0)
        self.send_sum(part, 2, away + (1 - spot["two"]) * 16, 16, 64, device)
        self.send_sum(part, 3, away + spot["two"] * 16, 16, 80, device)
        self.start_kept(part)

    def reduce_kept(self, part):
        self.wait(part, 1)
        self.add(part, self.spot[part]["first"], 32, 32)

    def reduce_second(self, part):
        spot = self.spot[part]
        first, flip = self.specs[part]
        away = spot["first"] + (1 - spot["two"]) * 16
        self.wait(part, 2)
        self.add(part, away, 16, 64)
        self.send_sum(part, 4, away, 16, 96, self.neighbour(first, 1 - flip))

    def reduce_third(self, part):
        spot = self.spot[part]
        axis = (self.specs[part][0] + 1) % 3
        self.wait(part, 3, 4)
        self.add(part, spot["second"], 16, 80, 96)
        for shift in (1, 2, 3):
            at = spot["second"] + (self.places[axis] + shift) % 4 * 4
            self.send_sum(part, 4 + shift, at, 4, 108 + 4 * shift, self.peer(axis, shift))

    def reduce_fourth(self, part):
        spot = self.spot[part]
        axis = (self.specs[part][0] + 2) % 3
        self.wait(part, 5, 6, 7)
        self.add(part, spot["third"], 4, 112, 116, 120)
        for shift in (1, 2, 3):
            at = spot["third"] + (self.places[axis] + shift) % 4
            self.send_sum(part, 7 + shift, at, 1, 123 + shift, self.peer(axis, shift))

    def reduce_last(self, part):
        self.wait(part, 8, 9, 10)
        self.add(part, self.spot[part]["last"], 1, 124, 125, 126)

    def gather_fourth(self, part):
        axis = (self.specs[part][0] + 2) % 3
        for shift in (1, 2, 3):
            self.send_block(part, 10 + shift, self.spot[part]["last"], 1, self.peer(axis, shift))

    def gather_third(self, part):
        axis = (self.specs[part][0] + 1) % 3
        self.wait(part, 11, 12, 13)
        for shift in (1, 2, 3):
            self.send_block(part, 13 + shift, self.spot[part]["third"], 4, self.peer(axis, shift))

    def gather_second(self, part):
        spot = self.spot[part]
        first, flip = self.specs[part]
        self.wait(part, 14, 15, 16)
        self.send_block(part, 17, spot["second"], 16, self.neighbour(first, 1 - flip))
        self.send_block(part, 20, spot["second"], 16, self.mate)

    def gather_first(self, part):
        spot = self.spot[part]
        first, flip = self.specs[part]
        device = self.neighbour(first, flip)
        self.wait(part, 17)
        self.send_block(part, 18, spot["first"], 16, device)
        self.send_block(part, 19, spot["first"] + 16, 16, device)
        self.send_block(part, 21, spot["first"] + (1 - spot["two"]) * 16, 16, self.mate)

    def gather_core(self, part):
        spot = self.spot[part]
        self.wait(part, 18)
        self.send_block(part, 22, spot["core"] + (1 - spot["one"]) * 32, 16, self.mate)

    def gather_rest(self, part):
        spot = self.spot[part]
        self.wait(part, 19)
        self.send_block(part, 23, spot["core"] + (1 - spot["one"]) * 32 + 16, 16, self.mate)

    def gather_last(self, part):
        self.wait(part, 20, 21, 22, 23)

    REDUCE = ("reduce_first", "reduce_kept", "reduce_second", "reduce_third", "reduce_fourth", "reduce_last")
    GATHER = ("gather_fourth", "gather_third", "gather_second", "gather_first", "gather_core", "gather_rest", "gather_last")

    def stage(self, stage, *parts):
        for part in parts:
            getattr(self, stage)(part)

    def run(self, stages, beside=()):
        beside = list(beside)
        for stage in stages:
            if beside:
                beside.pop(0)()
            self.stage(stage, *range(len(self.specs)))
        for work in beside:
            work()

    def finish_sum(self, part):
        self.reduce_last(part)
        last = pl.ds(self.spot[part]["last"], 1)
        self.out[part, last] = self.buf[part, last]
        self.gather_fourth(part)

    SUM = REDUCE[:-1] + ("finish_sum",) + GATHER[1:]


def exchange_scratch(parts, units):
    sem = pltpu.SemaphoreType.DMA((SEM_COUNT, parts))
    return [
        pltpu.VMEM((parts, 128, units, 8, 128), F32),
        pltpu.VMEM((parts, GOT_CHUNKS, units, 8, 128), F32),
        sem,
        sem,
    ]


def sum_out(units):
    return f32_out(LINKS, 128, units, 8, 128)


def remote_call(kernel, name_id, outs, scratch, limit, *args):
    return pl.pallas_call(
        kernel,
        out_shape=outs,
        in_specs=vmem_specs(len(args)),
        out_specs=vmem_specs(len(outs)),
        scratch_shapes=scratch,
        compiler_params=pltpu.CompilerParams(collective_id=name_id, has_side_effects=True, vmem_limit_bytes=limit << 20),
        cost_estimate=pl.CostEstimate(flops=int(3e10), bytes_accessed=int(3e7), transcendentals=0),
    )(*args)


def few_dot3(left, right, dims=NN):
    count = left[0].shape[0]
    both = dot(jnp.concatenate(left, axis=0), right[0], dims)
    return both[:count] + both[count:] + dot(left[0], right[1], dims)


class NodePass:
    def __init__(self, product, w_in, w_out):
        self.product, self.w_in, self.w_out = product, w_in, w_out

    def first(self, feats, agg):
        self.feats, self.agg = split(feats), split(agg)
        pre = self.product(self.feats, pair_at(self.w_in, pl.ds(0, FEAT)))
        self.pre = pre + self.product(self.agg, pair_at(self.w_in, pl.ds(FEAT, FEAT)))
        self.gate = sigmoid(self.pre)
        self.hidden = split(self.pre * self.gate)

    def second(self):
        self.normed, self.scale = norm(self.product(self.hidden, pair_at(self.w_out, pl.ds(0, FEAT))))

    def third(self, cot):
        self.tail = split(norm_back(cot, self.normed, self.scale))
        grad = self.product(self.tail, pair_at(self.w_out, pl.ds(0, FEAT)), NT)
        self.grad = split(grad * (self.gate * (1.0 + self.pre * (1.0 - self.gate))))

    def back(self, first):
        return self.product(self.grad, pair_at(self.w_in, pl.ds(first, FEAT)), NT)


def few_rows(ref, me):
    whole = COARSE // 8
    rows = ref[pl.ds(pl.multiple_of(me % whole * 8, 8), 8), :]
    rest = jnp.concatenate([ref[whole * 8 :, :], jnp.zeros((8 - COARSE % 8, FEAT), F32)], axis=0)
    return jnp.where(me < whole, rows, jnp.where(me == whole, rest, 0.0))


def node_kernel(*refs):
    agg_ref, fine_ref, cot_ref, coarse_ref, coarse_cot_ref, w_in_ref, w_out_ref = refs[:7]
    grad_agg_ref, own_ref, direct_ref, node_ref = refs[7:11]
    buf, got, sends, recvs, full, wi0, wi1, wo0, wo1, total = refs[11:]
    ring = Exchange(FOUR_PARTS, buf, got, full, sends, recvs)
    ring.signal()
    for part, spec in enumerate(FOUR_PARTS):
        for device in range(128):
            first = FINE + 8 * device
            if first < NEAR and 8 * device < COARSE:
                buf[part, position(device, spec), 0] = agg_ref[first : first + 8, part * 128 : (part + 1) * 128]
            else:
                buf[part, position(device, spec), 0] = jnp.zeros((8, 128), F32)
    ring.wait_signals()
    ring.stage("start", *range(4))

    wi, wo = (wi0, wi1), (wo0, wo1)
    fine = NodePass(dot3, wi, wo)
    few = NodePass(few_dot3, wi, wo)
    few_feats, few_cot = few_rows(coarse_ref, ring.me), few_rows(coarse_cot_ref, ring.me)

    def cut_weights():
        wi0[...], wi1[...] = split(w_in_ref[...])
        wo0[...], wo1[...] = split(w_out_ref[...])

    def fine_first():
        fine.first(fine_ref[...], agg_ref[:FINE, :])

    def fine_third():
        fine.third(cot_ref[...])

    def fine_back():
        own_ref[...] = cot_ref[...] + fine.back(0)

    def fine_agg():
        grad_agg_ref[:FINE, :] = fine.back(FEAT)

    ring.run(ring.REDUCE, [cut_weights, fine_first, fine.second, fine_third, fine_back, fine_agg])

    few_agg = jnp.concatenate([buf[part, ring.spot[part]["last"], 0] for part in range(4)], axis=1)
    blank = jnp.zeros((8, FEAT), F32)
    few.first(jnp.concatenate([few_feats, blank], axis=0), jnp.concatenate([few_agg, blank], axis=0))
    few.second()
    few.third(jnp.concatenate([few_cot, blank], axis=0))
    few_grad = few.back(FEAT)[:8]
    for part in range(4):
        full[part, ring.spot[part]["last"], 0] = few_grad[:, part * 128 : (part + 1) * 128]

    def few_back():
        direct = few_cot + few.back(0)[:8]
        for at in range(4):
            direct_ref[at] = direct[:, at * 128 : (at + 1) * 128]

    def weights_back(which, grad, first):
        def run():
            total[...] = dot3(getattr(fine, which), getattr(fine, grad), TN) + dot3(getattr(few, which), getattr(few, grad), TN)
            put_tiles(node_ref.at[pl.ds(first, 64)], total)

        return run

    def nothing():
        pass

    beside = [nothing, few_back]
    beside += [weights_back("feats", "grad", 0), weights_back("agg", "grad", 64), weights_back("hidden", "tail", 128)]
    ring.run(ring.GATHER, beside)
    for part, spec in enumerate(FOUR_PARTS):
        for device in range((NEAR - FINE) // 8):
            first = FINE + 8 * device
            grad_agg_ref[first : first + 8, part * 128 : (part + 1) * 128] = full[part, position(device, spec), 0]


def node_step(agg, fine, cot_fine, coarse, cot_coarse, w_in, w_out):
    half = pltpu.VMEM((2 * FEAT, FEAT), BF16)
    quarter = pltpu.VMEM((FEAT, FEAT), BF16)
    return remote_call(
        node_kernel,
        2,
        [f32_out(NEAR, FEAT), f32_out(FINE, FEAT), f32_out(4, 8, 128), f32_out(192, 4, 8, 128)],
        exchange_scratch(4, 1)
        + [pltpu.VMEM((4, 128, 1, 8, 128), F32), half, half, quarter, quarter, pltpu.VMEM((FEAT, FEAT), F32)],
        34,
        agg,
        fine,
        cot_fine,
        coarse,
        cot_coarse,
        w_in,
        w_out,
    )


CHIPS = 64


class Shuffle:
    def __init__(self, sends, recvs, core_sends, core_recvs):
        self.sends, self.recvs, self.core_sends, self.core_recvs = sends, recvs, core_sends, core_recvs
        self.me = lax.axis_index("patch")
        self.places, self.core = axis_places(self.me)
        self.chip = self.me // 2
        self.mate = self.me + 1 - 2 * self.core

    def other(self, step):
        step = step * 27 % CHIPS
        z, x, y = ((place + step // span) % 4 for place, span in zip(self.places, (16, 4, 1)))
        return z * 16 + x * 4 + y

    def each(self, run):
        def body(step, carry):
            run(self.other(step))
            return carry

        lax.fori_loop(1, CHIPS, body, 0)

    def signal(self):
        barrier = pltpu.get_barrier_semaphore()

        def run(chip):
            pl.semaphore_signal(barrier, inc=1, device_id=(chip * 2 + self.core,), device_id_type=MESH)

        self.each(run)
        pl.semaphore_signal(barrier, inc=1, device_id=(self.mate,), device_id_type=MESH)

    def wait_signals(self):
        pl.semaphore_wait(pltpu.get_barrier_semaphore(), CHIPS)

    def copy(self, src, dst, sends, recvs, device):
        return pltpu.make_async_remote_copy(
            src_ref=src, dst_ref=dst, send_sem=sends, recv_sem=recvs, device_id=(device,), device_id_type=MESH
        )

    def send_chips(self, src, dst):
        def run(chip):
            self.copy(src.at[chip], dst.at[self.chip], self.sends, self.recvs, chip * 2 + self.core).start()

        self.each(run)
        dst[self.chip] = src[self.chip]

    def wait_chips(self, src, dst):
        most = pl.ds(0, CHIPS - 1)
        self.copy(src.at[most], dst.at[most], self.sends, self.recvs, self.mate).wait()

    def core_copy(self, src, dst):
        return self.copy(src, dst, self.core_sends, self.core_recvs, self.mate)


def halo_place(senders, core):
    halo = senders - (FINE + COARSE)
    source = jnp.right_shift(halo, 3)
    kind = jnp.bitwise_and(source + core, 1)
    place = NEAR + kind * (EDGE // 2) + jnp.right_shift(source, 1) * 8 + jnp.bitwise_and(halo, 7)
    return jnp.where(halo < 0, senders, place)


def front_kernel(*refs):
    list_ref, sender_ref, recv_ref = refs[:3]
    far_in, agg_ref, far_out = refs[3:8], refs[8], refs[9:13]
    outgoing, got, from_mate, p0, p1, q0, q1, h0, h1, n0, n1, rep, recv_rep = refs[13:26]
    near_ref, coarse_ref, w_ref, edge_ref, w_out_ref, pre_ref, normed_ref, scale_ref, send_ref, loads, stores = refs[26:37]
    shuffle = Shuffle(*refs[37:])
    places = (near_ref.at[pl.ds(0, FINE)], w_ref, coarse_ref, edge_ref, w_out_ref)
    fetch = [pltpu.make_async_copy(src, dst, loads.at[at]) for at, (src, dst) in enumerate(zip(far_in, places))]
    for copy in fetch:
        copy.start()
    results = (pre_ref, normed_ref, scale_ref, near_ref)
    keep = [pltpu.make_async_copy(src, dst, stores.at[at]) for at, (src, dst) in enumerate(zip(results, far_out))]
    shuffle.signal()
    rep[...] = spread(list_ref[...])
    send_ref[...] = halo_place(sender_ref[...], shuffle.core)
    for copy in fetch[:2]:
        copy.wait()
    w_send = split(w_ref[FEAT : 2 * FEAT, :])
    own = split(dot3(split(near_ref[:FINE, :]), w_send))

    def request(at, carry):
        rows = block_at(at, WIDE)
        chips = pl.ds(at * (WIDE // 16), WIDE // 16)
        outgoing[chips] = dot2(hot_rows(rep[rows, :], 0, FINE), own).reshape(WIDE // 16, 2, 8, FEAT)
        return carry

    lax.fori_loop(0, EDGE // WIDE, request, 0)
    shuffle.wait_signals()
    shuffle.send_chips(outgoing, got)

    rep[...] = spread(send_ref[...])
    recv_rep[...] = spread(recv_ref[...])
    w_recv = split(w_ref[2 * FEAT :, :])
    whole = COARSE // 8 * 8
    for copy in fetch[2:]:
        copy.wait()
    near_ref[FINE : FINE + whole, :] = coarse_ref[:whole, :]
    near_ref[FINE + whole :, :] = jnp.zeros((NEAR - FINE - whole, FEAT), F32)
    near_ref[FINE + whole : FINE + COARSE, :] = coarse_ref[whole:, :]
    keep[3].start()

    def project(at, carry):
        rows = block_at(at, WIDE)
        feats = split(near_ref[rows, :])
        put_pair((p0, p1), rows, dot3(feats, w_send))
        put_pair((q0, q1), rows, dot3(feats, w_recv))
        return carry

    lax.fori_loop(0, NEAR // WIDE, project, 0)
    w_edge = split(w_ref[:FEAT, :])

    def near_step(at, carry):
        rows = block_at(at, WIDE)
        total = dot3(split(edge_ref[rows, :]), w_edge)
        total += dot2(hot_rows(recv_rep[rows, :], 0, NEAR), (q0[...], q1[...]))
        total += dot2(hot_rows(rep[rows, :], 0, NEAR), (p0[...], p1[...]))
        pre_ref[rows, :] = total
        return carry

    lax.fori_loop(0, EDGE // WIDE, near_step, 0)

    shuffle.wait_chips(outgoing, got)
    swap = shuffle.core_copy(got.at[:, 1 - shuffle.core], from_mate)
    swap.start()
    half = CHIPS * 8
    put_pair((h0, h1), pl.ds(0, half), got[:, shuffle.core].reshape(half, FEAT))
    w_out = split(w_out_ref[...])

    def halo_step(at, carry):
        rows = block_at(at, WIDE)
        pre_ref[rows, :] += dot2(hot_rows(rep[rows, :], NEAR, half), pair_at((h0, h1), pl.ds(0, half)))
        return carry

    lax.fori_loop(0, EDGE // WIDE, halo_step, 0)
    swap.wait()
    put_pair((h0, h1), pl.ds(half, half), from_mate[...].reshape(half, FEAT))

    def edge_step(at, carry):
        rows = block_at(at, WIDE)
        pre = pre_ref[rows, :] + dot2(hot_rows(rep[rows, :], NEAR + half, half), pair_at((h0, h1), pl.ds(half, half)))
        pre_ref[rows, :] = pre
        normed, scale = norm(dot3(split(pre * sigmoid(pre)), w_out))
        normed_ref[rows, :] = normed
        scale_ref[rows, :] = jnp.broadcast_to(scale, (WIDE, 128))
        put_pair((n0, n1), rows, edge_ref[rows, :] + normed)
        return carry

    lax.fori_loop(0, EDGE // WIDE, edge_step, 0)
    for copy in keep[:3]:
        copy.start()

    def gather(at, carry):
        rows = block_at(at, WIDE)
        agg_ref[rows, :] = dot2(hot_columns(recv_ref[...], at * WIDE, WIDE), (n0[...], n1[...]))
        return carry

    lax.fori_loop(0, NEAR // WIDE, gather, 0)
    for copy in keep:
        copy.wait()


def back_kernel(*refs):
    grad_agg_ref, cot_ref, pre_ref, normed_ref, scale_ref, w_out_ref, sender_ref, recv_ref = refs[:8]
    edge_ref, near_ref, w_ref, list_ref, direct_ref = refs[8:13]
    grad_edges_ref, grad_fine_ref, in_edge_ref, out_ref, in_recv_ref, coarse_ref, in_send_ref = refs[13:20]
    t0, t1, d0, d1, a0, a1, recv_rep, for_mate, pack, back = refs[20:30]
    edge_total, tail_total, recv_total, send_total, send_ref = refs[30:35]
    shuffle = Shuffle(*refs[35:])
    shuffle.signal()
    send_ref[...] = halo_place(sender_ref[...], shuffle.core)
    recv_rep[...] = spread(recv_ref[...])
    a0[...], a1[...] = split(grad_agg_ref[...])
    w_out = split(w_out_ref[...])

    def step(at, carry):
        rows = block_at(at, WIDE)
        grad = cot_ref[rows, :] + dot2(hot_rows(recv_rep[rows, :], 0, NEAR), (a0[...], a1[...]))
        grad_edges_ref[rows, :] = grad
        tail = split(norm_back(grad, normed_ref[rows, :], scale_ref[rows, :1]))
        t0[rows, :], t1[rows, :] = tail
        pre = pre_ref[rows, :]
        gate = sigmoid(pre)
        put_pair((d0, d1), rows, dot3(tail, w_out, NT) * (gate * (1.0 + pre * (1.0 - gate))))
        return carry

    lax.fori_loop(0, EDGE // WIDE, step, 0)

    half = CHIPS * 8

    def halo_rows(first):
        rows = dot2(hot_columns(send_ref[...], NEAR + first, half), (d0[...], d1[...]))
        return rows.reshape(CHIPS, 8, FEAT)

    for_mate[...] = halo_rows(half)
    shuffle.wait_signals()
    swap = shuffle.core_copy(for_mate, pack.at[:, 1])
    swap.start()
    pack[:, 0] = halo_rows(0)
    swap.wait()
    shuffle.send_chips(pack, back)

    edge_total[...] = jnp.zeros_like(edge_total)
    tail_total[...] = jnp.zeros_like(tail_total)
    w_edge = split(w_ref[:FEAT, :])

    def weight_step(at, carry):
        rows = block_at(at)
        grad_pre = (d0[rows, :], d1[rows, :])
        grad_edges_ref[rows, :] += dot3(grad_pre, w_edge, NT)
        edge_total[...] += dot3(split(edge_ref[rows, :]), grad_pre, TN)
        pre = pre_ref[rows, :]
        tail_total[...] += dot3(split(pre * sigmoid(pre)), (t0[rows, :], t1[rows, :]), TN)
        return carry

    lax.fori_loop(0, EDGE // BLOCK, weight_step, 0)
    put_tiles(in_edge_ref, edge_total)
    put_tiles(out_ref, tail_total)
    w_send = split(w_ref[FEAT : 2 * FEAT, :])
    w_recv = split(w_ref[2 * FEAT :, :])

    def sums(at):
        grad_pre = (d0[...], d1[...])
        sent = dot2(hot_columns(send_ref[...], at * BLOCK, BLOCK), grad_pre)
        return sent, split(dot2(hot_columns(recv_ref[...], at * BLOCK, BLOCK), grad_pre))

    fine_sent, received = sums(0)
    grad_fine_ref[...] = direct_ref[...] + dot3(received, w_recv, NT)
    recv_total[...] = dot3(split(near_ref[:FINE, :]), received, TN)
    send_total[...] = jnp.zeros_like(send_total)

    def coarse_step(at, carry):
        rows = block_at(at)
        sent, received = sums(at)
        sent = split(sent)
        value = dot3(sent, w_send, NT) + dot3(received, w_recv, NT)
        put_tiles(coarse_ref.at[pl.ds((at - 1) * (BLOCK // 8), BLOCK // 8)], value)
        feats = split(near_ref[rows, :])
        recv_total[...] += dot3(feats, received, TN)
        send_total[...] += dot3(feats, sent, TN)
        return carry

    lax.fori_loop(1, NEAR // BLOCK, coarse_step, 0)
    put_tiles(in_recv_ref, recv_total)

    shuffle.wait_chips(pack, back)
    pack[:, 0] = back[:, shuffle.core]
    pack[:, 1] = back[:, 1 - shuffle.core]
    returned = split(pack[...].reshape(EDGE, FEAT))
    fine_sent = split(fine_sent + dot2(hot_columns(list_ref[...], 0, FINE), returned))
    grad_fine_ref[...] += dot3(fine_sent, w_send, NT)
    send_total[...] += dot3(split(near_ref[:FINE, :]), fine_sent, TN)
    put_tiles(in_send_ref, send_total)


OUT_ROW, EDGE_ROW, RECV_ROW, COARSE_ROW, SEND_ROW, ROWS = 192, 256, 320, 384, 480, 576


def sum_kernel(*refs):
    node_ref, out_ref, in_edge_ref, in_recv_ref, coarse_ref, in_send_ref, direct_ref = refs[:7]
    sum_ref, buf, got, sends, recvs = refs[7:]
    flat = buf.reshape(ROWS * 4, 8, 128)
    ring = Exchange(ALL_PARTS, buf, got, sum_ref, sends, recvs)
    ring.signal()
    row = 0
    for ref in (node_ref, out_ref, in_edge_ref, in_recv_ref, coarse_ref, in_send_ref):
        size = ref.shape[0]
        flat[row * 4 : (row + size) * 4] = ref[...].reshape(size * 4, 8, 128)
        if row == COARSE_ROW:
            flat[pl.ds(row * 4 + ring.me % 96 * 4, 4)] += direct_ref[...]
        row += size
        if row == SEND_ROW + 64:
            flat[row * 4 :] = jnp.zeros(((ROWS - row) * 4, 8, 128), F32)
            row = ROWS
    ring.wait_signals()
    ring.stage("start", *range(LINKS))
    ring.run(ring.SUM)


def finish_kernel(pieces, sum_ref, edges_ref, fine_ref, coarse_ref, in_ref, out_ref, node_in_ref, node_out_ref, edges_out, fine_out, *rest):
    rows, stores, passes = rest[:-2], rest[-2], rest[-1]
    outs = (coarse_ref, in_ref, out_ref, node_in_ref, node_out_ref)
    tiles = sum_ref.reshape(ROWS, 4, 8, 128)
    puts = [
        pltpu.make_async_copy(edges_ref, edges_out, passes.at[0]),
        pltpu.make_async_copy(fine_ref, fine_out, passes.at[1]),
    ]
    for put in puts:
        put.start()
    for at, (first, count, which, to, scale) in enumerate(pieces):
        for column in range(FEAT // 128):
            lanes = slice(column * 128, (column + 1) * 128)
            whole = min(count, (outs[which].shape[0] - to) // 8)
            value = tiles[first : first + whole, column] * scale
            rows[which][to : to + whole * 8, lanes] = value.reshape(whole * 8, 128)
            if whole < count:
                rows[which][to + whole * 8 :, lanes] = tiles[first + whole, column][: COARSE - whole * 8] * scale
        src, dst = rows[which], outs[which]
        if count * 8 < src.shape[0]:
            src, dst = src.at[pl.ds(to, count * 8)], dst.at[pl.ds(to, count * 8)]
        puts.append(pltpu.make_async_copy(src, dst, stores.at[at]))
        puts[-1].start()
    for put in puts:
        put.wait()


def finish(summed, grad_edges, grad_fine, edge_scale, node_scale):
    pieces = [
        (0, 64, 3, 0, node_scale),
        (64, 64, 3, FEAT, node_scale),
        (128, 64, 4, 0, node_scale),
        (OUT_ROW, 64, 2, 0, edge_scale),
        (EDGE_ROW, 64, 1, 0, edge_scale),
        (RECV_ROW, 64, 1, 2 * FEAT, edge_scale),
        (COARSE_ROW, 81, 0, 0, 1.0),
        (SEND_ROW, 64, 1, FEAT, edge_scale),
    ]
    any_spec = pl.BlockSpec(memory_space=pl.ANY)
    sizes = (COARSE, 3 * FEAT, FEAT, 2 * FEAT, FEAT)
    sem = pltpu.SemaphoreType.DMA((len(pieces),))
    return pl.pallas_call(
        functools.partial(finish_kernel, pieces),
        out_shape=[f32_out(size, FEAT) for size in sizes + (EDGE, FINE)],
        in_specs=vmem_specs(1) + [any_spec] * 2,
        out_specs=[any_spec] * 7,
        scratch_shapes=[pltpu.VMEM((size, FEAT), F32) for size in sizes] + [sem, pltpu.SemaphoreType.DMA((2,))],
        compiler_params=pltpu.CompilerParams(vmem_limit_bytes=24 << 20),
    )(summed, grad_edges, grad_fine)


def per_device(
    fine_nodes,
    coarse_nodes,
    edge_feats,
    senders,
    receivers,
    send_rows,
    w_edge_in,
    w_edge_out,
    w_node_in,
    w_node_out,
    cot_fine,
    cot_coarse,
    cot_edges,
):
    peers = lax.axis_size("patch")
    send_list = send_rows.reshape(1, EDGE)
    send_at = senders.reshape(1, EDGE)
    recv_at = receivers.reshape(1, EDGE)
    half = pltpu.VMEM((EDGE, FEAT), BF16)
    index = pltpu.VMEM((EDGE, 128), jnp.int32)
    square = pltpu.VMEM((FEAT, FEAT), F32)
    chip_rows = pltpu.VMEM((CHIPS, 2, 8, FEAT), F32)
    core_rows = pltpu.VMEM((CHIPS, 8, FEAT), F32)
    sems = [pltpu.SemaphoreType.DMA] * 4
    wide = f32_out(EDGE, FEAT)
    fine_out = f32_out(FINE, FEAT)

    rows = pltpu.VMEM((EDGE, FEAT), F32)
    rep_out = f32_out(EDGE, 128)
    row_index = pltpu.VMEM((1, EDGE), jnp.int32)
    hbm = pl.BlockSpec(memory_space=pltpu.HBM)
    agg, pre, normed, scale, near = pl.pallas_call(
        front_kernel,
        out_shape=[wide, wide, wide, rep_out, wide],
        in_specs=vmem_specs(3) + [hbm] * 5,
        out_specs=vmem_specs(1) + [hbm] * 4,
        scratch_shapes=[chip_rows, chip_rows, core_rows]
        + [half] * 8
        + [index] * 2
        + [rows, pltpu.VMEM((COARSE, FEAT), F32), pltpu.VMEM((3 * FEAT, FEAT), F32), rows, square]
        + [rows, rows, pltpu.VMEM((EDGE, 128), F32), row_index]
        + [pltpu.SemaphoreType.DMA((5,)), pltpu.SemaphoreType.DMA((4,))]
        + sems,
        compiler_params=pltpu.CompilerParams(collective_id=1, has_side_effects=True, vmem_limit_bytes=FRONT_MIB << 20),
    )(send_list, send_at, recv_at, fine_nodes, w_edge_in, coarse_nodes, edge_feats, w_edge_out)
    grad_agg, direct, few_direct, node = node_step(
        agg, fine_nodes, cot_fine, coarse_nodes, cot_coarse, w_node_in, w_node_out
    )
    grad_edges, grad_fine, in_edge, edge_out, in_recv, coarse, in_send = remote_call(
        back_kernel,
        3,
        [wide, fine_out, TILES, TILES, TILES, f32_out(96, 4, 8, 128), TILES],
        [half] * 6 + [index, core_rows, chip_rows, chip_rows] + [square] * 4 + [row_index] + sems,
        BACK_MIB,
        grad_agg,
        cot_edges,
        pre,
        normed,
        scale,
        w_edge_out,
        send_at,
        recv_at,
        edge_feats,
        near,
        w_edge_in,
        send_list,
        direct,
    )
    (summed,) = remote_call(
        sum_kernel, 4, [sum_out(3)], exchange_scratch(LINKS, 3), SUM_MIB, node, edge_out, in_edge, in_recv, coarse, in_send, few_direct
    )
    edge_scale = 1.0 / math.sqrt(EDGE * peers)
    node_scale = 1.0 / math.sqrt(FINE * peers + COARSE)
    grad_coarse, grad_in, grad_out, grad_node_in, grad_node_out, grad_edges, grad_fine = finish(
        summed, grad_edges, grad_fine, edge_scale, node_scale
    )
    return grad_fine, grad_coarse, grad_edges, grad_in, grad_out, grad_node_in, grad_node_out


def solution(mesh):
    return jax.shard_map(
        per_device,
        mesh=mesh,
        in_specs=(
            P("patch", None),
            P(),
            P("patch", None),
            P("patch"),
            P("patch"),
            P("patch", None, None),
            P(),
            P(),
            P(),
            P(),
            P("patch", None),
            P(),
            P("patch", None),
        ),
        out_specs=(P("patch", None), P(), P("patch", None), P(), P(), P(), P()),
        check_vma=False,
    )
```

```python
import functools
import math

import jax
import jax.numpy as jnp
from jax import lax
from jax.experimental import pallas as pl
from jax.experimental.pallas import tpu as pltpu
from jax.sharding import PartitionSpec as P

MESH = pl.DeviceIdType.MESH
F32 = jnp.float32
BF16 = jnp.bfloat16
FEAT = 512
FINE = 256
COARSE = 642
NEAR = 1024
EDGE = 1024
BLOCK = 256
LINKS = 6
WIDE = 512
FRONT_MIB, BACK_MIB, SUM_MIB = 57, 41, 30

NN = (((1,), (0,)), ((), ()))
NT = (((1,), (1,)), ((), ()))
TN = (((0,), (0,)), ((), ()))


def split(value):
    high = value.astype(BF16)
    return high, (value - high.astype(F32)).astype(BF16)


def dot(left, right, dims=NN):
    return lax.dot_general(left, right, dims, preferred_element_type=F32)


def dot3(left, right, dims=NN):
    return dot(left[0], right[0], dims) + dot(left[0], right[1], dims) + dot(left[1], right[0], dims)


def dot2(left, right, dims=NN):
    return dot(left, right[0], dims) + dot(left, right[1], dims)


def block_at(step, size=BLOCK):
    return pl.ds(pl.multiple_of(step * size, size), size)


def pair_at(refs, rows):
    return refs[0][rows, :], refs[1][rows, :]


def put_pair(refs, rows, value):
    high, low = split(value)
    refs[0][rows, :] = high
    refs[1][rows, :] = low


def spread(index_row):
    return jnp.transpose(jnp.broadcast_to(index_row, (128, index_row.shape[1])))


def hot_rows(spread_block, first, width):
    lane = lax.broadcasted_iota(jnp.int32, (spread_block.shape[0], 128), 1)
    local = spread_block - first
    tiles = [jnp.where(local == lane + at, 1.0, 0.0).astype(BF16) for at in range(0, width, 128)]
    return jnp.concatenate(tiles, axis=1)


def hot_columns(index_row, first, height):
    row = lax.broadcasted_iota(jnp.int32, (height, index_row.shape[1]), 0) + first
    return jnp.where(row == index_row, 1.0, 0.0).astype(BF16)


def sigmoid(value):
    return 1.0 / (1.0 + jnp.exp(-value))


def mean(value):
    return jnp.sum(value, axis=1, keepdims=True) * (1.0 / FEAT)


def norm(value):
    center = value - mean(value)
    scale = lax.rsqrt(mean(center * center) + 1e-05)
    return center * scale, scale


def norm_back(grad, normed, scale):
    return scale * (grad - mean(grad) - normed * mean(grad * normed))


def put_tiles(ref, value):
    for at in range(FEAT // 128):
        ref[:, at] = value[:, at * 128 : (at + 1) * 128].reshape(-1, 8, 128)


def vmem_specs(count):
    return [pl.BlockSpec(memory_space=pltpu.VMEM)] * count


def f32_out(*shape):
    return jax.ShapeDtypeStruct(shape, F32)


def bf16_out(*shape):
    return jax.ShapeDtypeStruct(shape, BF16)


TILES = f32_out(64, 4, 8, 128)


STRIDES = (32, 8, 2)
ALL_PARTS = tuple((part % 3, part // 3) for part in range(6))
FOUR_PARTS = ALL_PARTS[:4]
GOT_CHUNKS = 127
SEM_COUNT = 24


def axis_places(device):
    return [(device // 32) % 4, (device // 8) % 4, (device // 2) % 4], device % 2


def axis_bits(place):
    return ((place + 1) // 2) % 2, place // 2


def position(device, spec):
    places, core = axis_places(device)
    first, flip = spec
    bits = axis_bits(places[first])
    spot = (core * 2 + bits[flip]) * 2 + bits[1 - flip]
    return (spot * 4 + places[(first + 1) % 3]) * 4 + places[(first + 2) % 3]


class Exchange:
    def __init__(self, specs, buf, got, out, sends, recvs):
        self.specs, self.buf, self.got, self.out, self.sends, self.recvs = specs, buf, got, out, sends, recvs
        self.me = lax.axis_index("patch")
        self.places, self.core = axis_places(self.me)
        self.mate = self.me + 1 - 2 * self.core
        self.bits = [axis_bits(place) for place in self.places]
        self.flying = {}
        self.spot = {}
        for part, (first, flip) in enumerate(specs):
            one, two = self.bits[first][flip], self.bits[first][1 - flip]
            third, fourth = self.places[(first + 1) % 3], self.places[(first + 2) % 3]
            at_core = self.core * 64
            at_one = at_core + one * 32
            at_two = at_one + two * 16
            at_three = at_two + third * 4
            self.spot[part] = dict(
                one=one, two=two, core=at_core, first=at_one, second=at_two, third=at_three, last=at_three + fourth
            )

    def signal(self):
        mates = [self.mate]
        mates += [self.peer(axis, shift) for axis in range(3) for shift in (1, 2, 3)]
        barrier = pltpu.get_barrier_semaphore()
        for mate in mates:
            pl.semaphore_signal(barrier, inc=1, device_id=(mate,), device_id_type=MESH)

    def wait_signals(self):
        pl.semaphore_wait(pltpu.get_barrier_semaphore(), 10)

    def peer(self, axis, shift):
        return self.me + ((self.places[axis] + shift) % 4 - self.places[axis]) * STRIDES[axis]

    def neighbour(self, axis, flip):
        place = self.places[axis]
        step = 3 - 2 * place if flip else 1 - 2 * (place % 2)
        return self.me + step * STRIDES[axis]

    def push(self, part, sem, src, dst, device):
        copy = pltpu.make_async_remote_copy(
            src_ref=src,
            dst_ref=dst,
            send_sem=self.sends.at[sem, part],
            recv_sem=self.recvs.at[sem, part],
            device_id=(device,),
            device_id_type=MESH,
        )
        copy.start()
        self.flying[part, sem] = copy

    def wait(self, part, *sems):
        for sem in sems:
            self.flying.pop((part, sem)).wait()

    def send_sum(self, part, sem, at, size, slot, device):
        self.push(part, sem, self.buf.at[part, pl.ds(at, size)], self.got.at[part, pl.ds(slot, size)], device)

    def add(self, part, at, size, *slots):
        total = self.buf[part, pl.ds(at, size)]
        for slot in slots:
            total += self.got[part, pl.ds(slot, size)]
        self.buf[part, pl.ds(at, size)] = total

    def send_block(self, part, sem, at, size, device):
        block = self.out.at[part, pl.ds(at, size)]
        self.push(part, sem, block, block, device)


    def start(self, part):
        spot = self.spot[part]
        other = 64 - spot["core"]
        self.send_sum(part, 0, other + (1 - spot["one"]) * 32, 32, 0, self.mate)

    def start_kept(self, part):
        spot = self.spot[part]
        other = 64 - spot["core"]
        self.send_sum(part, 1, other + spot["one"] * 32, 32, 32, self.mate)

    def reduce_first(self, part):
        spot = self.spot[part]
        first, flip = self.specs[part]
        away = spot["core"] + (1 - spot["one"]) * 32
        device = self.neighbour(first, flip)
        self.wait(part, 0)
        self.add(part, away, 32, 0)
        self.send_sum(part, 2, away + (1 - spot["two"]) * 16, 16, 64, device)
        self.send_sum(part, 3, away + spot["two"] * 16, 16, 80, device)

    def reduce_kept(self, part):
        self.wait(part, 1)
        self.add(part, self.spot[part]["first"], 32, 32)

    def reduce_second(self, part):
        spot = self.spot[part]
        first, flip = self.specs[part]
        away = spot["first"] + (1 - spot["two"]) * 16
        self.wait(part, 2)
        self.add(part, away, 16, 64)
        self.send_sum(part, 4, away, 16, 96, self.neighbour(first, 1 - flip))

    def reduce_third(self, part):
        spot = self.spot[part]
        axis = (self.specs[part][0] + 1) % 3
        self.wait(part, 3, 4)
        self.add(part, spot["second"], 16, 80, 96)
        for shift in (2, 1, 3):
            at = spot["second"] + (self.places[axis] + shift) % 4 * 4
            self.send_sum(part, 4 + shift, at, 4, 108 + 4 * shift, self.peer(axis, shift))

    def reduce_fourth(self, part):
        spot = self.spot[part]
        axis = (self.specs[part][0] + 2) % 3
        self.wait(part, 5, 6, 7)
        self.add(part, spot["third"], 4, 112, 116, 120)
        for shift in (2, 1, 3):
            at = spot["third"] + (self.places[axis] + shift) % 4
            self.send_sum(part, 7 + shift, at, 1, 123 + shift, self.peer(axis, shift))

    def reduce_last(self, part):
        self.wait(part, 8, 9, 10)
        self.add(part, self.spot[part]["last"], 1, 124, 125, 126)

    def gather_fourth(self, part):
        axis = (self.specs[part][0] + 2) % 3
        for shift in (2, 1, 3):
            self.send_block(part, 10 + shift, self.spot[part]["last"], 1, self.peer(axis, shift))

    def gather_third(self, part):
        axis = (self.specs[part][0] + 1) % 3
        self.wait(part, 11, 12, 13)
        for shift in (2, 1, 3):
            self.send_block(part, 13 + shift, self.spot[part]["third"], 4, self.peer(axis, shift))

    def gather_second(self, part):
        spot = self.spot[part]
        first, flip = self.specs[part]
        self.wait(part, 14, 15, 16)
        self.send_block(part, 17, spot["second"], 16, self.neighbour(first, 1 - flip))
        self.send_block(part, 20, spot["second"], 16, self.mate)

    def gather_first(self, part):
        spot = self.spot[part]
        first, flip = self.specs[part]
        device = self.neighbour(first, flip)
        self.wait(part, 17)
        self.send_block(part, 18, spot["first"], 16, device)
        self.send_block(part, 19, spot["first"] + 16, 16, device)
        self.send_block(part, 21, spot["first"] + (1 - spot["two"]) * 16, 16, self.mate)

    def gather_core(self, part):
        spot = self.spot[part]
        self.wait(part, 18)
        self.send_block(part, 22, spot["core"] + (1 - spot["one"]) * 32, 16, self.mate)

    def gather_rest(self, part):
        spot = self.spot[part]
        self.wait(part, 19)
        self.send_block(part, 23, spot["core"] + (1 - spot["one"]) * 32 + 16, 16, self.mate)

    def gather_last(self, part):
        self.wait(part, 20, 21, 22, 23)

    REDUCE = ("reduce_first", "reduce_kept", "reduce_second", "reduce_third", "reduce_fourth", "reduce_last")
    GATHER = ("gather_fourth", "gather_third", "gather_second", "gather_first", "gather_core", "gather_rest", "gather_last")

    def stage(self, stage, *parts):
        for part in parts:
            getattr(self, stage)(part)

    def run(self, stages, beside=()):
        beside = list(beside)
        for stage in stages:
            if beside:
                beside.pop(0)()
            self.stage(stage, *range(len(self.specs)))
        for work in beside:
            work()

    def finish_sum(self, part):
        self.reduce_last(part)
        last = pl.ds(self.spot[part]["last"], 1)
        self.out[part, last] = self.buf[part, last]
        self.gather_fourth(part)

    SUM = REDUCE[:-1] + ("finish_sum",) + GATHER[1:]


def exchange_scratch(parts, units):
    sem = pltpu.SemaphoreType.DMA((SEM_COUNT, parts))
    return [
        pltpu.VMEM((parts, 128, units, 8, 128), F32),
        pltpu.VMEM((parts, GOT_CHUNKS, units, 8, 128), F32),
        sem,
        sem,
    ]


def sum_out(units):
    return f32_out(LINKS, 128, units, 8, 128)


def remote_call(kernel, name_id, outs, scratch, limit, *args):
    return pl.pallas_call(
        kernel,
        out_shape=outs,
        in_specs=vmem_specs(len(args)),
        out_specs=vmem_specs(len(outs)),
        scratch_shapes=scratch,
        compiler_params=pltpu.CompilerParams(collective_id=name_id, has_side_effects=True, vmem_limit_bytes=limit << 20),
        cost_estimate=pl.CostEstimate(flops=int(3e10), bytes_accessed=int(3e7), transcendentals=0),
    )(*args)


def few_dot3(left, right, dims=NN):
    count = left[0].shape[0]
    both = dot(jnp.concatenate(left, axis=0), right[0], dims)
    return both[:count] + both[count:] + dot(left[0], right[1], dims)


class NodePass:
    def __init__(self, product, w_in, w_out):
        self.product, self.w_in, self.w_out = product, w_in, w_out

    def first(self, feats, agg):
        self.feats, self.agg = split(feats), split(agg)
        pre = self.product(self.feats, pair_at(self.w_in, pl.ds(0, FEAT)))
        self.pre = pre + self.product(self.agg, pair_at(self.w_in, pl.ds(FEAT, FEAT)))
        self.gate = sigmoid(self.pre)
        self.hidden = split(self.pre * self.gate)

    def second(self):
        self.normed, self.scale = norm(self.product(self.hidden, pair_at(self.w_out, pl.ds(0, FEAT))))

    def third(self, cot):
        self.tail = split(norm_back(cot, self.normed, self.scale))
        grad = self.product(self.tail, pair_at(self.w_out, pl.ds(0, FEAT)), NT)
        self.grad = split(grad * (self.gate * (1.0 + self.pre * (1.0 - self.gate))))

    def back(self, first):
        return self.product(self.grad, pair_at(self.w_in, pl.ds(first, FEAT)), NT)


def few_rows(ref, me):
    whole = COARSE // 8
    rows = ref[pl.ds(pl.multiple_of(me % whole * 8, 8), 8), :]
    rest = jnp.concatenate([ref[whole * 8 :, :], jnp.zeros((8 - COARSE % 8, FEAT), F32)], axis=0)
    return jnp.where(me < whole, rows, jnp.where(me == whole, rest, 0.0))


def node_kernel(*refs):
    agg_ref, fine_ref, cot_ref, coarse_ref, coarse_cot_ref, w_in_ref, w_out_ref = refs[:7]
    grad_agg_ref, own_ref, direct_ref, node_ref = refs[7:11]
    buf, got, sends, recvs, full, wi0, wi1, wo0, wo1, total = refs[11:]
    ring = Exchange(FOUR_PARTS, buf, got, full, sends, recvs)
    ring.signal()
    for part, spec in enumerate(FOUR_PARTS):
        for device in range(128):
            first = FINE + 8 * device
            if first < NEAR and 8 * device < COARSE:
                buf[part, position(device, spec), 0] = agg_ref[first : first + 8, part * 128 : (part + 1) * 128]
            else:
                buf[part, position(device, spec), 0] = jnp.zeros((8, 128), F32)
    ring.wait_signals()
    ring.stage("start", *range(4))
    ring.stage("start_kept", *range(4))

    wi, wo = (wi0, wi1), (wo0, wo1)
    fine = NodePass(dot3, wi, wo)
    few = NodePass(few_dot3, wi, wo)
    few_feats, few_cot = few_rows(coarse_ref, ring.me), few_rows(coarse_cot_ref, ring.me)

    def cut_weights():
        wi0[...], wi1[...] = split(w_in_ref[...])
        wo0[...], wo1[...] = split(w_out_ref[...])

    def fine_first():
        fine.first(fine_ref[...], agg_ref[:FINE, :])

    def fine_third():
        fine.third(cot_ref[...])

    def fine_back():
        own_ref[...] = cot_ref[...] + fine.back(0)

    def fine_agg():
        grad_agg_ref[:FINE, :] = fine.back(FEAT)

    ring.run(ring.REDUCE, [cut_weights, fine_first, fine.second, fine_third, fine_back, fine_agg])

    few_agg = jnp.concatenate([buf[part, ring.spot[part]["last"], 0] for part in range(4)], axis=1)
    blank = jnp.zeros((8, FEAT), F32)
    few.first(jnp.concatenate([few_feats, blank], axis=0), jnp.concatenate([few_agg, blank], axis=0))
    few.second()
    few.third(jnp.concatenate([few_cot, blank], axis=0))
    few_grad = few.back(FEAT)[:8]
    for part in range(4):
        full[part, ring.spot[part]["last"], 0] = few_grad[:, part * 128 : (part + 1) * 128]

    def few_back():
        direct = few_cot + few.back(0)[:8]
        for at in range(4):
            direct_ref[at] = direct[:, at * 128 : (at + 1) * 128]

    def weights_back(which, grad, first):
        def run():
            total[...] = dot3(getattr(fine, which), getattr(fine, grad), TN) + dot3(getattr(few, which), getattr(few, grad), TN)
            put_tiles(node_ref.at[pl.ds(first, 64)], total)

        return run

    def nothing():
        pass

    beside = [nothing, few_back]
    beside += [weights_back("feats", "grad", 0), weights_back("agg", "grad", 64), weights_back("hidden", "tail", 128)]
    ring.run(ring.GATHER, beside)
    for part, spec in enumerate(FOUR_PARTS):
        for device in range((NEAR - FINE) // 8):
            first = FINE + 8 * device
            grad_agg_ref[first : first + 8, part * 128 : (part + 1) * 128] = full[part, position(device, spec), 0]


def node_step(agg, fine, cot_fine, coarse, cot_coarse, w_in, w_out):
    half = pltpu.VMEM((2 * FEAT, FEAT), BF16)
    quarter = pltpu.VMEM((FEAT, FEAT), BF16)
    return remote_call(
        node_kernel,
        2,
        [f32_out(NEAR, FEAT), f32_out(FINE, FEAT), f32_out(4, 8, 128), f32_out(192, 4, 8, 128)],
        exchange_scratch(4, 1)
        + [pltpu.VMEM((4, 128, 1, 8, 128), F32), half, half, quarter, quarter, pltpu.VMEM((FEAT, FEAT), F32)],
        34,
        agg,
        fine,
        cot_fine,
        coarse,
        cot_coarse,
        w_in,
        w_out,
    )


CHIPS = 64


class Shuffle:
    def __init__(self, sends, recvs, core_sends, core_recvs):
        self.sends, self.recvs, self.core_sends, self.core_recvs = sends, recvs, core_sends, core_recvs
        self.me = lax.axis_index("patch")
        self.places, self.core = axis_places(self.me)
        self.chip = self.me // 2
        self.mate = self.me + 1 - 2 * self.core

    def other(self, step):
        step = step * 27 % CHIPS
        z, x, y = ((place + step // span) % 4 for place, span in zip(self.places, (16, 4, 1)))
        return z * 16 + x * 4 + y

    def each(self, run):
        def body(step, carry):
            run(self.other(step))
            return carry

        lax.fori_loop(1, CHIPS, body, 0)

    def signal(self):
        barrier = pltpu.get_barrier_semaphore()

        def run(chip):
            pl.semaphore_signal(barrier, inc=1, device_id=(chip * 2 + self.core,), device_id_type=MESH)

        self.each(run)
        pl.semaphore_signal(barrier, inc=1, device_id=(self.mate,), device_id_type=MESH)

    def wait_signals(self):
        pl.semaphore_wait(pltpu.get_barrier_semaphore(), CHIPS)

    def copy(self, src, dst, sends, recvs, device):
        return pltpu.make_async_remote_copy(
            src_ref=src, dst_ref=dst, send_sem=sends, recv_sem=recvs, device_id=(device,), device_id_type=MESH
        )

    def send_chips(self, src, dst):
        def run(chip):
            self.copy(src.at[chip], dst.at[self.chip], self.sends, self.recvs, chip * 2 + self.core).start()

        self.each(run)
        dst[self.chip] = src[self.chip]

    def wait_chips(self, src, dst):
        most = pl.ds(0, CHIPS - 1)
        self.copy(src.at[most], dst.at[most], self.sends, self.recvs, self.mate).wait()

    def core_copy(self, src, dst):
        return self.copy(src, dst, self.core_sends, self.core_recvs, self.mate)


def halo_place(senders, core):
    halo = senders - (FINE + COARSE)
    source = jnp.right_shift(halo, 3)
    kind = jnp.bitwise_and(source + core, 1)
    place = NEAR + kind * (EDGE // 2) + jnp.right_shift(source, 1) * 8 + jnp.bitwise_and(halo, 7)
    return jnp.where(halo < 0, senders, place)


def front_kernel(*refs):
    list_ref, sender_ref, recv_ref = refs[:3]
    far_in, agg_ref, far_out = refs[3:8], refs[8], refs[9:13]
    outgoing, got, from_mate, p0, p1, q0, q1, h0, h1, n0, n1, rep, recv_rep = refs[13:26]
    near_ref, coarse_ref, w_ref, edge_ref, w_out_ref, pre_ref, normed_ref, scale_ref, send_ref, loads, stores = refs[26:37]
    shuffle = Shuffle(*refs[37:])
    places = (near_ref.at[pl.ds(0, FINE)], w_ref, coarse_ref, edge_ref, w_out_ref)
    fetch = [pltpu.make_async_copy(src, dst, loads.at[at]) for at, (src, dst) in enumerate(zip(far_in, places))]
    for copy in fetch:
        copy.start()
    results = (pre_ref, normed_ref, scale_ref, near_ref)
    keep = [pltpu.make_async_copy(src, dst, stores.at[at]) for at, (src, dst) in enumerate(zip(results, far_out))]
    shuffle.signal()
    rep[...] = spread(list_ref[...])
    send_ref[...] = halo_place(sender_ref[...], shuffle.core)
    for copy in fetch[:2]:
        copy.wait()
    w_send = split(w_ref[FEAT : 2 * FEAT, :])
    own = split(dot3(split(near_ref[:FINE, :]), w_send))

    def request(at, carry):
        rows = block_at(at, WIDE)
        chips = pl.ds(at * (WIDE // 16), WIDE // 16)
        outgoing[chips] = dot2(hot_rows(rep[rows, :], 0, FINE), own).reshape(WIDE // 16, 2, 8, FEAT)
        return carry

    lax.fori_loop(0, EDGE // WIDE, request, 0)
    shuffle.wait_signals()
    shuffle.send_chips(outgoing, got)

    rep[...] = spread(send_ref[...])
    recv_rep[...] = spread(recv_ref[...])
    w_recv = split(w_ref[2 * FEAT :, :])
    whole = COARSE // 8 * 8
    for copy in fetch[2:]:
        copy.wait()
    near_ref[FINE : FINE + whole, :] = coarse_ref[:whole, :]
    near_ref[FINE + whole :, :] = jnp.zeros((NEAR - FINE - whole, FEAT), F32)
    near_ref[FINE + whole : FINE + COARSE, :] = coarse_ref[whole:, :]
    keep[3].start()

    def project(at, carry):
        rows = block_at(at, WIDE)
        feats = split(near_ref[rows, :])
        put_pair((p0, p1), rows, dot3(feats, w_send))
        put_pair((q0, q1), rows, dot3(feats, w_recv))
        return carry

    lax.fori_loop(0, NEAR // WIDE, project, 0)
    w_edge = split(w_ref[:FEAT, :])

    def near_step(at, carry):
        rows = block_at(at, WIDE)
        total = dot3(split(edge_ref[rows, :]), w_edge)
        total += dot2(hot_rows(recv_rep[rows, :], 0, NEAR), (q0[...], q1[...]))
        total += dot2(hot_rows(rep[rows, :], 0, NEAR), (p0[...], p1[...]))
        pre_ref[rows, :] = total
        return carry

    lax.fori_loop(0, EDGE // WIDE, near_step, 0)

    shuffle.wait_chips(outgoing, got)
    swap = shuffle.core_copy(got.at[:, 1 - shuffle.core], from_mate)
    swap.start()
    half = CHIPS * 8
    put_pair((h0, h1), pl.ds(0, half), got[:, shuffle.core].reshape(half, FEAT))
    w_out = split(w_out_ref[...])

    def halo_step(at, carry):
        rows = block_at(at, WIDE)
        pre_ref[rows, :] += dot2(hot_rows(rep[rows, :], NEAR, half), pair_at((h0, h1), pl.ds(0, half)))
        return carry

    lax.fori_loop(0, EDGE // WIDE, halo_step, 0)
    swap.wait()
    put_pair((h0, h1), pl.ds(half, half), from_mate[...].reshape(half, FEAT))

    def edge_step(at, carry):
        rows = block_at(at, WIDE)
        pre = pre_ref[rows, :] + dot2(hot_rows(rep[rows, :], NEAR + half, half), pair_at((h0, h1), pl.ds(half, half)))
        pre_ref[rows, :] = pre
        normed, scale = norm(dot3(split(pre * sigmoid(pre)), w_out))
        normed_ref[rows, :] = normed
        scale_ref[rows, :] = jnp.broadcast_to(scale, (WIDE, 128))
        put_pair((n0, n1), rows, edge_ref[rows, :] + normed)
        return carry

    lax.fori_loop(0, EDGE // WIDE, edge_step, 0)
    for copy in keep[:3]:
        copy.start()

    def gather(at, carry):
        rows = block_at(at, WIDE)
        agg_ref[rows, :] = dot2(hot_columns(recv_ref[...], at * WIDE, WIDE), (n0[...], n1[...]))
        return carry

    lax.fori_loop(0, NEAR // WIDE, gather, 0)
    for copy in keep:
        copy.wait()


def back_kernel(*refs):
    grad_agg_ref, cot_ref, pre_ref, normed_ref, scale_ref, w_out_ref, sender_ref, recv_ref = refs[:8]
    edge_ref, near_ref, w_ref, list_ref, direct_ref = refs[8:13]
    grad_edges_ref, grad_fine_ref, in_edge_ref, out_ref, in_recv_ref, coarse_ref, in_send_ref = refs[13:20]
    t0, t1, d0, d1, a0, a1, recv_rep, for_mate, pack, back = refs[20:30]
    edge_total, tail_total, recv_total, send_total, send_ref = refs[30:35]
    shuffle = Shuffle(*refs[35:])
    shuffle.signal()
    send_ref[...] = halo_place(sender_ref[...], shuffle.core)
    recv_rep[...] = spread(recv_ref[...])
    a0[...], a1[...] = split(grad_agg_ref[...])
    w_out = split(w_out_ref[...])

    def step(at, carry):
        rows = block_at(at, WIDE)
        grad = cot_ref[rows, :] + dot2(hot_rows(recv_rep[rows, :], 0, NEAR), (a0[...], a1[...]))
        grad_edges_ref[rows, :] = grad
        tail = split(norm_back(grad, normed_ref[rows, :], scale_ref[rows, :1]))
        t0[rows, :], t1[rows, :] = tail
        pre = pre_ref[rows, :]
        gate = sigmoid(pre)
        put_pair((d0, d1), rows, dot3(tail, w_out, NT) * (gate * (1.0 + pre * (1.0 - gate))))
        return carry

    lax.fori_loop(0, EDGE // WIDE, step, 0)

    half = CHIPS * 8

    def halo_rows(first):
        rows = dot2(hot_columns(send_ref[...], NEAR + first, half), (d0[...], d1[...]))
        return rows.reshape(CHIPS, 8, FEAT)

    for_mate[...] = halo_rows(half)
    shuffle.wait_signals()
    swap = shuffle.core_copy(for_mate, pack.at[:, 1])
    swap.start()
    pack[:, 0] = halo_rows(0)
    swap.wait()
    shuffle.send_chips(pack, back)

    edge_total[...] = jnp.zeros_like(edge_total)
    tail_total[...] = jnp.zeros_like(tail_total)
    w_edge = split(w_ref[:FEAT, :])

    def weight_step(at, carry):
        rows = block_at(at)
        grad_pre = (d0[rows, :], d1[rows, :])
        grad_edges_ref[rows, :] += dot3(grad_pre, w_edge, NT)
        edge_total[...] += dot3(split(edge_ref[rows, :]), grad_pre, TN)
        pre = pre_ref[rows, :]
        tail_total[...] += dot3(split(pre * sigmoid(pre)), (t0[rows, :], t1[rows, :]), TN)
        return carry

    lax.fori_loop(0, EDGE // BLOCK, weight_step, 0)
    put_tiles(in_edge_ref, edge_total)
    put_tiles(out_ref, tail_total)
    w_send = split(w_ref[FEAT : 2 * FEAT, :])
    w_recv = split(w_ref[2 * FEAT :, :])

    def sums(at):
        grad_pre = (d0[...], d1[...])
        sent = dot2(hot_columns(send_ref[...], at * BLOCK, BLOCK), grad_pre)
        return sent, split(dot2(hot_columns(recv_ref[...], at * BLOCK, BLOCK), grad_pre))

    fine_sent, received = sums(0)
    grad_fine_ref[...] = direct_ref[...] + dot3(received, w_recv, NT)
    recv_total[...] = dot3(split(near_ref[:FINE, :]), received, TN)
    send_total[...] = jnp.zeros_like(send_total)

    def coarse_step(at, carry):
        rows = block_at(at)
        sent, received = sums(at)
        sent = split(sent)
        value = dot3(sent, w_send, NT) + dot3(received, w_recv, NT)
        put_tiles(coarse_ref.at[pl.ds((at - 1) * (BLOCK // 8), BLOCK // 8)], value)
        feats = split(near_ref[rows, :])
        recv_total[...] += dot3(feats, received, TN)
        send_total[...] += dot3(feats, sent, TN)
        return carry

    lax.fori_loop(1, NEAR // BLOCK, coarse_step, 0)
    put_tiles(in_recv_ref, recv_total)

    shuffle.wait_chips(pack, back)
    pack[:, 0] = back[:, shuffle.core]
    pack[:, 1] = back[:, 1 - shuffle.core]
    returned = split(pack[...].reshape(EDGE, FEAT))
    fine_sent = split(fine_sent + dot2(hot_columns(list_ref[...], 0, FINE), returned))
    grad_fine_ref[...] += dot3(fine_sent, w_send, NT)
    send_total[...] += dot3(split(near_ref[:FINE, :]), fine_sent, TN)
    put_tiles(in_send_ref, send_total)


OUT_ROW, EDGE_ROW, RECV_ROW, COARSE_ROW, SEND_ROW, ROWS = 192, 256, 320, 384, 480, 576


def sum_kernel(*refs):
    node_ref, out_ref, in_edge_ref, in_recv_ref, coarse_ref, in_send_ref, direct_ref = refs[:7]
    sum_ref, buf, got, sends, recvs = refs[7:]
    flat = buf.reshape(ROWS * 4, 8, 128)
    ring = Exchange(ALL_PARTS, buf, got, sum_ref, sends, recvs)
    ring.signal()
    row = 0
    for ref in (node_ref, out_ref, in_edge_ref, in_recv_ref, coarse_ref, in_send_ref):
        size = ref.shape[0]
        flat[row * 4 : (row + size) * 4] = ref[...].reshape(size * 4, 8, 128)
        if row == COARSE_ROW:
            flat[pl.ds(row * 4 + ring.me % 96 * 4, 4)] += direct_ref[...]
        row += size
        if row == SEND_ROW + 64:
            flat[row * 4 :] = jnp.zeros(((ROWS - row) * 4, 8, 128), F32)
            row = ROWS
    ring.wait_signals()
    ring.stage("start", *range(LINKS))
    ring.stage("start_kept", *range(LINKS))
    ring.run(ring.SUM)


def finish_kernel(pieces, sum_ref, edges_ref, fine_ref, coarse_ref, in_ref, out_ref, node_in_ref, node_out_ref, edges_out, fine_out, *rest):
    rows, stores, passes = rest[:-2], rest[-2], rest[-1]
    outs = (coarse_ref, in_ref, out_ref, node_in_ref, node_out_ref)
    tiles = sum_ref.reshape(ROWS, 4, 8, 128)
    puts = [
        pltpu.make_async_copy(edges_ref, edges_out, passes.at[0]),
        pltpu.make_async_copy(fine_ref, fine_out, passes.at[1]),
    ]
    for put in puts:
        put.start()
    for at, (first, count, which, to, scale) in enumerate(pieces):
        for column in range(FEAT // 128):
            lanes = slice(column * 128, (column + 1) * 128)
            whole = min(count, (outs[which].shape[0] - to) // 8)
            value = tiles[first : first + whole, column] * scale
            rows[which][to : to + whole * 8, lanes] = value.reshape(whole * 8, 128)
            if whole < count:
                rows[which][to + whole * 8 :, lanes] = tiles[first + whole, column][: COARSE - whole * 8] * scale
        src, dst = rows[which], outs[which]
        if count * 8 < src.shape[0]:
            src, dst = src.at[pl.ds(to, count * 8)], dst.at[pl.ds(to, count * 8)]
        puts.append(pltpu.make_async_copy(src, dst, stores.at[at]))
        puts[-1].start()
    for put in puts:
        put.wait()


def finish(summed, grad_edges, grad_fine, edge_scale, node_scale):
    pieces = [
        (0, 64, 3, 0, node_scale),
        (64, 64, 3, FEAT, node_scale),
        (128, 64, 4, 0, node_scale),
        (OUT_ROW, 64, 2, 0, edge_scale),
        (EDGE_ROW, 64, 1, 0, edge_scale),
        (RECV_ROW, 64, 1, 2 * FEAT, edge_scale),
        (COARSE_ROW, 81, 0, 0, 1.0),
        (SEND_ROW, 64, 1, FEAT, edge_scale),
    ]
    any_spec = pl.BlockSpec(memory_space=pl.ANY)
    sizes = (COARSE, 3 * FEAT, FEAT, 2 * FEAT, FEAT)
    sem = pltpu.SemaphoreType.DMA((len(pieces),))
    return pl.pallas_call(
        functools.partial(finish_kernel, pieces),
        out_shape=[f32_out(size, FEAT) for size in sizes + (EDGE, FINE)],
        in_specs=vmem_specs(1) + [any_spec] * 2,
        out_specs=[any_spec] * 7,
        scratch_shapes=[pltpu.VMEM((size, FEAT), F32) for size in sizes] + [sem, pltpu.SemaphoreType.DMA((2,))],
        compiler_params=pltpu.CompilerParams(vmem_limit_bytes=24 << 20),
    )(summed, grad_edges, grad_fine)


def per_device(
    fine_nodes,
    coarse_nodes,
    edge_feats,
    senders,
    receivers,
    send_rows,
    w_edge_in,
    w_edge_out,
    w_node_in,
    w_node_out,
    cot_fine,
    cot_coarse,
    cot_edges,
):
    peers = lax.axis_size("patch")
    send_list = send_rows.reshape(1, EDGE)
    send_at = senders.reshape(1, EDGE)
    recv_at = receivers.reshape(1, EDGE)
    half = pltpu.VMEM((EDGE, FEAT), BF16)
    index = pltpu.VMEM((EDGE, 128), jnp.int32)
    square = pltpu.VMEM((FEAT, FEAT), F32)
    chip_rows = pltpu.VMEM((CHIPS, 2, 8, FEAT), F32)
    core_rows = pltpu.VMEM((CHIPS, 8, FEAT), F32)
    sems = [pltpu.SemaphoreType.DMA] * 4
    wide = f32_out(EDGE, FEAT)
    fine_out = f32_out(FINE, FEAT)

    rows = pltpu.VMEM((EDGE, FEAT), F32)
    rep_out = f32_out(EDGE, 128)
    row_index = pltpu.VMEM((1, EDGE), jnp.int32)
    hbm = pl.BlockSpec(memory_space=pltpu.HBM)
    agg, pre, normed, scale, near = pl.pallas_call(
        front_kernel,
        out_shape=[wide, wide, wide, rep_out, wide],
        in_specs=vmem_specs(3) + [hbm] * 5,
        out_specs=vmem_specs(1) + [hbm] * 4,
        scratch_shapes=[chip_rows, chip_rows, core_rows]
        + [half] * 8
        + [index] * 2
        + [rows, pltpu.VMEM((COARSE, FEAT), F32), pltpu.VMEM((3 * FEAT, FEAT), F32), rows, square]
        + [rows, rows, pltpu.VMEM((EDGE, 128), F32), row_index]
        + [pltpu.SemaphoreType.DMA((5,)), pltpu.SemaphoreType.DMA((4,))]
        + sems,
        compiler_params=pltpu.CompilerParams(collective_id=1, has_side_effects=True, vmem_limit_bytes=FRONT_MIB << 20),
    )(send_list, send_at, recv_at, fine_nodes, w_edge_in, coarse_nodes, edge_feats, w_edge_out)
    grad_agg, direct, few_direct, node = node_step(
        agg, fine_nodes, cot_fine, coarse_nodes, cot_coarse, w_node_in, w_node_out
    )
    grad_edges, grad_fine, in_edge, edge_out, in_recv, coarse, in_send = remote_call(
        back_kernel,
        3,
        [wide, fine_out, TILES, TILES, TILES, f32_out(96, 4, 8, 128), TILES],
        [half] * 6 + [index, core_rows, chip_rows, chip_rows] + [square] * 4 + [row_index] + sems,
        BACK_MIB,
        grad_agg,
        cot_edges,
        pre,
        normed,
        scale,
        w_edge_out,
        send_at,
        recv_at,
        edge_feats,
        near,
        w_edge_in,
        send_list,
        direct,
    )
    (summed,) = remote_call(
        sum_kernel, 4, [sum_out(3)], exchange_scratch(LINKS, 3), SUM_MIB, node, edge_out, in_edge, in_recv, coarse, in_send, few_direct
    )
    edge_scale = 1.0 / math.sqrt(EDGE * peers)
    node_scale = 1.0 / math.sqrt(FINE * peers + COARSE)
    grad_coarse, grad_in, grad_out, grad_node_in, grad_node_out, grad_edges, grad_fine = finish(
        summed, grad_edges, grad_fine, edge_scale, node_scale
    )
    return grad_fine, grad_coarse, grad_edges, grad_in, grad_out, grad_node_in, grad_node_out


def solution(mesh):
    return jax.shard_map(
        per_device,
        mesh=mesh,
        in_specs=(
            P("patch", None),
            P(),
            P("patch", None),
            P("patch"),
            P("patch"),
            P("patch", None, None),
            P(),
            P(),
            P(),
            P(),
            P("patch", None),
            P(),
            P("patch", None),
        ),
        out_specs=(P("patch", None), P(), P("patch", None), P(), P(), P(), P()),
        check_vma=False,
    )
```
